32 devices in a mesh: blk: 8 (over z, x), head: 4 (over y, core).
Axes of the slice: x: 2, y: 2, z: 4, core: 2. Of those that a mesh axis runs over, the one named last changes fastest.
Arguments:
- tokens: bfloat16 [4096, 2048], P(('blk', 'head')), may hold values from -6 to 6
- seg_ids: int32 [4096], P('blk'), may hold values from 0 to 14, as said below
- cotangent: bfloat16 [4096, 2048], P(('blk', 'head')), may hold values from -6 to 6
- gain_mix: bfloat16 [2048], P(('blk', 'head')), may hold values from 0.25 to 1.75
- q_w: bfloat16 [2048, 1024], P('blk', 'head'), may hold values from -0.125 to 0.125
- kv_w: bfloat16 [2048, 2, 256], P(('blk', 'head')), may hold values from -0.125 to 0.125
- zx_w: bfloat16 [2048, 2, 3072], P('blk', None, 'head'), may hold values from -0.125 to 0.125
- dt_w: bfloat16 [2048, 48], P('blk', 'head'), may hold values from -0.125 to 0.125
- bc_w: bfloat16 [2048, 512], P(('blk', 'head')), may hold values from -0.125 to 0.125
- a_log: float32 [48], P('head'), may hold values from 0 to 2.77
- dt_bias: float32 [48], P('head'), may hold values from -6.9 to -2.3
- skip: float32 [48], P('head'), may hold values from 0.5 to 1.5
- wo_w: bfloat16 [2048, 1024], P('blk', 'head'), may hold values from -0.75 to 0.75
- wm_w: bfloat16 [2048, 3072], P('blk', 'head'), may hold values from -0.109375 to 0.109375
- gain_ff: bfloat16 [2048], P(('blk', 'head')), may hold values from 0.25 to 1.75
- gu_w: bfloat16 [2048, 2, 4096], P('blk', None, 'head'), may hold values from -0.125 to 0.125
- down_w: bfloat16 [2048, 4096], P('blk', 'head'), may hold values from -0.09375 to 0.09375
Outputs:
- layer_out: bfloat16 [4096, 2048], P(('blk', 'head'))
- input_grad: float32 [4096, 2048], P(('blk', 'head'))
- gain_mix_grad: float32 [2048], P(('blk', 'head'))
- q_grad: float32 [2048, 1024], P('blk', 'head')
- kv_grad: float32 [2048, 2, 256], P(('blk', 'head'))
- zx_grad: float32 [2048, 2, 3072], P('blk', None, 'head')
- dt_grad: float32 [2048, 48], P('blk', 'head')
- bc_grad: float32 [2048, 512], P(('blk', 'head'))
- a_log_grad: float32 [48], P('head')
- dt_bias_grad: float32 [48], P('head')
- skip_grad: float32 [48], P('head')
- wo_grad: float32 [2048, 1024], P('blk', 'head')
- wm_grad: float32 [2048, 3072], P('blk', 'head')
- gain_ff_grad: float32 [2048], P(('blk', 'head'))
- gu_grad: float32 [2048, 2, 4096], P('blk', None, 'head')
- down_grad: float32 [2048, 4096], P('blk', 'head')
The draws below stay inside these ranges and needn't reach their ends.
Inputs may be any that keep to these rules, and one draw needn't show every extreme that they name: `seg_ids`: ids never fall along the stream, begin at 0 and use every number up to 14.
All inputs are finite; a program needn't handle non-finite values.
Results may differ from the reference program's by a relative error of at most 0.025.
Values may be sent and summed in bfloat16 or wider, within the bound.
No kernel may reach another device: no remote copies, remote signals or barrier semaphores. Data moves between devices by JAX's collectives and lax.ppermute only.
A program may use at most 256 MiB of HBM per device.

```python
import math
import jax
import jax.numpy as jnp
from jax import lax

D = 2048
FF = 4096
QH = 8
KVH = 2
HD = 128
MH = 48
MP = 64
NS = 256
STRETCH = 256
GROUP = 512
TOKENS = 4096
N_HEAD = 4


def draw_seg_ids(key, part):
    key = jax.random.fold_in(key, 7)
    keys = jax.random.split(key, 5)
    quarter = GROUP // 4
    start_long = jax.random.randint(keys[0], (), quarter, 2 * quarter)
    end_long = TOKENS // 2 + GROUP + quarter + jax.random.randint(keys[1], (), 0, quarter)
    start_last = TOKENS - 2 * GROUP + quarter + jax.random.randint(keys[2], (), 0, quarter)
    splits = 12
    powers = jax.random.randint(keys[3], (splits,), 0, 10)
    base = jnp.left_shift(jnp.ones((splits,), jnp.int32), powers)
    extra = jax.random.randint(keys[4], (splits,), 0, 1 << 20) % base
    lengths = base + extra
    running = jnp.cumsum(lengths)[:splits - 1]
    whole = jnp.sum(lengths)
    span = start_last - end_long - splits
    order = jnp.arange(1, splits, dtype=jnp.int32)
    cuts = end_long + order + span * running // whole
    flags = jnp.zeros((TOKENS,), jnp.int32)
    flags = flags.at[start_long].set(1).at[end_long].set(1).at[cuts].set(1).at[start_last].set(1)
    return jnp.cumsum(flags).astype(jnp.int32)


def draw_dt_bias(key, part):
    key = jax.random.fold_in(key, 13)
    return jax.random.uniform(key, (MH,), jnp.float32, -6.9, -2.3)


def levels(rng, dims, cuts, smallest, high):
    loudness, own = 1.0, jax.random.fold_in(rng, 6)
    for position, parts in cuts:
        steps = jnp.exp(jax.random.uniform(jax.random.fold_in(own, position), (parts,), jnp.float32, smallest / len(cuts), high / len(cuts)))
        loudness = loudness * jnp.repeat(steps, dims[position] // parts).reshape([-1 if axis == position else 1 for axis in range(len(dims))])
    return loudness


def bell_draw(key, extent, scale, most, cuts=(), kind=jnp.bfloat16):
    values = scale * jax.random.normal(key, extent, jnp.float32)
    if cuts:
        values = values * levels(key, extent, cuts, -0.22, 0.18)
    return jnp.clip(values, -most, most).astype(kind)


def setup_inputs(seed: int = 0) -> dict:
    key_of = jax.random.split(jax.random.key(seed), 18)
    return {
        "tokens": bell_draw(key_of[0], (TOKENS, D), 1.0, 6.0, ((0, 32),)),
        "seg_ids": draw_seg_ids(jax.random.fold_in(key_of[17], 71), 0),
        "cotangent": bell_draw(key_of[2], (TOKENS, D), 1.0, 6.0, ((0, 32),)),
        "gain_mix": jnp.clip(1.0 + 0.15 * jax.random.normal(key_of[3], (D,), jnp.float32), 0.25, 1.75).astype(jnp.bfloat16),
        "q_w": bell_draw(key_of[4], (D, QH * HD), D ** -0.5, 0.125, ((0, 8), (1, 4))),
        "kv_w": bell_draw(key_of[5], (D, 2, KVH * HD), D ** -0.5, 0.125, ((0, 32),)),
        "zx_w": bell_draw(key_of[6], (D, 2, MH * MP), D ** -0.5, 0.125, ((0, 8), (2, 4))),
        "dt_w": bell_draw(key_of[7], (D, MH), D ** -0.5, 0.125, ((0, 8), (1, 4))),
        "bc_w": bell_draw(key_of[8], (D, 2 * NS), D ** -0.5, 0.125, ((0, 32),)),
        "a_log": jnp.clip(2.77 * jax.random.uniform(key_of[9], (MH,), jnp.float32) ** levels(key_of[9], (MH,), ((0, 4),), -0.2, 0.2), 0.0, 2.77),
        "dt_bias": draw_dt_bias(jax.random.fold_in(key_of[17], 71), 0),
        "skip": jnp.clip(0.5 + 1.0 * jax.random.uniform(key_of[11], (MH,), jnp.float32) ** levels(key_of[11], (MH,), ((0, 4),), -0.2, 0.2), 0.5, 1.5),
        "wo_w": bell_draw(key_of[12], (D, QH * HD), (QH * HD // 16) ** -0.5, 0.75, ((0, 8), (1, 4))),
        "wm_w": bell_draw(key_of[13], (D, MH * MP), (MH * MP) ** -0.5, 0.109375, ((0, 8), (1, 4))),
        "gain_ff": jnp.clip(1.0 + 0.15 * jax.random.normal(key_of[14], (D,), jnp.float32), 0.25, 1.75).astype(jnp.bfloat16),
        "gu_w": bell_draw(key_of[15], (D, 2, FF), D ** -0.5, 0.125, ((0, 8), (2, 4))),
        "down_w": bell_draw(key_of[16], (D, FF), FF ** -0.5, 0.09375, ((0, 8), (1, 4))),
    }


EPS = 1e-05
THETA = 100000000000.0
NEGATIVE = -1e+30
HIGH = lax.Precision.HIGHEST

@jax.custom_vjp
def low(v):
    return lax.optimization_barrier(v.astype(jnp.bfloat16)).astype(jnp.float32)

@jax.custom_vjp
def low_back(v):
    return v

def low_keep(v):
    return (low(v), None)

def low_pass(kept, grad):
    return (grad,)

def back_keep(v):
    return (v, None)

def back_low(kept, grad):
    return (low(grad),)
low.defvjp(low_keep, low_pass)
low_back.defvjp(back_keep, back_low)

def rms_norm(values, gain):
    scale = lax.rsqrt(lax.optimization_barrier(jnp.mean(values * values, axis=-1, keepdims=True)) + EPS)
    return values * scale * gain

def rope(values, positions):
    half = values.shape[-1] // 2
    frequency = jnp.exp(jnp.arange(half, dtype=jnp.float32) * (-2.0 * math.log(THETA) / values.shape[-1]))
    angle = positions.astype(jnp.float32)[:, None] * frequency[None, :]
    cosine = jnp.cos(angle)[:, None, :]
    sine = jnp.sin(angle)[:, None, :]
    first = values[..., :half]
    second = values[..., half:]
    return jnp.concatenate([first * cosine - second * sine, second * cosine + first * sine], axis=-1)

def stretch_step(carry, block, rates, skip):
    held, label = carry
    x_val, z_val, b_val, c_val, dt_val, segment = block
    length = segment.shape[0]
    running = jnp.cumsum(-dt_val * rates[None, :], axis=0)
    running_heads = running.T
    order = jnp.arange(length)
    allowed = (segment[:, None] == segment[None, :]) & (order[:, None] >= order[None, :])
    spread = running_heads[:, :, None] - running_heads[:, None, :]
    decay = jnp.where(allowed[None], jnp.exp(jnp.where(allowed[None], spread, 0.0)), 0.0)
    intersection = jnp.einsum('tn,sn->ts', c_val, b_val, precision=HIGH)
    mixing = decay * intersection[None] * dt_val.T[:, None, :]
    y_val = jnp.einsum('hts,shp->thp', mixing, x_val, precision=HIGH)
    entry = jnp.where((segment == label)[:, None], jnp.exp(running), 0.0)
    y_val = y_val + entry[:, :, None] * jnp.einsum('hpn,tn->thp', held, c_val, precision=HIGH)
    y_val = y_val + skip[None, :, None] * x_val
    gated = y_val * jax.nn.silu(z_val)
    final = segment[length - 1]
    tail = jnp.where((segment == final)[:, None], jnp.exp(running[length - 1][None, :] - running), 0.0) * dt_val
    fresh = jnp.einsum('sh,shp,sn->hpn', tail, x_val, b_val, precision=HIGH)
    kept = jnp.where(label == final, jnp.exp(running[length - 1]), 0.0)
    return ((kept[:, None, None] * held + fresh, final), gated.reshape(length, -1))

def mamba_run(x_val, z_val, b_val, c_val, dt_raw, a_log, dt_bias, skip, segment, held, label):
    size = x_val.shape[0]
    count = size // STRETCH
    dt_val = jax.nn.softplus(dt_raw + dt_bias[None, :])
    rates = jnp.exp(a_log)
    blocks = tuple((part.reshape((count, STRETCH) + part.shape[1:]) for part in (x_val, z_val, b_val, c_val, dt_val, segment)))
    step = jax.checkpoint(lambda carry, block: stretch_step(carry, block, rates, skip))
    (held, label), gated = lax.scan(step, (held, label), blocks)
    total = jnp.exp(-lax.optimization_barrier(jnp.sum(dt_val * rates[None, :], axis=0)))
    return (gated.reshape(size, -1), held, total)

def attention(query, keys, values, segment):
    size = query.shape[0]
    block = min(512, size)
    count = size // block
    positions = jnp.arange(size)
    scale = HD ** (-0.5)

    def one(item):
        q_block, pos_block, seg_block = item
        scores = low_back(jnp.einsum('qard,kad->arqk', q_block, keys, precision=HIGH) * scale)
        allowed = (positions[None, :] <= pos_block[:, None]) & (segment[None, :] == seg_block[:, None])
        masked = jnp.where(allowed, scores, NEGATIVE)
        peak = lax.optimization_barrier(jnp.max(masked, axis=-1, keepdims=True))
        weights = jnp.where(allowed, jnp.exp(masked - peak), 0.0)
        probs = weights / lax.optimization_barrier(jnp.sum(weights, axis=-1, keepdims=True))
        return jnp.einsum('arqk,kad->qard', probs, values, precision=HIGH)
    items = (query.reshape((count, block) + query.shape[1:]), positions.reshape(count, block), segment.reshape(count, block))
    return lax.map(jax.checkpoint(one), items).reshape(size, -1)

def layer(tokens, seg_ids, gain_mix, q_w, kv_w, zx_w, dt_w, bc_w, a_log, dt_bias, skip, wo_w, wm_w, gain_ff, gu_w, down_w):
    slots = N_HEAD
    per_slot = QH // slots
    local_ssm = MH // slots
    slot_heads = [slot * per_slot // (QH // KVH) for slot in range(slots)]
    positions = jnp.arange(TOKENS)
    segment = seg_ids.astype(jnp.float32)
    normed = low(rms_norm(tokens, gain_mix))
    q_proj = low_back(jnp.dot(normed, q_w, precision=HIGH)).reshape(TOKENS, QH, HD)
    query = low(rope(q_proj, positions)).reshape(TOKENS, slots, per_slot, HD)
    kv_proj = jnp.einsum('td,dgc->tgc', normed, kv_w, precision=HIGH).reshape(TOKENS, 2, KVH, HD)
    kv_copies = low_back(kv_proj[:, :, slot_heads])
    keys = low(rope(kv_copies[:, 0], positions))
    values = low(kv_copies[:, 1])
    zx = low(low_back(jnp.einsum('td,dgc->tgc', normed, zx_w, precision=HIGH)))
    dt_raw = low(low_back(jnp.dot(normed, dt_w, precision=HIGH)))
    bc_full = jnp.dot(normed, bc_w, precision=HIGH)
    bc_copies = low(low_back(jnp.broadcast_to(bc_full[:, None, :], (TOKENS, slots, 2 * NS))))
    att = low(low_back(attention(query, keys, values, segment)))
    x_val = zx[:, 1].reshape(TOKENS, MH, MP)
    z_val = zx[:, 0].reshape(TOKENS, MH, MP)
    pieces = []
    for slot in range(slots):
        lower = slot * local_ssm
        upper = lower + local_ssm
        gated, unused_held, unused_total = mamba_run(x_val[:, lower:upper], z_val[:, lower:upper], bc_copies[:, slot, :NS], bc_copies[:, slot, NS:], dt_raw[:, lower:upper], a_log[lower:upper], dt_bias[lower:upper], skip[lower:upper], segment, jnp.zeros((local_ssm, MP, NS), jnp.float32), jnp.float32(-1.0))
        pieces.append(gated)
    ssm = low(low_back(jnp.concatenate(pieces, axis=1)))
    mixed = low_back(jnp.dot(att, wo_w.T, precision=HIGH) + jnp.dot(ssm, wm_w.T, precision=HIGH))
    middle = tokens + mixed
    normed_two = low(rms_norm(middle, gain_ff))
    gate_up = low(low_back(jnp.einsum('td,dgf->tgf', normed_two, gu_w, precision=HIGH)))
    hidden = low(low_back(jax.nn.silu(gate_up[:, 0]) * gate_up[:, 1]))
    return middle + low_back(jnp.dot(hidden, down_w.T, precision=HIGH))

def reference(tokens, seg_ids, cotangent, gain_mix, q_w, kv_w, zx_w, dt_w, bc_w, a_log, dt_bias, skip, wo_w, wm_w, gain_ff, gu_w, down_w):
    floats = tuple((arg.astype(jnp.float32) for arg in (tokens, gain_mix, q_w, kv_w, zx_w, dt_w, bc_w, a_log, dt_bias, skip, wo_w, wm_w, gain_ff, gu_w, down_w)))
    result, pullback = jax.vjp(lambda *vals: layer(vals[0], seg_ids, *vals[1:]), *floats)
    grads = pullback(cotangent.astype(jnp.float32))
    return (result.astype(jnp.bfloat16), grads[0], grads[1], grads[2], grads[3], grads[4], grads[5], grads[6], grads[7], grads[8], grads[9], grads[10], grads[11], grads[12], grads[13], grads[14])
```

```python
import functools
import math

import jax
import jax.numpy as jnp
from jax import lax
from jax.experimental import pallas as pl
from jax.experimental.pallas import tpu as pltpu
from jax.sharding import Mesh
from jax.sharding import PartitionSpec as P

QH = 8
KVH = 2
HD = 128
MP = 64
CHUNK = 256
KEYS = 512
EPS = 1e-05
THETA = 100000000000.0
NEGATIVE = -1e30
EXACT = lax.Precision.HIGHEST
F32 = jnp.float32
BF16 = jnp.bfloat16
VMEM_BYTES = 56 * 1024 * 1024
SWAP = [(0, 1), (1, 0)]


def mm(a, b, ca, cb, precision=None):
    return lax.dot_general(
        a, b, (((ca,), (cb,)), ((), ())), preferred_element_type=F32, precision=precision
    )


def swap(a, axis):
    return lax.ppermute(a, axis, SWAP)


def line_gather(pieces, put, out, up_only=False):
    count = lax.axis_size("z")
    place = lax.axis_index("z")
    ups, downs = [list(pieces)], [list(pieces)]
    for step in range(1, count):
        ups.append(
            [lax.ppermute(a, "z", [(i, i + 1) for i in range(step - 1, count - 1)]) for a in ups[-1]]
        )
        if not up_only:
            downs.append(
                [lax.ppermute(a, "z", [(i, i - 1) for i in range(count - step, 0, -1)]) for a in downs[-1]]
            )
    for number, piece in enumerate(pieces):
        out = put(out, place, number, piece)
    for step in range(1, count):
        for number in range(len(pieces)):
            value = ups[step][number]
            if not up_only:
                value = jnp.where(place >= step, value, downs[count - step][number])
            out = put(out, (place - step + count) % count, number, value)
    return out


def line_scatter(take, down_only=False):
    count = lax.axis_size("z")
    place = lax.axis_index("z")
    up = down = None
    for step in range(1, count):
        if not down_only:
            give = take(jnp.clip(count - step + place, 0, count - 1))
            give = give if up is None else give + up
            up = lax.ppermute(give, "z", [(i, i + 1) for i in range(step)])
        give = take(jnp.clip(place - (count - step), 0, count - 1))
        give = give if down is None else give + down
        down = lax.ppermute(give, "z", [(i, i - 1) for i in range(count - 1, count - 1 - step, -1)])
    total = take(place).astype(F32) + down.astype(F32)
    return total if down_only else total + up.astype(F32)


def spots(dx, dy, dc):
    x, y, c = (lax.axis_index(name) for name in "xyc")
    return ((x ^ dx) * 2 + (y ^ dy)) * 2 + (c ^ dc)


def cube_gather(a, axis):
    half = a.shape[0] // 2
    by_x, by_y = swap(a, "x"), swap(a, "y")
    far_low = swap(by_x[:half], "y")
    far_high = swap(by_y[half:], "x")
    far = jnp.concatenate([far_low, far_high], 0)
    out = jnp.zeros(a.shape[:axis] + (8,) + a.shape[axis:], a.dtype)
    other_far = jnp.concatenate([swap(far_low, "c"), swap(far_high, "c")], 0)
    for (dx, dy), near, other in (
        ((0, 0), a, swap(a, "c")),
        ((1, 0), by_x, swap(by_x, "c")),
        ((0, 1), by_y, swap(by_y, "c")),
        ((1, 1), far, other_far),
    ):
        out = lax.dynamic_update_index_in_dim(out, near, spots(dx, dy, 0), axis)
        out = lax.dynamic_update_index_in_dim(out, other, spots(dx, dy, 1), axis)
    return out


def cube_scatter(terms, axis):
    x, y, c = (lax.axis_index(name) for name in "xyc")
    pairs = terms.reshape(terms.shape[:axis] + (4, 2) + terms.shape[axis + 1 :])
    mine = lax.dynamic_index_in_dim(pairs, c, axis + 1, False)
    mine = mine + swap(lax.dynamic_index_in_dim(pairs, c ^ 1, axis + 1, False), "c")

    def share(dx, dy):
        return lax.dynamic_index_in_dim(mine, (x ^ dx) * 2 + (y ^ dy), axis, False)

    far, to_x, to_y = share(1, 1), share(1, 0), share(0, 1)
    half = far.shape[0] // 2
    from_x = swap(far[:half], "x")
    from_y = swap(far[half:], "y")
    to_x = jnp.concatenate([to_x[:half], to_x[half:] + from_y], 0)
    to_y = jnp.concatenate([to_y[:half] + from_x, to_y[half:]], 0)
    return share(0, 0).astype(F32) + swap(to_x, "x").astype(F32) + swap(to_y, "y").astype(F32)


def weight_gather(pack, after=None):
    if after is not None:
        pack, _ = lax.optimization_barrier((pack, after))
    x = lax.axis_index("x")
    own = lax.dynamic_index_in_dim(pack, x, 0, False)
    got = swap(lax.dynamic_index_in_dim(pack, x ^ 1, 0, False), "x")
    rows, cols = own.shape
    count = lax.axis_size("z")

    def put(out, group, number, value):
        return lax.dynamic_update_slice(out, value[None, None], (group, x ^ number, 0, 0))

    out = line_gather([own, got], put, jnp.zeros((count, 2, rows, cols), pack.dtype))
    return out.reshape(count * 2 * rows, cols)


def weight_scatter(grad):
    count = lax.axis_size("z")
    x = lax.axis_index("x")
    blocks = grad.reshape(count, 2, -1, grad.shape[1])

    def take(number):
        return lambda group: lax.dynamic_slice(
            blocks, (group, number, 0, 0), (1, 1) + blocks.shape[2:]
        )[0, 0]

    give = line_scatter(take(x ^ 1)).astype(BF16)
    got = swap(give, "x").astype(F32)
    own = line_scatter(take(x))
    return jnp.stack([jnp.where(x == 0, own, got), jnp.where(x == 0, got, own)], axis=1)


def lanes_of(cols, heads):
    rows = cols.shape[0]
    low = lax.broadcasted_iota(jnp.int32, (rows, 2 * MP), 1) < MP
    return jnp.concatenate(
        [
            jnp.where(low, cols[:, 2 * j : 2 * j + 1], cols[:, 2 * j + 1 : 2 * j + 2])
            for j in range(heads // 2)
        ],
        axis=1,
    )


def head_sums(values):
    wide = values.shape[1]
    lane = lax.broadcasted_iota(jnp.int32, (wide, 128), 0) // MP
    pick = (lane == lax.broadcasted_iota(jnp.int32, (wide, 128), 1)).astype(F32)
    return mm(values, pick, 1, 0, EXACT)


def softplus(v):
    return jnp.maximum(v, 0.0) + jnp.log1p(jnp.exp(-jnp.abs(v)))


def sigmoid(v):
    return 1.0 / (1.0 + jnp.exp(-v))


def chunk_common(rest_ref, dt_row_ref, par_ref, par_col_ref, seg_col_ref, seg_row_ref, wide):
    heads = wide // MP
    base = 2 * wide + HD
    states = (rest_ref.shape[1] - base - 128) // 2
    b_val = rest_ref[:, base : base + states]
    c_val = rest_ref[:, base + states : base + 2 * states]
    raw = rest_ref[:, base + 2 * states :].astype(F32) + par_ref[0:1, :]
    dt = softplus(raw)
    rate = par_ref[1:2, :]
    raw_row = dt_row_ref[...].astype(F32) + par_col_ref[:, 0:1]
    e_row = -softplus(raw_row) * par_col_ref[:, 1:2]
    first = lax.broadcasted_iota(jnp.int32, (CHUNK, CHUNK), 0)
    second = lax.broadcasted_iota(jnp.int32, (CHUNK, CHUNK), 1)
    lower = (first >= second).astype(F32)
    run = mm(lower, -dt * rate, 1, 0, EXACT)
    run_row = mm(e_row, lower, 1, 1, EXACT)
    bias = jnp.where((first >= second) & (seg_col_ref[...] == seg_row_ref[0]), 0.0, NEGATIVE)
    return heads, b_val, c_val, raw, dt, rate, run, run_row, bias, lower


def mamba_local_kernel(
    rest_ref, dt_row_ref, par_ref, par_col_ref, skip_ref, seg_col_ref, seg_row_ref, marks_ref,
    y_ref, run_ref, held_ref, total_ref, starts_ref, state, base_run,
):
    step = pl.program_id(0)
    wide = skip_ref.shape[1]
    heads, b_val, c_val, raw, dt, rate, run, run_row, bias, _ = chunk_common(
        rest_ref, dt_row_ref, par_ref, par_col_ref, seg_col_ref, seg_row_ref, wide
    )

    @pl.when(step == 0)
    def _():
        state[...] = jnp.zeros_like(state)
        base_run[...] = jnp.zeros_like(base_run)

    x_val = rest_ref[:, wide : 2 * wide].astype(F32)
    seg = seg_col_ref[...]
    label = marks_ref[step]
    final = marks_ref[step + 1]
    held = state[...]
    starts_ref[0] = held
    x_dt = x_val * lanes_of(dt, heads)
    x_dt_b = x_dt.astype(BF16)
    entry = jnp.where(seg == label, jnp.exp(run), 0.0)
    last = run[CHUNK - 1 : CHUNK, :]
    tail = jnp.where(seg == final, jnp.exp(last - run), 0.0)
    y_val = skip_ref[...] * x_val
    y_val = y_val + lanes_of(entry, heads) * mm(c_val, held.astype(BF16), 1, 0)
    gram = mm(c_val, b_val, 1, 1)
    low = lax.broadcasted_iota(jnp.int32, (CHUNK, 2 * MP), 1) < MP
    parts = []
    for pair in range(heads // 2):
        both = x_dt_b[:, pair * 2 * MP : (pair + 1) * 2 * MP]
        outs = []
        for h in (2 * pair, 2 * pair + 1):
            decay = jnp.exp(run[:, h : h + 1] - run_row[h : h + 1, :] + bias)
            outs.append(mm((decay * gram).astype(BF16), both, 1, 0))
        parts.append(jnp.where(low, outs[0], outs[1]))
    y_ref[...] = y_val + jnp.concatenate(parts, axis=1)
    fresh = mm(b_val, (x_dt * lanes_of(tail, heads)).astype(BF16), 0, 0)
    kept = jnp.where(label == final, jnp.exp(last), 0.0)
    new = lanes_of(jnp.broadcast_to(kept, (8, 128)), heads)[0:1] * held + fresh
    state[...] = new
    held_ref[...] = new
    run_all = run + base_run[0:1, :]
    run_ref[...] = run_all
    base_run[...] = jnp.broadcast_to(run_all[CHUNK - 1 : CHUNK, :], base_run.shape)
    total_ref[...] = jnp.exp(base_run[...])


def mamba_close_kernel(rest_ref, y_ref, run_ref, seg_col_ref, held_ref, marks_ref, out_ref, full_ref):
    wide = y_ref.shape[1]
    heads = wide // MP
    states = held_ref.shape[0]
    base = 2 * wide + HD + states
    c_val = rest_ref[:, base : base + states]
    entry = jnp.where(seg_col_ref[...] == marks_ref[0], jnp.exp(run_ref[...]), 0.0)
    y_val = y_ref[...] + lanes_of(entry, heads) * mm(c_val, held_ref[...].astype(BF16), 1, 0)
    full_ref[...] = y_val
    z_val = rest_ref[:, :wide].astype(F32)
    out_ref[...] = (y_val * z_val * sigmoid(z_val)).astype(BF16)


def mamba_grad_state_kernel(rest_ref, grad_ref, run_ref, seg_col_ref, marks_ref, out_ref):
    wide = grad_ref.shape[1]
    heads = wide // MP
    states = out_ref.shape[0]
    base = 2 * wide + HD + states
    c_val = rest_ref[:, base : base + states]
    z_val = rest_ref[:, :wide].astype(F32)
    entry = jnp.where(seg_col_ref[...] == marks_ref[0], jnp.exp(run_ref[...]), 0.0)
    grad_y = grad_ref[...].astype(F32) * z_val * sigmoid(z_val)

    @pl.when(pl.program_id(0) == 0)
    def _():
        out_ref[...] = jnp.zeros_like(out_ref)

    out_ref[...] += mm(c_val, (grad_y * lanes_of(entry, heads)).astype(BF16), 0, 0)


def mamba_grad_kernel(
    rest_ref, dt_row_ref, par_ref, par_col_ref, skip_ref, seg_col_ref, seg_row_ref, marks_ref,
    y_ref, run_ref, starts_ref, held_ref, grad_ref, deep_ref,
    zx_ref, bc_ref, dt_ref, sums_ref, skip_sum_ref, deep,
):
    step = pl.num_programs(0) - 1 - pl.program_id(0)
    wide = skip_ref.shape[1]
    heads, b_val, c_val, raw, dt, rate, run, run_row, bias, lower = chunk_common(
        rest_ref, dt_row_ref, par_ref, par_col_ref, seg_col_ref, seg_row_ref, wide
    )
    states = b_val.shape[1]

    @pl.when(pl.program_id(0) == 0)
    def _():
        deep[...] = deep_ref[...]
        sums_ref[...] = jnp.zeros_like(sums_ref)
        skip_sum_ref[...] = jnp.zeros_like(skip_sum_ref)

    z_val = rest_ref[:, :wide].astype(F32)
    x_val = rest_ref[:, wide : 2 * wide].astype(F32)
    seg = seg_col_ref[...]
    label = marks_ref[step]
    final = marks_ref[step + 1]
    last = run[CHUNK - 1 : CHUNK, :]
    before = run_ref[0:1, :] - run[0:1, :]
    carry = jnp.where(label == marks_ref[0], jnp.exp(before), 0.0)
    held = starts_ref[0] + lanes_of(jnp.broadcast_to(carry, (8, 128)), heads)[0:1] * held_ref[...]
    held_b = held.astype(BF16)
    after = deep[...]
    after_b = after.astype(BF16)
    grad = grad_ref[...].astype(F32)
    sig = sigmoid(z_val)
    grad_y = grad * z_val * sig
    grad_z = grad * y_ref[...] * (sig * (1.0 + z_val * (1.0 - sig)))
    dt_wide = lanes_of(dt, heads)
    x_dt = x_val * dt_wide
    entry = lanes_of(jnp.where(seg == label, jnp.exp(run), 0.0), heads)
    tail = lanes_of(jnp.where(seg == final, jnp.exp(last - run), 0.0), heads)
    grad_in = (entry * grad_y).astype(BF16)
    run_grad = head_sums(grad_y * entry * mm(c_val, held_b, 1, 0))
    grad_c = mm(grad_in, held_b, 1, 1)
    x_tail = x_dt * tail
    back = mm(b_val, after_b, 1, 0)
    grad_b = mm(x_tail.astype(BF16), after_b, 1, 1)
    tail_grad = head_sums(x_tail * back)
    run_grad = run_grad - tail_grad
    kept = jnp.where(label == final, jnp.exp(last), 0.0)
    kept_wide = lanes_of(jnp.broadcast_to(kept, (8, 128)), heads)[0:1]
    kept_grad = head_sums(
        jnp.broadcast_to(kept_wide * jnp.sum(after * held, axis=0, keepdims=True), (8, wide))
    )
    last_grad = jnp.sum(tail_grad, axis=0, keepdims=True) + kept_grad[0:1]
    deep[...] = kept_wide * after + mm(c_val, grad_in, 0, 0)
    gram = mm(c_val, b_val, 1, 1)
    low = lax.broadcasted_iota(jnp.int32, (CHUNK, 2 * MP), 1) < MP
    lane = lax.broadcasted_iota(jnp.int32, (CHUNK, 128), 1)
    x_dt_b = x_dt.astype(BF16)
    grad_y_b = grad_y.astype(BF16)
    none = jnp.zeros((CHUNK, 2 * MP), BF16)
    gram_grad = None
    parts, cols = [], []
    for pair in range(heads // 2):
        span = slice(pair * 2 * MP, (pair + 1) * 2 * MP)
        outs = []
        for h in (2 * pair, 2 * pair + 1):
            mask = low if h % 2 == 0 else ~low
            decay = jnp.exp(run[:, h : h + 1] - run_row[h : h + 1, :] + bias)
            mixing = (decay * gram).astype(BF16)
            outs.append(mm(mixing, grad_y_b[:, span], 0, 0))
            mixing_grad = mm(jnp.where(mask, grad_y_b[:, span], none), x_dt_b[:, span], 1, 1)
            weighted = mixing_grad * decay
            gram_grad = weighted if gram_grad is None else gram_grad + weighted
            weighted = weighted * gram
            run_grad = run_grad + jnp.where(
                lane == h, jnp.sum(weighted, axis=1, keepdims=True), 0.0
            )
            cols.append(jnp.sum(weighted, axis=0, keepdims=True))
        parts.append(jnp.where(low, outs[0], outs[1]))
    gram_grad_b = gram_grad.astype(BF16)
    grad_c = grad_c + mm(gram_grad_b, b_val, 1, 0)
    grad_b = grad_b + mm(gram_grad_b, c_val, 0, 0)
    x_dt_grad = jnp.concatenate(parts, axis=1) + tail * back
    zx_ref[:, :wide] = grad_z.astype(BF16)
    zx_ref[:, wide:] = (x_dt_grad * dt_wide + skip_ref[...] * grad_y).astype(BF16)
    bc_ref[:, :states] = grad_b.astype(BF16)
    bc_ref[:, states:] = grad_c.astype(BF16)
    col_grad = jnp.concatenate(cols + [jnp.zeros((128 - heads, CHUNK), F32)], axis=0)
    e_grad = mm(lower, run_grad, 0, 0, EXACT) - mm(lower, col_grad, 0, 1, EXACT) + last_grad
    dt_grad = head_sums(x_dt_grad * x_val) - rate * e_grad
    raw_grad = dt_grad * sigmoid(raw)
    dt_ref[...] = jnp.where(lane < heads, raw_grad, 0.0).astype(BF16)
    sums_ref[0:1, :] += jnp.sum(-rate * dt * e_grad, axis=0, keepdims=True)
    sums_ref[1:2, :] += jnp.sum(raw_grad, axis=0, keepdims=True)
    skip_sum_ref[0:1, :] += jnp.sum(grad_y * x_val, axis=0, keepdims=True)


def seen(kseg_ref, qseg, first_query, block):
    rows = qseg.shape[0]
    key_pos = block * KEYS + lax.broadcasted_iota(jnp.int32, (rows, KEYS), 1)
    query_pos = first_query + lax.broadcasted_iota(jnp.int32, (rows, KEYS), 0)
    return (key_pos <= query_pos) & (kseg_ref[pl.ds(block, 1), :] == qseg)


def attend_kernel(low_ref, high_ref, start_ref, q_ref, kv_ref, kseg_ref, qseg_ref, att_ref, log_ref):
    step = pl.program_id(0)
    rows = q_ref.shape[0]
    query = q_ref[...]
    qseg = qseg_ref[...]
    first_query = start_ref[0] + step * rows
    scale = HD**-0.5

    def visit(block, state):
        peak, total, acc = state
        span = pl.ds(pl.multiple_of(block * KEYS, KEYS), KEYS)
        scores = mm(query, kv_ref[span, :HD], 1, 1) * scale
        scores = jnp.where(seen(kseg_ref, qseg, first_query, block), scores, NEGATIVE)
        new_peak = jnp.maximum(peak, jnp.max(scores, axis=1, keepdims=True))
        weights = jnp.exp(scores - new_peak)
        rescale = jnp.exp(peak - new_peak)
        total = total * rescale + jnp.sum(weights, axis=1, keepdims=True)
        acc = acc * rescale + mm(weights.astype(BF16), kv_ref[span, HD:], 1, 0)
        return new_peak, total, acc

    peak, total, acc = lax.fori_loop(
        low_ref[step],
        high_ref[step],
        visit,
        (
            jnp.full((rows, 1), NEGATIVE, F32),
            jnp.zeros((rows, 1), F32),
            jnp.zeros((rows, HD), F32),
        ),
    )
    att_ref[...] = acc / total
    log_ref[...] = jnp.broadcast_to(peak + jnp.log(total), log_ref.shape)


def attend_grad_kernel(
    low_ref, high_ref, start_ref, q_ref, kv_ref, kseg_ref, qseg_ref, att_ref, log_ref, grad_ref,
    dq_ref, dkv_ref, sums,
):
    step = pl.program_id(0)
    rows = q_ref.shape[0]
    query = q_ref[...]
    grad = grad_ref[...]
    qseg = qseg_ref[...]
    log_total = log_ref[:, 0:1]
    first_query = start_ref[0] + step * rows
    scale = HD**-0.5
    delta = jnp.sum(grad.astype(F32) * att_ref[...], axis=1, keepdims=True)

    @pl.when(step == 0)
    def _():
        sums[...] = jnp.zeros_like(sums)

    def visit(block, acc):
        span = pl.ds(pl.multiple_of(block * KEYS, KEYS), KEYS)
        keys = kv_ref[span, :HD]
        scores = mm(query, keys, 1, 1) * scale - log_total
        scores = jnp.where(seen(kseg_ref, qseg, first_query, block), scores, NEGATIVE)
        probs = jnp.exp(scores)
        probs_grad = mm(grad, kv_ref[span, HD:], 1, 1)
        scores_grad = (probs * (probs_grad - delta)).astype(BF16)
        sums[span, :HD] += mm(scores_grad, query, 0, 0)
        sums[span, HD:] += mm(probs.astype(BF16), grad, 0, 0)
        return acc + mm(scores_grad, keys, 1, 0)

    acc = lax.fori_loop(low_ref[step], high_ref[step], visit, jnp.zeros((rows, HD), F32))
    dq_ref[...] = acc * scale

    @pl.when(step == pl.num_programs(0) - 1)
    def _():
        dkv_ref[:, :HD] = (sums[:, :HD] * scale).astype(BF16)
        dkv_ref[:, HD:] = sums[:, HD:].astype(BF16)


def call(kernel, out_shape, grid, in_specs, out_specs, scratch=(), prefetch=0, cost=None):
    return pl.pallas_call(
        kernel,
        out_shape=out_shape,
        grid_spec=pltpu.PrefetchScalarGridSpec(
            num_scalar_prefetch=prefetch,
            grid=grid,
            in_specs=in_specs,
            out_specs=out_specs,
            scratch_shapes=list(scratch),
        ),
        compiler_params=pltpu.CompilerParams(
            vmem_limit_bytes=VMEM_BYTES, dimension_semantics=("arbitrary",) * len(grid)
        ),
        cost_estimate=cost,
    )


def shape(dims, dtype=F32):
    return jax.ShapeDtypeStruct(dims, dtype)


def rope_tables(positions):
    half = HD // 2
    frequency = jnp.exp(jnp.arange(half, dtype=F32) * (-2.0 * math.log(THETA) / HD))
    angle = positions.astype(F32)[:, None] * frequency[None, :]
    cosine, sine = jnp.cos(angle), jnp.sin(angle)
    return jnp.concatenate([cosine, cosine], 1), jnp.concatenate([-sine, sine], 1)


def rope(values, tables):
    cosine, sine = tables
    return values * cosine + jnp.concatenate([values[:, HD // 2 :], values[:, : HD // 2]], 1) * sine


def rope_back(values, tables):
    cosine, sine = tables
    return values * cosine - jnp.concatenate([values[:, HD // 2 :], values[:, : HD // 2]], 1) * sine


def unit(values):
    return values * lax.rsqrt(jnp.mean(values * values, axis=-1, keepdims=True) + EPS)


def norm_back(values, gain, grad):
    scale = lax.rsqrt(jnp.mean(values * values, axis=-1, keepdims=True) + EPS)
    u = values * scale
    inner = jnp.mean(grad * gain * u, axis=-1, keepdims=True)
    return scale * (grad * gain - u * inner), jnp.sum(grad * u, axis=0)


def shards(
    tokens, seg_ids, cotangent, gain_mix, q_w, kv_w, zx_w, dt_w, bc_w,
    a_log, dt_bias, skip, wo_w, wm_w, gain_ff, gu_w, down_w,
):
    groups = lax.axis_size("z")
    z, x, y, c = (lax.axis_index(name) for name in "zxyc")
    own_rows, width = tokens.shape
    group = 8 * own_rows
    rows_w = q_w.shape[0]
    part = kv_w.shape[0]
    ratio = rows_w // part
    heads = dt_w.shape[1] // 2
    wide = heads * MP
    states = bc_w.shape[1] // 2
    ff = gu_w.shape[2] // 2
    inner = q_w.shape[1] // 2
    steps = group // CHUNK

    pack_one = jnp.concatenate(
        [
            q_w.reshape(rows_w, 2, inner).transpose(1, 0, 2),
            zx_w.reshape(rows_w, 2, 2, wide).transpose(2, 0, 1, 3).reshape(2, rows_w, 2 * wide),
        ],
        axis=2,
    )
    pack_out = jnp.concatenate(
        [
            wo_w.reshape(rows_w, 2, inner).transpose(1, 0, 2),
            wm_w.reshape(rows_w, 2, wide).transpose(1, 0, 2),
        ],
        axis=2,
    )
    pack_gu = gu_w.reshape(rows_w, 2, 2, ff).transpose(2, 0, 1, 3).reshape(2, rows_w, 2 * ff)
    pack_down = down_w.reshape(rows_w, 2, ff).transpose(1, 0, 2)
    kv_cols = kv_w.shape[1] * kv_w.shape[2]
    bc_cols = bc_w.shape[1]
    lead = kv_cols + bc_cols
    dt_cols = dt_w.shape[1]
    dt_part = dt_w.reshape(ratio, part, dt_cols).transpose(1, 0, 2).reshape(part, ratio * dt_cols)
    pack_two = jnp.concatenate(
        [kv_w.reshape(part, kv_cols), bc_w, gain_mix[:, None], gain_ff[:, None], dt_part], axis=1
    )
    used = pack_two.shape[1]
    total_cols = -(-used // 128) * 128
    pack_two = jnp.pad(pack_two, ((0, 0), (0, total_cols - used)))

    def put_two(out, at, number, value):
        return lax.dynamic_update_slice(out, value[None], (at, 0, 0))

    rows_all = cube_gather(tokens, 0).reshape(group, width)
    two = line_gather([pack_two], put_two, jnp.zeros((groups,) + pack_two.shape, BF16))
    two = cube_gather(two, 1).reshape(width, total_cols)
    w_one = weight_gather(pack_one)
    w_out = weight_gather(pack_out, w_one[0, 0])
    w_gu = weight_gather(pack_gu, w_out[0, 0])
    w_down = weight_gather(pack_down, w_gu[0, 0])
    grad_rows = cube_gather(cotangent, 0).reshape(group, width)

    seg_pair = jnp.zeros((2, seg_ids.shape[0]), jnp.int32)
    seg_pair = lax.dynamic_update_index_in_dim(seg_pair, seg_ids, x, 0)
    seg_pair = lax.dynamic_update_index_in_dim(seg_pair, swap(seg_ids, "x"), x ^ 1, 0)
    seg_own = seg_pair.reshape(1, group)
    seg_all = line_gather(
        [seg_own],
        lambda out, at, number, value: lax.dynamic_update_slice(out, value, (at, 0)),
        jnp.zeros((groups, group), jnp.int32),
        up_only=True,
    )
    segment = seg_own.astype(F32)
    seg_col = segment.reshape(group, 1)
    seg_row = segment.reshape(steps, 1, CHUNK)
    previous = lax.dynamic_index_in_dim(seg_all, jnp.maximum(z - 1, 0), 0, False)[group - 1]
    in_label = jnp.where(z > 0, previous, -1).astype(F32)
    marks = jnp.concatenate([in_label[None], segment[0, CHUNK - 1 :: CHUNK]])

    gain_one = two[:, lead].astype(F32)
    gain_two = two[:, lead + 1].astype(F32)
    dt_all = two[:, lead + 2 : lead + 2 + ratio * dt_cols].reshape(
        groups, 2, 4, part, ratio, 2, heads
    )
    dt_own = lax.dynamic_index_in_dim(dt_all, y * 2 + c, 2, False)
    dt_own = lax.dynamic_index_in_dim(dt_own, x, 4, False)
    w_dt = dt_own.transpose(0, 1, 3, 2, 4).reshape(width, heads)
    kv_head = ((y * 2 + c) * 2 + x) * (inner // HD) // (QH // KVH)
    w_k = lax.dynamic_slice_in_dim(two, kv_head * HD, HD, 1)
    w_v = lax.dynamic_slice_in_dim(two, kv_cols // 2 + kv_head * HD, HD, 1)
    w_rest = jnp.concatenate(
        [
            w_one[:, inner:],
            w_v,
            two[:, kv_cols:lead],
            jnp.pad(w_dt, ((0, 0), (0, 128 - heads))),
        ],
        axis=1,
    )
    w_qk = jnp.concatenate([w_one[:, :inner], w_k], axis=1)

    stream = rows_all.astype(F32)
    normed = (unit(stream) * gain_one).astype(BF16)
    positions = z * group + jnp.arange(group, dtype=jnp.int32)
    tables = rope_tables(positions)
    qk = mm(normed, w_qk, 1, 0)
    rest = mm(normed, w_rest, 1, 0).astype(BF16)
    query = rope(qk[:, :HD], tables).astype(BF16)
    kv_own = jnp.concatenate(
        [rope(qk[:, HD:], tables).astype(BF16), rest[:, 2 * wide : 2 * wide + HD]], axis=1
    )
    half = group // 2
    kv_half = lax.dynamic_slice_in_dim(kv_own, c * half, half, 0)
    kv_got = line_gather(
        [kv_half], put_two, jnp.zeros((groups, half, 2 * HD), BF16), up_only=True
    )
    kv_other = swap(kv_got, "c")
    kv_all = jnp.zeros((groups, 2, half, 2 * HD), BF16)
    kv_all = lax.dynamic_update_index_in_dim(kv_all, kv_got, c, 1)
    kv_all = lax.dynamic_update_index_in_dim(kv_all, kv_other, c ^ 1, 1)
    kv_all = kv_all.reshape(groups * group, 2 * HD)

    dt_row = jnp.pad(rest[:, -128 : -128 + 8].T, ((0, 8), (0, 0)))
    pad = ((0, 128 - heads),)

    def pick(values):
        return lax.dynamic_slice_in_dim(values, x * heads, heads, 0)

    rates = jnp.exp(pick(a_log))
    params = jnp.stack([jnp.pad(pick(dt_bias), pad), jnp.pad(rates, pad)])
    params = jnp.pad(params, ((0, 6), (0, 0)))
    params_col = jnp.pad(
        jnp.stack([pick(dt_bias), rates], axis=1), ((0, 16 - heads), (0, 126))
    )
    skip_wide = jnp.repeat(pick(skip), MP)[None, :]
    rest_cols = rest.shape[1]

    def flow(cols, back=False):
        at = (lambda i: (steps - 1 - i, 0)) if back else (lambda i: (i, 0))
        return pl.BlockSpec((CHUNK, cols), at)

    def chunk_specs(back=False):
        def turn(i):
            return steps - 1 - i if back else i

        return [
            flow(rest_cols, back),
            pl.BlockSpec((16, CHUNK), lambda i: (0, turn(i))),
            pl.BlockSpec((8, 128), lambda i: (0, 0)),
            pl.BlockSpec((16, 128), lambda i: (0, 0)),
            pl.BlockSpec((1, wide), lambda i: (0, 0)),
            flow(1, back),
            pl.BlockSpec((1, 1, CHUNK), lambda i: (turn(i), 0, 0)),
            pl.BlockSpec(memory_space=pltpu.SMEM),
        ]

    whole = pl.BlockSpec((states, wide), lambda i: (0, 0))
    smem = pl.BlockSpec(memory_space=pltpu.SMEM)
    chunk_args = (rest, dt_row, params, params_col, skip_wide, seg_col, seg_row, marks)
    y_local, run, held_own, total, starts = call(
        mamba_local_kernel,
        (
            shape((group, wide)),
            shape((group, 128)),
            shape((states, wide)),
            shape((8, 128)),
            shape((steps, states, wide)),
        ),
        (steps,),
        chunk_specs(),
        (
            flow(wide),
            flow(128),
            whole,
            pl.BlockSpec((8, 128), lambda i: (0, 0)),
            pl.BlockSpec((1, states, wide), lambda i: (i, 0, 0)),
        ),
        [pltpu.VMEM((states, wide), F32), pltpu.VMEM((8, 128), F32)],
    )(*chunk_args)
    joined = jnp.where(in_label == segment[0, group - 1], 1.0, 0.0)
    factor = jnp.repeat(total[0, :heads] * joined, MP)[None, :]
    up_line = [(i, i + 1) for i in range(groups - 1)]
    down_line = [(i + 1, i) for i in range(groups - 1)]
    entering = jnp.zeros((states, wide), BF16)
    for step in range(groups - 1):
        leaving = held_own if step == 0 else held_own + factor * entering.astype(F32)
        entering = lax.ppermute(leaving.astype(BF16), "z", up_line)
    in_held = entering

    q_rows = CHUNK
    blocks = group // q_rows
    first_rows = z * group + q_rows * jnp.arange(blocks, dtype=jnp.int32)
    first_seg = seg_own[0, ::q_rows]
    reached = jnp.arange(groups * group, dtype=jnp.int32)[None, :] < (z + 1) * group
    earlier = (seg_all.reshape(1, -1) < first_seg[:, None]) & reached
    low = jnp.sum(earlier, axis=1, dtype=jnp.int32) // KEYS
    high = (first_rows + q_rows - 1) // KEYS + 1
    start = (z * group)[None].astype(jnp.int32)
    key_seg = seg_all.astype(F32).reshape(groups * group // KEYS, KEYS)

    def rows_spec(cols):
        return pl.BlockSpec((q_rows, cols), lambda i, *_: (i, 0))

    def full_spec(a):
        return pl.BlockSpec(a.shape, lambda i, *_: (0, 0))

    att_full, log_total = call(
        attend_kernel,
        (shape((group, HD)), shape((group, 128))),
        (blocks,),
        [rows_spec(HD), full_spec(kv_all), full_spec(key_seg), rows_spec(1)],
        (rows_spec(HD), rows_spec(128)),
        prefetch=3,
    )(low, high, start, query, kv_all, key_seg, seg_col)

    ssm_out, y_full = call(
        mamba_close_kernel,
        (shape((group, wide), BF16), shape((group, wide))),
        (steps,),
        [flow(rest_cols), flow(wide), flow(128), flow(1), whole, smem],
        (flow(wide), flow(wide)),
    )(rest, y_local, run, seg_col, in_held, marks)
    mixer_out = jnp.concatenate([att_full.astype(BF16), ssm_out], axis=1)

    def to_rows(term):
        return cube_scatter(term.astype(BF16).reshape(8, own_rows, width), 0)

    stream_own = tokens.astype(F32)
    middle = stream_own + to_rows(mm(mixer_out, w_out, 1, 1))
    normed_two = (unit(middle) * gain_two).astype(BF16)
    rows_two = cube_gather(normed_two, 0).reshape(group, width)
    gate_up = mm(rows_two, w_gu, 1, 0).astype(BF16)
    gate = gate_up[:, :ff].astype(F32)
    up = gate_up[:, ff:].astype(F32)
    sig = jax.nn.sigmoid(gate)
    hidden = (gate * sig * up).astype(BF16)
    grad_hidden = mm(grad_rows, w_down, 1, 0).astype(BF16).astype(F32)
    grad_gate = grad_hidden * up * (sig * (1.0 + gate * (1.0 - sig)))
    grad_gu = jnp.concatenate([grad_gate, grad_hidden * gate * sig], axis=1).astype(BF16)
    grad_normed_two = to_rows(mm(grad_gu, w_gu, 1, 1))
    layer_out = (middle + to_rows(mm(hidden, w_down, 1, 1))).astype(BF16)
    down_part = weight_scatter(mm(grad_rows, hidden, 0, 0).astype(BF16))
    gu_part = weight_scatter(mm(rows_two, grad_gu, 0, 0).astype(BF16))
    middle_part, gain_two_part = norm_back(middle, gain_two, grad_normed_two)
    grad_middle = cotangent.astype(F32) + middle_part
    mixed_rows = cube_gather(grad_middle.astype(BF16), 0).reshape(group, width)
    grad_mixer = mm(mixed_rows, w_out, 1, 0).astype(BF16)
    out_part = weight_scatter(mm(mixed_rows, mixer_out, 0, 0).astype(BF16))

    grad_att = grad_mixer[:, :inner]
    grad_ssm = grad_mixer[:, inner:]
    state_grad = call(
        mamba_grad_state_kernel,
        shape((states, wide)),
        (steps,),
        [flow(rest_cols), flow(wide), flow(128), flow(1), smem],
        whole,
    )(rest, grad_ssm, run, seg_col, marks)
    deep = jnp.zeros((states, wide), BF16)
    for step in range(groups - 1):
        leaving = state_grad if step == 0 else state_grad + factor * deep.astype(F32)
        deep = lax.ppermute(leaving.astype(BF16), "z", down_line)
    deep = deep.astype(F32)
    grad_query, grad_kv_all = call(
        attend_grad_kernel,
        (shape((group, HD)), shape((groups * group, 2 * HD), BF16)),
        (blocks,),
        [
            rows_spec(HD), full_spec(kv_all), full_spec(key_seg), rows_spec(1),
            rows_spec(HD), rows_spec(128), rows_spec(HD),
        ],
        (rows_spec(HD), full_spec(kv_all)),
        [pltpu.VMEM((groups * group, 2 * HD), F32)],
        prefetch=3,
    )(low, high, start, query, kv_all, key_seg, seg_col, att_full, log_total, grad_att)
    kv_terms = grad_kv_all.reshape(groups, 2, half, 2 * HD)
    kv_terms = lax.dynamic_index_in_dim(kv_terms, c, 1, False) + swap(
        lax.dynamic_index_in_dim(kv_terms, c ^ 1, 1, False), "c"
    )
    grad_kv_half = line_scatter(
        lambda at: lax.dynamic_index_in_dim(kv_terms, at, 0, False), down_only=True
    )
    half_tables = tuple(lax.dynamic_slice_in_dim(table, c * half, half, 0) for table in tables)
    grad_kv_half = jnp.concatenate(
        [rope_back(grad_kv_half[:, :HD], half_tables), grad_kv_half[:, HD:]], axis=1
    ).astype(BF16)
    grad_kv = lax.dynamic_update_slice(
        jnp.zeros((group, 2 * HD), BF16), grad_kv_half, (c * half, 0)
    )
    grad_q = rope_back(grad_query, tables).astype(BF16)
    grad_zx, grad_bc, grad_dt, sums, skip_sums = call(
        mamba_grad_kernel,
        (
            shape((group, 2 * wide), BF16),
            shape((group, 2 * states), BF16),
            shape((group, 128), BF16),
            shape((8, 128)),
            shape((8, wide)),
        ),
        (steps,),
        chunk_specs(True)
        + [
            flow(wide, True),
            flow(128, True),
            pl.BlockSpec((1, states, wide), lambda i: (steps - 1 - i, 0, 0)),
            whole,
            flow(wide, True),
            whole,
        ],
        (
            flow(2 * wide, True),
            flow(2 * states, True),
            flow(128, True),
            pl.BlockSpec((8, 128), lambda i: (0, 0)),
            pl.BlockSpec((8, wide), lambda i: (0, 0)),
        ),
        [pltpu.VMEM((states, wide), F32)],
    )(*chunk_args, y_full, run, starts, in_held, grad_ssm, deep)

    grad_rest = jnp.concatenate([grad_zx, grad_kv[:, HD:], grad_bc, grad_dt], axis=1)
    grad_qk = jnp.concatenate([grad_q, grad_kv[:, :HD]], axis=1)
    in_term = (mm(grad_rest, w_rest, 1, 1) + mm(grad_qk, w_qk, 1, 1)).astype(BF16)
    gain_one_part = jnp.sum(in_term.astype(F32) * unit(stream), axis=0)
    rest_w = mm(normed, grad_rest, 0, 0).astype(BF16)
    qk_w = mm(normed, grad_qk, 0, 0).astype(BF16)
    one_part = weight_scatter(jnp.concatenate([qk_w[:, :inner], rest_w[:, : 2 * wide]], axis=1))
    input_part, _ = norm_back(stream_own, gain_one, to_rows(in_term))
    input_grad = grad_middle + input_part
    kv_grads = jnp.zeros((width, kv_cols), BF16)
    kv_grads = lax.dynamic_update_slice_in_dim(kv_grads, qk_w[:, inner:], kv_head * HD, 1)
    kv_grads = lax.dynamic_update_slice_in_dim(
        kv_grads, rest_w[:, 2 * wide : 2 * wide + HD], kv_cols // 2 + kv_head * HD, 1
    )
    dt_full = rest_w[:, -128 : -128 + heads].reshape(groups, 2, ratio, part, heads)
    dt_full = dt_full.transpose(0, 1, 3, 2, 4)[:, :, :, :, None, :]
    dt_full = jnp.where(jnp.arange(2)[:, None] == x, dt_full, 0).reshape(
        groups, 2, 1, part, ratio * dt_cols
    )
    dt_full = jnp.where(
        jnp.arange(4)[:, None, None] == y * 2 + c, dt_full, 0
    ).reshape(width, ratio * dt_cols)
    two_grads = jnp.concatenate(
        [
            kv_grads,
            rest_w[:, 2 * wide + HD : 2 * wide + HD + bc_cols],
            gain_one_part.astype(BF16)[:, None],
            gain_two_part.astype(BF16)[:, None],
            dt_full,
            jnp.zeros((width, total_cols - used), BF16),
        ],
        axis=1,
    )
    two_part = cube_scatter(two_grads.reshape(groups, 8, part, total_cols), 1).astype(BF16)
    two_part = line_scatter(lambda at: lax.dynamic_index_in_dim(two_part, at, 0, False))
    kv_grad = two_part[:, :kv_cols].reshape(kv_w.shape)
    bc_grad = two_part[:, kv_cols:lead]
    dt_grad = two_part[:, lead + 2 : used].reshape(part, ratio, dt_cols)
    dt_grad = dt_grad.transpose(1, 0, 2).reshape(rows_w, dt_cols)
    small = jnp.stack(
        [sums[0, :heads], sums[1, :heads], jnp.sum(skip_sums[0].reshape(heads, MP), axis=1)]
    )
    small_pair = jnp.zeros((2, 3, heads), F32)
    small_pair = lax.dynamic_update_index_in_dim(small_pair, small, x, 0)
    small_pair = lax.dynamic_update_index_in_dim(small_pair, swap(small, "x"), x ^ 1, 0)
    small_line = line_gather(
        [small_pair],
        lambda out, at, number, value: lax.dynamic_update_slice(out, value[None], (at, 0, 0, 0)),
        jnp.zeros((groups, 2, 3, heads), F32),
    )
    small_sum = jnp.sum(small_line, axis=0).transpose(1, 0, 2).reshape(3, 2 * heads)
    return (
        layer_out,
        input_grad,
        two_part[:, lead],
        one_part[:, :, :inner].reshape(rows_w, 2 * inner),
        kv_grad,
        one_part[:, :, inner:].reshape(rows_w, 2, 2, wide).transpose(0, 2, 1, 3).reshape(zx_w.shape),
        dt_grad,
        bc_grad,
        small_sum[0],
        small_sum[1],
        small_sum[2],
        out_part[:, :, :inner].reshape(wo_w.shape),
        out_part[:, :, inner:].reshape(wm_w.shape),
        two_part[:, lead + 1],
        gu_part.reshape(rows_w, 2, 2, ff).transpose(0, 2, 1, 3).reshape(gu_w.shape),
        down_part.reshape(down_w.shape),
    )


def solution(mesh):
    groups = mesh.shape["blk"] // 2
    fine = Mesh(mesh.devices.reshape(groups, 2, 2, mesh.shape["head"] // 2), ("z", "x", "y", "c"))
    blk, head = ("z", "x"), ("y", "c")
    every = blk + head
    rows = P(every, None)
    return jax.shard_map(
        shards,
        mesh=fine,
        in_specs=(
            rows,
            P(blk),
            rows,
            P(every),
            P(blk, head),
            P(every, None, None),
            P(blk, None, head),
            P(blk, head),
            rows,
            P(head),
            P(head),
            P(head),
            P(blk, head),
            P(blk, head),
            P(every),
            P(blk, None, head),
            P(blk, head),
        ),
        out_specs=(
            rows,
            rows,
            P(every),
            P(blk, head),
            P(every, None, None),
            P(blk, None, head),
            P(blk, head),
            rows,
            P(head),
            P(head),
            P(head),
            P(blk, head),
            P(blk, head),
            P(every),
            P(blk, None, head),
            P(blk, head),
        ),
        check_vma=False,
    )
```

```python
import functools
import math

import jax
import jax.numpy as jnp
from jax import lax
from jax.experimental import pallas as pl
from jax.experimental.pallas import tpu as pltpu
from jax.sharding import Mesh
from jax.sharding import PartitionSpec as P

QH = 8
KVH = 2
HD = 128
MP = 64
CHUNK = 256
KEYS = 512
EPS = 1e-05
THETA = 100000000000.0
NEGATIVE = -1e30
EXACT = lax.Precision.HIGHEST
F32 = jnp.float32
BF16 = jnp.bfloat16
VMEM_BYTES = 56 * 1024 * 1024
SWAP = [(0, 1), (1, 0)]


def mm(a, b, ca, cb, precision=None):
    return lax.dot_general(
        a, b, (((ca,), (cb,)), ((), ())), preferred_element_type=F32, precision=precision
    )


def swap(a, axis):
    return lax.ppermute(a, axis, SWAP)


class Order:
    def __init__(self):
        self.done = ()

    def begin(self, *values):
        out = lax.optimization_barrier(tuple(values) + self.done)
        return out[0] if len(values) == 1 else out[: len(values)]

    def finish(self, *values):
        self.done = tuple(values)


def after(value, *earlier):
    return lax.optimization_barrier((value,) + earlier)[0]


def up_pairs(step):
    return [(i, i + 1) for i in range(step - 1, lax.axis_size("z") - 1)]


def down_pairs(step):
    return [(i, i - 1) for i in range(lax.axis_size("z") - step, 0, -1)]


class Line:
    def __init__(self, piece, both=True):
        self.ups, self.downs, self.both = [piece], [piece], both

    def moving(self):
        return (self.ups[-1], self.downs[-1]) if self.both else (self.ups[-1],)

    def step(self, moving):
        number = len(self.ups)
        self.ups.append(lax.ppermute(moving[0], "z", up_pairs(number)))
        if self.both:
            self.downs.append(lax.ppermute(moving[1], "z", down_pairs(number)))

    def place(self, out, put):
        count = lax.axis_size("z")
        here = lax.axis_index("z")
        out = put(out, here, self.ups[0])
        for step in range(1, count):
            value = self.ups[step]
            if self.both:
                value = jnp.where(here >= step, value, self.downs[count - step])
            out = put(out, (here - step + count) % count, value)
        return out


def spots(dx, dy, dc):
    x, y, c = (lax.axis_index(name) for name in "xyc")
    return ((x ^ dx) * 2 + (y ^ dy)) * 2 + (c ^ dc)


def cube_gather(piece):
    half = piece.shape[0] // 2
    by_x, by_y = swap(piece, "x"), swap(piece, "y")
    low, high = swap(by_x[:half], "y"), swap(by_y[half:], "x")
    own = jnp.concatenate([piece, by_y, by_x, low, high], axis=0)
    return own, swap(own, "c")


def cube_scatter(mine, other):
    mine = mine + swap(other, "c")
    here, to_y, to_x, far = mine[0], mine[1], mine[2], mine[3]
    half = far.shape[0] // 2
    from_x, from_y = swap(far[:half], "x"), swap(far[half:], "y")
    x_low, y_high = swap(to_x[:half], "x"), swap(to_y[half:], "y")
    x_high = swap(to_x[half:] + from_y, "x")
    y_low = swap(to_y[:half] + from_x, "y")
    by_x = jnp.concatenate([x_low, x_high], 0).astype(F32)
    by_y = jnp.concatenate([y_low, y_high], 0).astype(F32)
    return here.astype(F32) + by_x + by_y


def place_ref():
    x, y, c = (lax.axis_index(name) for name in "xyc")
    return jnp.stack([x * 2 + y, c]).astype(jnp.int32)


def settle_kernel(place, own_ref, other_ref, out_ref):
    near = (pl.program_id(0) & 1) == place[1]
    out_ref[...] = jnp.where(near, own_ref[...], other_ref[...]).reshape(out_ref.shape)


def settle(own, other, rows):
    cols = own.shape[1]
    spec = pl.BlockSpec((rows, cols), lambda i, place: ((i // 2) ^ place[0], 0))
    return call(
        settle_kernel,
        shape((8 * rows, cols), own.dtype),
        (8,),
        [spec, spec],
        pl.BlockSpec((rows, cols), lambda i, place: (i, 0)),
        prefetch=1,
    )(place_ref(), own, other)


def settle_groups_kernel(place, own_ref, other_ref, main_ref, misc_ref):
    near = (pl.program_id(0) & 1) == place[1]
    values = jnp.where(near, own_ref[...], other_ref[...])
    main = main_ref.shape[-1]
    main_ref[:, 0] = values[:, :, :main]
    misc_ref[:, 0] = values[:, :, main:]


def settle_groups(own, other, groups, main):
    rows, cols = own.shape[1:]
    spec = pl.BlockSpec((groups, rows, cols), lambda i, place: ((i // 2) ^ place[0], 0, 0))
    outs = call(
        settle_groups_kernel,
        tuple(shape((groups, 8, rows, n), own.dtype) for n in (main, cols - main)),
        (8,),
        [spec, spec],
        tuple(
            pl.BlockSpec((groups, 1, rows, n), lambda i, place: (0, i, 0, 0))
            for n in (main, cols - main)
        ),
        prefetch=1,
    )(place_ref(), own, other)
    return tuple(out.reshape(groups * 8 * rows, -1) for out in outs)


def settle_norm_kernel(place, own_ref, other_ref, gain_ref, out_ref):
    near = (pl.program_id(0) & 1) == place[1]
    values = jnp.where(near, own_ref[...], other_ref[...]).astype(F32)
    scale = lax.rsqrt(jnp.mean(values * values, axis=1, keepdims=True) + EPS)
    out_ref[...] = (values * scale * gain_ref[...]).astype(BF16)


def settle_norm(own, other, gain, rows):
    cols = own.shape[1]
    spec = pl.BlockSpec((rows, cols), lambda i, place: ((i // 2) ^ place[0], 0))
    return call(
        settle_norm_kernel,
        shape((8 * rows, cols), BF16),
        (8,),
        [spec, spec, pl.BlockSpec((1, cols), lambda i, place: (0, 0))],
        pl.BlockSpec((rows, cols), lambda i, place: (i, 0)),
        prefetch=1,
    )(place_ref(), own, other, gain)


def unsettle_kernel(place, in_ref, out_ref):
    out_ref[...] = in_ref[...]


def unsettle(values, rows):
    cols = values.shape[1]

    def source(i, place):
        return (((i % 4) ^ place[0]) * 2 + ((i // 4) ^ place[1]), 0)

    out = call(
        unsettle_kernel,
        shape(values.shape, values.dtype),
        (8,),
        [pl.BlockSpec((rows, cols), source)],
        pl.BlockSpec((rows, cols), lambda i, place: (i, 0)),
        prefetch=1,
    )(place_ref(), values)
    return out[: 4 * rows], out[4 * rows :]


def assemble_kernel(
    place, q_ref, x_ref, kv_ref, bc_ref, dt_ref, z_ref, all_ref, two_ref
):
    head = place[2]
    zero = jnp.zeros((kv_ref.shape[0], HD), BF16)
    parts = []
    for part in (kv_ref[:, :HD], kv_ref[:, HD:]):
        parts += [jnp.where(head == i, part, zero) for i in range(KVH)]
    two = jnp.concatenate(parts + [bc_ref[...]], axis=1)
    two_ref[...] = two
    all_ref[...] = jnp.concatenate(
        [q_ref[...], x_ref[...], two, dt_ref[...], z_ref[...]], axis=1
    )


def assemble(kv_head, rows, *parts):
    total = parts[0].shape[0]

    def source(i, place):
        return (((i % 4) ^ place[0]) * 2 + ((i // 4) ^ place[1]), 0)

    two = 2 * KVH * HD + parts[3].shape[1]
    wide = sum(a.shape[1] for a in parts) - parts[2].shape[1] - parts[3].shape[1] + two
    return call(
        assemble_kernel,
        (shape((total, wide), BF16), shape((total, two), BF16)),
        (8,),
        [pl.BlockSpec((rows, a.shape[1]), source) for a in parts],
        (
            pl.BlockSpec((rows, wide), lambda i, place: (i, 0)),
            pl.BlockSpec((rows, two), source),
        ),
        prefetch=1,
    )(jnp.concatenate([place_ref(), kv_head[None].astype(jnp.int32)]), *parts)


def halves(pack):
    x = lax.axis_index("x")
    own = lax.dynamic_index_in_dim(pack, x, 0, False)
    return own, lax.dynamic_index_in_dim(pack, x ^ 1, 0, False)


def weight_gather(own, got):
    x = lax.axis_index("x")
    both = jnp.concatenate([jnp.where(x == 0, own, got), jnp.where(x == 0, got, own)], axis=0)
    return lax.all_gather(both, "z", axis=0, tiled=True)


def both_halves(own, got):
    x = lax.axis_index("x")
    return jnp.stack([jnp.where(x == 0, own, got), jnp.where(x == 0, got, own)], axis=1)


def weight_scatter(grad):
    x = lax.axis_index("x")
    part = lax.psum_scatter(grad, "z", scatter_dimension=0, tiled=True)
    part = part.reshape(2, -1, grad.shape[1])
    got = swap(lax.dynamic_index_in_dim(part, x ^ 1, 0, False), "x")
    return both_halves(lax.dynamic_index_in_dim(part, x, 0, False), got).astype(F32)


def line_sum(value):
    count = lax.axis_size("z")
    ring = [(i, (i + 1) % count) for i in range(count)]
    total, moving = value, value
    for _ in range(count - 1):
        moving = lax.ppermute(moving, "z", ring)
        total = total + moving
    return total


def lanes_of(cols, heads):
    rows = cols.shape[0]
    low = lax.broadcasted_iota(jnp.int32, (rows, 2 * MP), 1) < MP
    return jnp.concatenate(
        [
            jnp.where(low, cols[:, 2 * j : 2 * j + 1], cols[:, 2 * j + 1 : 2 * j + 2])
            for j in range(heads // 2)
        ],
        axis=1,
    )


def head_sums(values):
    wide = values.shape[1]
    lane = lax.broadcasted_iota(jnp.int32, (wide, 128), 0) // MP
    pick = (lane == lax.broadcasted_iota(jnp.int32, (wide, 128), 1)).astype(F32)
    return mm(values, pick, 1, 0, EXACT)


def softplus(v):
    return jnp.maximum(v, 0.0) + jnp.log1p(jnp.exp(-jnp.abs(v)))


def sigmoid(v):
    return 1.0 / (1.0 + jnp.exp(-v))


def chunk_common(bc_ref, dt_in_ref, dt_row_ref, par_ref, par_col_ref, seg_col_ref, seg_row_ref, wide):
    heads = wide // MP
    states = bc_ref.shape[1] // 2
    b_val = bc_ref[:, :states]
    c_val = bc_ref[:, states:]
    raw = dt_in_ref[...].astype(F32) + par_ref[0:1, :]
    dt = softplus(raw)
    rate = par_ref[1:2, :]
    raw_row = dt_row_ref[...].astype(F32) + par_col_ref[:, 0:1]
    e_row = -softplus(raw_row) * par_col_ref[:, 1:2]
    first = lax.broadcasted_iota(jnp.int32, (CHUNK, CHUNK), 0)
    second = lax.broadcasted_iota(jnp.int32, (CHUNK, CHUNK), 1)
    lower = (first >= second).astype(F32)
    run = mm(lower, -dt * rate, 1, 0, EXACT)
    run_row = mm(e_row, lower, 1, 1, EXACT)
    bias = jnp.where((first >= second) & (seg_col_ref[...] == seg_row_ref[0]), 0.0, NEGATIVE)
    return heads, b_val, c_val, raw, dt, rate, run, run_row, bias, lower


def mamba_local_kernel(
    x_in_ref, bc_in_ref, dt_in_ref, dt_row_ref, par_ref, par_col_ref, skip_ref, seg_col_ref, seg_row_ref, marks_ref,
    y_ref, run_ref, held_ref, total_ref, starts_ref, state, base_run,
):
    step = pl.program_id(0)
    wide = skip_ref.shape[1]
    heads, b_val, c_val, raw, dt, rate, run, run_row, bias, _ = chunk_common(
        bc_in_ref, dt_in_ref, dt_row_ref, par_ref, par_col_ref, seg_col_ref, seg_row_ref, wide
    )

    @pl.when(step == 0)
    def _():
        state[...] = jnp.zeros_like(state)
        base_run[...] = jnp.zeros_like(base_run)

    x_val = x_in_ref[...].astype(F32)
    seg = seg_col_ref[...]
    label = marks_ref[step]
    final = marks_ref[step + 1]
    held = state[...]
    starts_ref[0] = held
    x_dt = x_val * lanes_of(dt, heads)
    x_dt_b = x_dt.astype(BF16)
    entry = jnp.where(seg == label, jnp.exp(run), 0.0)
    last = run[CHUNK - 1 : CHUNK, :]
    tail = jnp.where(seg == final, jnp.exp(last - run), 0.0)
    y_val = skip_ref[...] * x_val
    y_val = y_val + lanes_of(entry, heads) * mm(c_val, held.astype(BF16), 1, 0)
    gram = mm(c_val, b_val, 1, 1)
    low = lax.broadcasted_iota(jnp.int32, (CHUNK, 2 * MP), 1) < MP
    parts = []
    for pair in range(heads // 2):
        both = x_dt_b[:, pair * 2 * MP : (pair + 1) * 2 * MP]
        outs = []
        for h in (2 * pair, 2 * pair + 1):
            decay = jnp.exp(run[:, h : h + 1] - run_row[h : h + 1, :] + bias)
            outs.append(mm((decay * gram).astype(BF16), both, 1, 0))
        parts.append(jnp.where(low, outs[0], outs[1]))
    y_ref[...] = y_val + jnp.concatenate(parts, axis=1)
    fresh = mm(b_val, (x_dt * lanes_of(tail, heads)).astype(BF16), 0, 0)
    kept = jnp.where(label == final, jnp.exp(last), 0.0)
    new = lanes_of(jnp.broadcast_to(kept, (8, 128)), heads)[0:1] * held + fresh
    state[...] = new
    held_ref[...] = new
    run_all = run + base_run[0:1, :]
    run_ref[...] = run_all
    base_run[...] = jnp.broadcast_to(run_all[CHUNK - 1 : CHUNK, :], base_run.shape)
    total_ref[...] = jnp.exp(base_run[...])


def mamba_close_kernel(bc_in_ref, gate_ref, y_ref, run_ref, seg_col_ref, held_ref, marks_ref, out_ref, full_ref):
    wide = y_ref.shape[1]
    heads = wide // MP
    states = held_ref.shape[0]
    c_val = bc_in_ref[:, states:]
    entry = jnp.where(seg_col_ref[...] == marks_ref[0], jnp.exp(run_ref[...]), 0.0)
    y_val = y_ref[...] + lanes_of(entry, heads) * mm(c_val, held_ref[...].astype(BF16), 1, 0)
    full_ref[...] = y_val
    z_val = gate_ref[...].astype(F32)
    out_ref[...] = (y_val * z_val * sigmoid(z_val)).astype(BF16)


def mamba_grad_state_kernel(
    bc_in_ref, gate_ref, y_ref, grad_ref, run_ref, seg_col_ref, marks_ref, out_ref, gate_grad_ref
):
    wide = grad_ref.shape[1]
    heads = wide // MP
    states = out_ref.shape[0]
    c_val = bc_in_ref[:, states:]
    z_val = gate_ref[...].astype(F32)
    entry = jnp.where(seg_col_ref[...] == marks_ref[0], jnp.exp(run_ref[...]), 0.0)
    grad = grad_ref[...].astype(F32)
    sig = sigmoid(z_val)
    grad_y = grad * z_val * sig
    gate_grad_ref[...] = (grad * y_ref[...] * (sig * (1.0 + z_val * (1.0 - sig)))).astype(BF16)

    @pl.when(pl.program_id(0) == 0)
    def _():
        out_ref[...] = jnp.zeros_like(out_ref)

    out_ref[...] += mm(c_val, (grad_y * lanes_of(entry, heads)).astype(BF16), 0, 0)


def mamba_grad_kernel(
    x_in_ref, bc_in_ref, dt_in_ref, dt_row_ref, par_ref, par_col_ref, skip_ref, seg_col_ref, seg_row_ref, marks_ref,
    gate_ref, run_ref, starts_ref, held_ref, grad_ref, deep_ref,
    x_ref, bc_ref, dt_ref, sums_ref, skip_sum_ref, deep,
):
    step = pl.num_programs(0) - 1 - pl.program_id(0)
    wide = skip_ref.shape[1]
    heads, b_val, c_val, raw, dt, rate, run, run_row, bias, lower = chunk_common(
        bc_in_ref, dt_in_ref, dt_row_ref, par_ref, par_col_ref, seg_col_ref, seg_row_ref, wide
    )
    states = b_val.shape[1]

    @pl.when(pl.program_id(0) == 0)
    def _():
        deep[...] = deep_ref[...]
        sums_ref[...] = jnp.zeros_like(sums_ref)
        skip_sum_ref[...] = jnp.zeros_like(skip_sum_ref)

    z_val = gate_ref[...].astype(F32)
    x_val = x_in_ref[...].astype(F32)
    seg = seg_col_ref[...]
    label = marks_ref[step]
    final = marks_ref[step + 1]
    last = run[CHUNK - 1 : CHUNK, :]
    before = run_ref[0:1, :] - run[0:1, :]
    carry = jnp.where(label == marks_ref[0], jnp.exp(before), 0.0)
    held = starts_ref[0] + lanes_of(jnp.broadcast_to(carry, (8, 128)), heads)[0:1] * held_ref[...]
    held_b = held.astype(BF16)
    after = deep[...]
    after_b = after.astype(BF16)
    grad = grad_ref[...].astype(F32)
    sig = sigmoid(z_val)
    grad_y = grad * z_val * sig
    dt_wide = lanes_of(dt, heads)
    x_dt = x_val * dt_wide
    entry = lanes_of(jnp.where(seg == label, jnp.exp(run), 0.0), heads)
    tail = lanes_of(jnp.where(seg == final, jnp.exp(last - run), 0.0), heads)
    grad_in = (entry * grad_y).astype(BF16)
    run_grad = head_sums(grad_y * entry * mm(c_val, held_b, 1, 0))
    grad_c = mm(grad_in, held_b, 1, 1)
    x_tail = x_dt * tail
    back = mm(b_val, after_b, 1, 0)
    grad_b = mm(x_tail.astype(BF16), after_b, 1, 1)
    tail_grad = head_sums(x_tail * back)
    run_grad = run_grad - tail_grad
    kept = jnp.where(label == final, jnp.exp(last), 0.0)
    kept_wide = lanes_of(jnp.broadcast_to(kept, (8, 128)), heads)[0:1]
    kept_grad = head_sums(
        jnp.broadcast_to(kept_wide * jnp.sum(after * held, axis=0, keepdims=True), (8, wide))
    )
    last_grad = jnp.sum(tail_grad, axis=0, keepdims=True) + kept_grad[0:1]
    deep[...] = kept_wide * after + mm(c_val, grad_in, 0, 0)
    gram = mm(c_val, b_val, 1, 1)
    low = lax.broadcasted_iota(jnp.int32, (CHUNK, 2 * MP), 1) < MP
    lane = lax.broadcasted_iota(jnp.int32, (CHUNK, 128), 1)
    x_dt_b = x_dt.astype(BF16)
    grad_y_b = grad_y.astype(BF16)
    none = jnp.zeros((CHUNK, 2 * MP), BF16)
    gram_grad = None
    parts, cols = [], []
    for pair in range(heads // 2):
        span = slice(pair * 2 * MP, (pair + 1) * 2 * MP)
        outs = []
        for h in (2 * pair, 2 * pair + 1):
            mask = low if h % 2 == 0 else ~low
            decay = jnp.exp(run[:, h : h + 1] - run_row[h : h + 1, :] + bias)
            mixing = (decay * gram).astype(BF16)
            outs.append(mm(mixing, grad_y_b[:, span], 0, 0))
            mixing_grad = mm(jnp.where(mask, grad_y_b[:, span], none), x_dt_b[:, span], 1, 1)
            weighted = mixing_grad * decay
            gram_grad = weighted if gram_grad is None else gram_grad + weighted
            weighted = weighted * gram
            run_grad = run_grad + jnp.where(
                lane == h, jnp.sum(weighted, axis=1, keepdims=True), 0.0
            )
            cols.append(jnp.sum(weighted, axis=0, keepdims=True))
        parts.append(jnp.where(low, outs[0], outs[1]))
    gram_grad_b = gram_grad.astype(BF16)
    grad_c = grad_c + mm(gram_grad_b, b_val, 1, 0)
    grad_b = grad_b + mm(gram_grad_b, c_val, 0, 0)
    x_dt_grad = jnp.concatenate(parts, axis=1) + tail * back
    x_ref[...] = (x_dt_grad * dt_wide + skip_ref[...] * grad_y).astype(BF16)
    bc_ref[:, :states] = grad_b.astype(BF16)
    bc_ref[:, states:] = grad_c.astype(BF16)
    col_grad = jnp.concatenate(cols + [jnp.zeros((128 - heads, CHUNK), F32)], axis=0)
    e_grad = mm(lower, run_grad, 0, 0, EXACT) - mm(lower, col_grad, 0, 1, EXACT) + last_grad
    dt_grad = head_sums(x_dt_grad * x_val) - rate * e_grad
    raw_grad = dt_grad * sigmoid(raw)
    dt_ref[...] = jnp.where(lane < heads, raw_grad, 0.0).astype(BF16)
    sums_ref[0:1, :] += jnp.sum(-rate * dt * e_grad, axis=0, keepdims=True)
    sums_ref[1:2, :] += jnp.sum(raw_grad, axis=0, keepdims=True)
    skip_sum_ref[0:1, :] += jnp.sum(grad_y * x_val, axis=0, keepdims=True)


def seen(kseg_ref, qseg, first_query, block):
    rows = qseg.shape[0]
    key_pos = block * KEYS + lax.broadcasted_iota(jnp.int32, (rows, KEYS), 1)
    query_pos = first_query + lax.broadcasted_iota(jnp.int32, (rows, KEYS), 0)
    return (key_pos <= query_pos) & (kseg_ref[pl.ds(block, 1), :] == qseg)


def attend_kernel(low_ref, high_ref, start_ref, q_ref, kv_ref, kseg_ref, qseg_ref, att_ref, log_ref):
    step = pl.program_id(0)
    rows = q_ref.shape[0]
    query = q_ref[...]
    qseg = qseg_ref[...]
    first_query = start_ref[0] + step * rows
    scale = HD**-0.5

    def visit(block, state):
        peak, total, acc = state
        span = pl.ds(pl.multiple_of(block * KEYS, KEYS), KEYS)
        scores = mm(query, kv_ref[span, :HD], 1, 1) * scale
        scores = jnp.where(seen(kseg_ref, qseg, first_query, block), scores, NEGATIVE)
        new_peak = jnp.maximum(peak, jnp.max(scores, axis=1, keepdims=True))
        weights = jnp.exp(scores - new_peak)
        rescale = jnp.exp(peak - new_peak)
        total = total * rescale + jnp.sum(weights, axis=1, keepdims=True)
        acc = acc * rescale + mm(weights.astype(BF16), kv_ref[span, HD:], 1, 0)
        return new_peak, total, acc

    peak, total, acc = lax.fori_loop(
        low_ref[step],
        high_ref[step],
        visit,
        (
            jnp.full((rows, 1), NEGATIVE, F32),
            jnp.zeros((rows, 1), F32),
            jnp.zeros((rows, HD), F32),
        ),
    )
    att_ref[...] = acc / total
    log_ref[...] = jnp.broadcast_to(peak + jnp.log(total), log_ref.shape)


def attend_grad_kernel(
    low_ref, high_ref, start_ref, q_ref, kv_ref, kseg_ref, qseg_ref, att_ref, log_ref, grad_ref,
    dq_ref, dkv_ref, sums,
):
    step = pl.program_id(0)
    rows = q_ref.shape[0]
    query = q_ref[...]
    grad = grad_ref[...]
    qseg = qseg_ref[...]
    log_total = log_ref[:, 0:1]
    first_query = start_ref[0] + step * rows
    scale = HD**-0.5
    delta = jnp.sum(grad.astype(F32) * att_ref[...], axis=1, keepdims=True)

    @pl.when(step == 0)
    def _():
        sums[...] = jnp.zeros_like(sums)

    def visit(block, acc):
        span = pl.ds(pl.multiple_of(block * KEYS, KEYS), KEYS)
        keys = kv_ref[span, :HD]
        scores = mm(query, keys, 1, 1) * scale - log_total
        scores = jnp.where(seen(kseg_ref, qseg, first_query, block), scores, NEGATIVE)
        probs = jnp.exp(scores)
        probs_grad = mm(grad, kv_ref[span, HD:], 1, 1)
        scores_grad = (probs * (probs_grad - delta)).astype(BF16)
        sums[span, :HD] += mm(scores_grad, query, 0, 0)
        sums[span, HD:] += mm(probs.astype(BF16), grad, 0, 0)
        return acc + mm(scores_grad, keys, 1, 0)

    acc = lax.fori_loop(low_ref[step], high_ref[step], visit, jnp.zeros((rows, HD), F32))
    dq_ref[...] = acc * scale

    @pl.when(step == pl.num_programs(0) - 1)
    def _():
        dkv_ref[:, :HD] = (sums[:, :HD] * scale).astype(BF16)
        dkv_ref[:, HD:] = sums[:, HD:].astype(BF16)


def call(kernel, out_shape, grid, in_specs, out_specs, scratch=(), prefetch=0, cost=None):
    return pl.pallas_call(
        kernel,
        out_shape=out_shape,
        grid_spec=pltpu.PrefetchScalarGridSpec(
            num_scalar_prefetch=prefetch,
            grid=grid,
            in_specs=in_specs,
            out_specs=out_specs,
            scratch_shapes=list(scratch),
        ),
        compiler_params=pltpu.CompilerParams(
            vmem_limit_bytes=VMEM_BYTES, dimension_semantics=("arbitrary",) * len(grid)
        ),
        cost_estimate=cost,
        name=kernel.__name__,
    )


def shape(dims, dtype=F32):
    return jax.ShapeDtypeStruct(dims, dtype)


def rope_tables(positions):
    half = HD // 2
    frequency = jnp.exp(jnp.arange(half, dtype=F32) * (-2.0 * math.log(THETA) / HD))
    angle = positions.astype(F32)[:, None] * frequency[None, :]
    cosine, sine = jnp.cos(angle), jnp.sin(angle)
    return jnp.concatenate([cosine, cosine], 1), jnp.concatenate([-sine, sine], 1)


def rope(values, tables):
    cosine, sine = tables
    return values * cosine + jnp.concatenate([values[:, HD // 2 :], values[:, : HD // 2]], 1) * sine


def rope_back(values, tables):
    cosine, sine = tables
    return values * cosine - jnp.concatenate([values[:, HD // 2 :], values[:, : HD // 2]], 1) * sine


def unit(values):
    return values * lax.rsqrt(jnp.mean(values * values, axis=-1, keepdims=True) + EPS)


def norm_back(values, gain, grad):
    scale = lax.rsqrt(jnp.mean(values * values, axis=-1, keepdims=True) + EPS)
    u = values * scale
    inner = jnp.mean(grad * gain * u, axis=-1, keepdims=True)
    return scale * (grad * gain - u * inner), jnp.sum(grad * u, axis=0)


def shards(
    tokens, seg_ids, cotangent, gain_mix, q_w, kv_w, zx_w, dt_w, bc_w,
    a_log, dt_bias, skip, wo_w, wm_w, gain_ff, gu_w, down_w,
):
    groups = lax.axis_size("z")
    z, x, y, c = (lax.axis_index(name) for name in "zxyc")
    own_rows, width = tokens.shape
    group = 8 * own_rows
    rows_w = q_w.shape[0]
    part = kv_w.shape[0]
    ratio = rows_w // part
    heads = dt_w.shape[1] // 2
    wide = heads * MP
    states = bc_w.shape[1] // 2
    ff = gu_w.shape[2] // 2
    inner = q_w.shape[1] // 2
    steps = group // CHUNK

    zx_cut = zx_w.reshape(rows_w, 2, 2, wide).transpose(1, 2, 0, 3)
    pack_z = zx_cut[0]
    pack_one = jnp.concatenate([q_w.reshape(rows_w, 2, inner).transpose(1, 0, 2), zx_cut[1]], axis=2)
    pack_out = jnp.concatenate(
        [
            wo_w.reshape(rows_w, 2, inner).transpose(1, 0, 2),
            wm_w.reshape(rows_w, 2, wide).transpose(1, 0, 2),
        ],
        axis=2,
    )
    pack_gu = gu_w.reshape(rows_w, 2, 2, ff).transpose(2, 0, 1, 3).reshape(2, rows_w, 2 * ff)
    pack_down = down_w.reshape(rows_w, 2, ff).transpose(1, 0, 2)
    kv_cols = kv_w.shape[1] * kv_w.shape[2]
    bc_cols = bc_w.shape[1]
    lead = kv_cols + bc_cols
    dt_cols = dt_w.shape[1]
    dt_part = dt_w.reshape(ratio, part, dt_cols).transpose(1, 0, 2).reshape(part, ratio * dt_cols)
    pack_two = jnp.concatenate(
        [kv_w.reshape(part, kv_cols), bc_w, gain_mix[:, None], gain_ff[:, None], dt_part], axis=1
    )
    used = pack_two.shape[1]
    total_cols = -(-used // 128) * 128
    pack_two = jnp.pad(pack_two, ((0, 0), (0, total_cols - used)))

    def put_two(out, at, number, value):
        return lax.dynamic_update_slice(out, value[None], (at, 0, 0))

    own_one, give_one = halves(pack_one)
    own_z, give_z = halves(pack_z)
    own_out, give_out = halves(pack_out)
    own_gu, give_gu = halves(pack_gu)
    own_down, give_down = halves(pack_down)
    w_one = weight_gather(own_one, swap(give_one, "x"))
    line_two = Line(pack_two)
    for step in range(1, groups):
        line_two.step(line_two.moving())
    two = line_two.place(
        jnp.zeros((groups,) + pack_two.shape, BF16),
        lambda out, at, value: lax.dynamic_update_slice(out, value[None], (at, 0, 0)),
    )
    rows_own, rows_other = cube_gather(tokens)
    w_two, misc = settle_groups(*cube_gather(two), groups, lead)
    got_z, got_out = swap(after(give_z, rows_own), "x"), swap(after(give_out, rows_own), "x")
    w_z = weight_gather(own_z, got_z)
    w_out = weight_gather(own_out, got_out)
    w_gu = weight_gather(own_gu, swap(after(give_gu, got_out), "x"))
    w_down = weight_gather(own_down, swap(after(give_down, got_out), "x"))

    seg_pair = jnp.zeros((2, seg_ids.shape[0]), jnp.int32)
    seg_pair = lax.dynamic_update_index_in_dim(seg_pair, seg_ids, x, 0)
    seg_pair = lax.dynamic_update_index_in_dim(seg_pair, swap(seg_ids, "x"), x ^ 1, 0)
    seg_own = seg_pair.reshape(1, group)
    seg_line = Line(seg_own, both=False)
    for step in range(1, groups):
        seg_line.step(seg_line.moving())
    seg_all = seg_line.place(
        jnp.zeros((groups, group), jnp.int32),
        lambda out, at, value: lax.dynamic_update_slice(out, value, (at, 0)),
    )
    segment = seg_own.astype(F32)
    seg_col = segment.reshape(group, 1)
    seg_row = segment.reshape(steps, 1, CHUNK)
    previous = lax.dynamic_index_in_dim(seg_all, jnp.maximum(z - 1, 0), 0, False)[group - 1]
    in_label = jnp.where(z > 0, previous, -1).astype(F32)
    marks = jnp.concatenate([in_label[None], segment[0, CHUNK - 1 :: CHUNK]])

    gain_one = misc[:, 0].astype(F32)
    gain_two = misc[:, 1].astype(F32)
    dt_all = misc[:, 2 : 2 + ratio * dt_cols].reshape(
        groups, 2, 4, part, ratio, 2, heads
    )
    dt_own = lax.dynamic_index_in_dim(dt_all, y * 2 + c, 2, False)
    dt_own = lax.dynamic_index_in_dim(dt_own, x, 4, False)
    w_dt = dt_own.transpose(0, 1, 3, 2, 4).reshape(width, heads)
    kv_head = ((y * 2 + c) * 2 + x) * (inner // HD) // (QH // KVH)
    w_dt = jnp.pad(w_dt, ((0, 0), (0, 128 - heads)))

    normed = settle_norm(rows_own, rows_other, gain_one[None, :], own_rows)
    positions = z * group + jnp.arange(group, dtype=jnp.int32)
    tables = rope_tables(positions)
    one = mm(normed, w_one, 1, 0)
    other = mm(normed, w_two, 1, 0).astype(BF16)
    dt_in = mm(normed, w_dt, 1, 0).astype(BF16)
    query = rope(one[:, :inner], tables).astype(BF16)
    x_in = one[:, inner:].astype(BF16)
    bc_in = other[:, kv_cols:lead]
    key = lax.dynamic_slice_in_dim(other, kv_head * HD, HD, 1).astype(F32)
    value = lax.dynamic_slice_in_dim(other, kv_cols // 2 + kv_head * HD, HD, 1)
    kv_own = jnp.concatenate([rope(key, tables).astype(BF16), value], axis=1)
    x_in, w_z = lax.optimization_barrier((x_in, w_z))
    cotangent_now = after(cotangent, normed)
    gate_in = mm(normed, w_z, 1, 0).astype(BF16)

    dt_row = jnp.pad(dt_in[:, :8].T, ((0, 8), (0, 0)))
    pad = ((0, 128 - heads),)

    def pick(values):
        return lax.dynamic_slice_in_dim(values, x * heads, heads, 0)

    rates = jnp.exp(pick(a_log))
    params = jnp.stack([jnp.pad(pick(dt_bias), pad), jnp.pad(rates, pad)])
    params = jnp.pad(params, ((0, 6), (0, 0)))
    params_col = jnp.pad(
        jnp.stack([pick(dt_bias), rates], axis=1), ((0, 16 - heads), (0, 126))
    )
    skip_wide = jnp.repeat(pick(skip), MP)[None, :]

    def flow(cols, back=False):
        at = (lambda i: (steps - 1 - i, 0)) if back else (lambda i: (i, 0))
        return pl.BlockSpec((CHUNK, cols), at)

    def chunk_specs(back=False):
        def turn(i):
            return steps - 1 - i if back else i

        return [
            flow(wide, back),
            flow(2 * states, back),
            flow(128, back),
            pl.BlockSpec((16, CHUNK), lambda i: (0, turn(i))),
            pl.BlockSpec((8, 128), lambda i: (0, 0)),
            pl.BlockSpec((16, 128), lambda i: (0, 0)),
            pl.BlockSpec((1, wide), lambda i: (0, 0)),
            flow(1, back),
            pl.BlockSpec((1, 1, CHUNK), lambda i: (turn(i), 0, 0)),
            pl.BlockSpec(memory_space=pltpu.SMEM),
        ]

    whole = pl.BlockSpec((states, wide), lambda i: (0, 0))
    smem = pl.BlockSpec(memory_space=pltpu.SMEM)
    chunk_args = (x_in, bc_in, dt_in, dt_row, params, params_col, skip_wide, seg_col, seg_row, marks)
    y_local, run, held_own, total, starts = call(
        mamba_local_kernel,
        (
            shape((group, wide)),
            shape((group, 128)),
            shape((states, wide)),
            shape((8, 128)),
            shape((steps, states, wide)),
        ),
        (steps,),
        chunk_specs(),
        (
            flow(wide),
            flow(128),
            whole,
            pl.BlockSpec((8, 128), lambda i: (0, 0)),
            pl.BlockSpec((1, states, wide), lambda i: (i, 0, 0)),
        ),
        [pltpu.VMEM((states, wide), F32), pltpu.VMEM((8, 128), F32)],
    )(*chunk_args)
    joined = jnp.where(in_label == segment[0, group - 1], 1.0, 0.0)
    factor = jnp.repeat(total[0, :heads] * joined, MP)[None, :]
    half = group // 2
    kv_line = Line(lax.dynamic_slice_in_dim(kv_own, c * half, half, 0), both=False)
    order = Order()
    entering = jnp.zeros((states, wide), BF16)
    for step in range(1, groups + 1):
        if step == 1:
            kv_line.step((order.begin(*kv_line.moving()),))
            order.finish(*kv_line.moving())
            continue
        leaving = held_own if step == 2 else held_own + factor * entering.astype(F32)
        leaving = leaving.astype(BF16)
        if step < groups:
            moving, leaving = order.begin(*kv_line.moving(), leaving)
            kv_line.step((moving,))
        entering = lax.ppermute(leaving, "z", up_pairs(1))
        order.finish(*kv_line.moving(), entering)
    in_held = entering
    kv_got = kv_line.place(
        jnp.zeros((groups, half, 2 * HD), BF16),
        lambda out, at, value: lax.dynamic_update_slice(out, value[None], (at, 0, 0)),
    )
    kv_all = jnp.zeros((groups, 2, half, 2 * HD), BF16)
    kv_all = lax.dynamic_update_index_in_dim(kv_all, kv_got, c, 1)
    kv_all = lax.dynamic_update_index_in_dim(kv_all, swap(kv_got, "c"), c ^ 1, 1)
    kv_all = kv_all.reshape(groups * group, 2 * HD)
    cot_own, cot_other = cube_gather(cotangent_now)
    query, cot_own, cot_other, w_out = lax.optimization_barrier((query, cot_own, cot_other, w_out))
    w_all = jnp.concatenate([w_one, w_two, w_dt, w_z], axis=1)

    q_rows = CHUNK
    blocks = group // q_rows
    first_rows = z * group + q_rows * jnp.arange(blocks, dtype=jnp.int32)
    first_seg = seg_own[0, ::q_rows]
    reached = jnp.arange(groups * group, dtype=jnp.int32)[None, :] < (z + 1) * group
    earlier = (seg_all.reshape(1, -1) < first_seg[:, None]) & reached
    low = jnp.sum(earlier, axis=1, dtype=jnp.int32) // KEYS
    high = (first_rows + q_rows - 1) // KEYS + 1
    start = (z * group)[None].astype(jnp.int32)
    key_seg = seg_all.astype(F32).reshape(groups * group // KEYS, KEYS)

    def rows_spec(cols):
        return pl.BlockSpec((q_rows, cols), lambda i, *_: (i, 0))

    def full_spec(a):
        return pl.BlockSpec(a.shape, lambda i, *_: (0, 0))

    att_full, log_total = call(
        attend_kernel,
        (shape((group, HD)), shape((group, 128))),
        (blocks,),
        [rows_spec(HD), full_spec(kv_all), full_spec(key_seg), rows_spec(1)],
        (rows_spec(HD), rows_spec(128)),
        prefetch=3,
    )(low, high, start, query, kv_all, key_seg, seg_col)

    ssm_out, y_full = call(
        mamba_close_kernel,
        (shape((group, wide), BF16), shape((group, wide))),
        (steps,),
        [flow(2 * states), flow(wide), flow(wide), flow(128), flow(1), whole, smem],
        (flow(wide), flow(wide)),
    )(bc_in, gate_in, y_local, run, seg_col, in_held, marks)
    mixer_out = jnp.concatenate([att_full.astype(BF16), ssm_out], axis=1)

    def to_rows(mine, other):
        def term(products):
            total = None
            for a, w in products:
                value = mm(a, w, 1, 1)
                total = value if total is None else total + value
            return total.astype(BF16).reshape(4, own_rows, width)

        return cube_scatter(term(mine), term(other))

    def weight_grad(pairs):
        total = None
        for a, g in pairs:
            value = mm(a, g, 0, 0)
            total = value if total is None else total + value
        return weight_scatter(total.astype(BF16))

    stream_own = tokens.astype(F32)
    mixer_own, mixer_other = unsettle(mixer_out, own_rows)
    middle = stream_own + to_rows([(mixer_own, w_out)], [(mixer_other, w_out)])
    normed_two = (unit(middle) * gain_two).astype(BF16)
    normed_two, w_gu = lax.optimization_barrier((normed_two, w_gu))
    two_rows = cube_gather(normed_two)

    def forward(rows):
        gate_up = mm(rows, w_gu, 1, 0).astype(BF16)
        gate = gate_up[:, :ff].astype(F32)
        up = gate_up[:, ff:].astype(F32)
        sig = jax.nn.sigmoid(gate)
        return gate, up, sig, (gate * sig * up).astype(BF16)

    def backward(rows, gate, up, sig):
        grad_hidden = mm(rows, w_down, 1, 0).astype(BF16).astype(F32)
        grad_gate = grad_hidden * up * (sig * (1.0 + gate * (1.0 - sig)))
        return jnp.concatenate([grad_gate, grad_hidden * gate * sig], axis=1).astype(BF16)

    *kept_own, hidden_own = forward(two_rows[0])
    *kept_other, hidden_other = forward(two_rows[1])
    gu_other = backward(cot_other, *kept_other)
    gu_own = backward(cot_own, *kept_own)
    grad_normed_two = to_rows([(gu_own, w_gu)], [(gu_other, w_gu)])
    down_part = weight_grad([(cot_own, hidden_own), (cot_other, hidden_other)])
    gu_part = weight_grad([(two_rows[0], gu_own), (two_rows[1], gu_other)])
    middle_part, gain_two_part = norm_back(middle, gain_two, grad_normed_two)
    grad_middle = cotangent.astype(F32) + middle_part
    mixed_own, mixed_other = cube_gather(grad_middle.astype(BF16))
    hidden_own, hidden_other = after(hidden_own, mixed_own), after(hidden_other, mixed_own)
    layer_out = middle + to_rows([(hidden_own, w_down)], [(hidden_other, w_down)])
    layer_out = layer_out.astype(BF16)
    grad_mixer = settle(
        mm(mixed_own, w_out, 1, 0).astype(BF16), mm(mixed_other, w_out, 1, 0).astype(BF16), own_rows
    )
    out_part = weight_grad([(mixed_own, mixer_own), (mixed_other, mixer_other)])

    grad_att = grad_mixer[:, :inner]
    grad_ssm = grad_mixer[:, inner:]
    state_grad, grad_z = call(
        mamba_grad_state_kernel,
        (shape((states, wide)), shape((group, wide), BF16)),
        (steps,),
        [flow(2 * states), flow(wide), flow(wide), flow(wide), flow(128), flow(1), smem],
        (whole, flow(wide)),
    )(bc_in, gate_in, y_full, grad_ssm, run, seg_col, marks)
    order = Order()
    grad_att, down_part = lax.optimization_barrier((after(grad_att, state_grad), down_part))
    deep = lax.ppermute(state_grad.astype(BF16), "z", down_pairs(1))
    grad_query, grad_kv_all = call(
        attend_grad_kernel,
        (shape((group, HD)), shape((groups * group, 2 * HD), BF16)),
        (blocks,),
        [
            rows_spec(HD), full_spec(kv_all), full_spec(key_seg), rows_spec(1),
            rows_spec(HD), rows_spec(128), rows_spec(HD),
        ],
        (rows_spec(HD), full_spec(kv_all)),
        [pltpu.VMEM((groups * group, 2 * HD), F32)],
        prefetch=3,
    )(low, high, start, query, kv_all, key_seg, seg_col, att_full, log_total, grad_att)
    kv_terms = grad_kv_all.reshape(groups, 2, half, 2 * HD)
    kv_terms = lax.dynamic_index_in_dim(kv_terms, c, 1, False) + swap(
        lax.dynamic_index_in_dim(kv_terms, c ^ 1, 1, False), "c"
    )
    def kv_term(at):
        at = jnp.clip(at, 0, groups - 1)
        return lax.dynamic_index_in_dim(kv_terms, at, 0, False)

    moved = None
    for step in range(1, groups):
        give = kv_term(z - (groups - step))
        give = give if moved is None else give + moved
        order.finish(deep)
        leaving = (state_grad + factor * deep.astype(F32)).astype(BF16)
        if step < groups - 1:
            give, leaving = order.begin(give, leaving)
            deep = lax.ppermute(leaving, "z", down_pairs(1))
        last_ones = [(i, i - 1) for i in range(groups - 1, groups - 1 - step, -1)]
        moved = lax.ppermute(give, "z", last_ones)
        order.finish(deep, moved)
    deep, gu_part = lax.optimization_barrier((deep.astype(F32), gu_part))
    grad_kv_half = kv_term(z).astype(F32) + moved.astype(F32)
    half_tables = tuple(lax.dynamic_slice_in_dim(table, c * half, half, 0) for table in tables)
    grad_kv_half = jnp.concatenate(
        [rope_back(grad_kv_half[:, :HD], half_tables), grad_kv_half[:, HD:]], axis=1
    ).astype(BF16)
    grad_kv = lax.dynamic_update_slice(
        jnp.zeros((group, 2 * HD), BF16), grad_kv_half, (c * half, 0)
    )
    grad_q = rope_back(grad_query, tables).astype(BF16)
    grad_qz = jnp.concatenate([grad_q, grad_z], axis=1)
    qz_w = mm(normed, grad_qz, 0, 0)
    qz_part = weight_scatter(qz_w.astype(BF16))
    grad_x, grad_bc, grad_dt, sums, skip_sums = call(
        mamba_grad_kernel,
        (
            shape((group, wide), BF16),
            shape((group, 2 * states), BF16),
            shape((group, 128), BF16),
            shape((8, 128)),
            shape((8, wide)),
        ),
        (steps,),
        chunk_specs(True)
        + [
            flow(wide, True),
            flow(128, True),
            pl.BlockSpec((1, states, wide), lambda i: (steps - 1 - i, 0, 0)),
            whole,
            flow(wide, True),
            whole,
        ],
        (
            flow(wide, True),
            flow(2 * states, True),
            flow(128, True),
            pl.BlockSpec((8, 128), lambda i: (0, 0)),
            pl.BlockSpec((8, wide), lambda i: (0, 0)),
        ),
        [pltpu.VMEM((states, wide), F32)],
    )(*chunk_args, gate_in, run, starts, in_held, grad_ssm, deep)

    grad_x, out_part = lax.optimization_barrier((grad_x, out_part))
    x_w = mm(normed, grad_x, 0, 0)
    x_part = weight_scatter(x_w.astype(BF16))
    grad_all, grad_two = assemble(
        kv_head, own_rows, grad_q, grad_x, grad_kv, grad_bc, grad_dt, grad_z
    )
    cut = group // 2
    in_grad = to_rows([(grad_all[:cut], w_all)], [(grad_all[cut:], w_all)])
    input_part, _ = norm_back(stream_own, gain_one, in_grad)
    input_grad = grad_middle + input_part
    two_w = mm(normed, grad_two, 0, 0)
    dt_w_grad = mm(normed, grad_dt, 0, 0)
    two_cut = two_w.astype(BF16).reshape(groups, 8, part, lead)

    def two_terms(core):
        spot = [((x ^ dx) * 2 + (y ^ dy)) * 2 + core for dx, dy in ((0, 0), (0, 1), (1, 0), (1, 1))]
        return jnp.stack([lax.dynamic_index_in_dim(two_cut, at, 1, False) for at in spot])

    two_part = cube_scatter(two_terms(c), two_terms(c ^ 1)).astype(BF16)
    two_part = lax.psum_scatter(two_part, "z", scatter_dimension=0).astype(F32)
    kv_grad = two_part[:, :kv_cols].reshape(kv_w.shape)
    bc_grad = two_part[:, kv_cols:lead]
    gain_one_part = jnp.sum(two_w * w_two.astype(F32), axis=1)
    gain_one_part += jnp.sum(dt_w_grad * w_dt.astype(F32), axis=1)
    gain_one_part += jnp.sum(x_w * w_one[:, inner:].astype(F32), axis=1)
    gain_one_part += jnp.sum(qz_w[:, :inner] * w_one[:, :inner].astype(F32), axis=1)
    gain_one_part += jnp.sum(qz_w[:, inner:] * w_z.astype(F32), axis=1)
    gain_one_part = gain_one_part / gain_one
    small = jnp.concatenate(
        [sums[0, :heads], sums[1, :heads], jnp.sum(skip_sums[0].reshape(heads, MP), axis=1)]
    )
    small = jnp.pad(small, (0, width - small.shape[0]))
    tiny = jnp.concatenate(
        [dt_w_grad[:, :heads].T, jnp.stack([small, gain_one_part, gain_two_part])], axis=0
    )
    tiny = line_sum(tiny)
    gains = tiny[heads + 1 :]
    gains = gains + swap(gains, "c")
    gains = gains + swap(gains, "y")
    tiny_other = swap(jnp.concatenate([tiny[: heads + 1], gains], axis=0), "x")
    gains = gains + tiny_other[heads + 1 :]
    spot = spots(0, 0, 0) + z * 8
    gain_grads = lax.dynamic_slice_in_dim(gains, spot * part, part, 1)
    dt_grad = both_halves(
        *(
            lax.dynamic_slice_in_dim(a[:heads], (z * 2 + x) * rows_w, rows_w, 1).T
            for a in (tiny, tiny_other)
        )
    ).reshape(rows_w, dt_cols)
    small_sum = both_halves(
        *(a[heads, : 3 * heads].reshape(3, heads) for a in (tiny, tiny_other))
    ).reshape(3, dt_cols)
    return (
        layer_out,
        input_grad,
        gain_grads[0],
        qz_part[:, :, :inner].reshape(rows_w, 2 * inner),
        kv_grad,
        jnp.stack([qz_part[:, :, inner:], x_part], axis=1).reshape(zx_w.shape),
        dt_grad,
        bc_grad,
        small_sum[0],
        small_sum[1],
        small_sum[2],
        out_part[:, :, :inner].reshape(wo_w.shape),
        out_part[:, :, inner:].reshape(wm_w.shape),
        gain_grads[1],
        gu_part.reshape(rows_w, 2, 2, ff).transpose(0, 2, 1, 3).reshape(gu_w.shape),
        down_part.reshape(down_w.shape),
    )


def solution(mesh):
    groups = mesh.shape["blk"] // 2
    fine = Mesh(mesh.devices.reshape(groups, 2, 2, mesh.shape["head"] // 2), ("z", "x", "y", "c"))
    blk, head = ("z", "x"), ("y", "c")
    every = blk + head
    rows = P(every, None)
    return jax.shard_map(
        shards,
        mesh=fine,
        in_specs=(
            rows,
            P(blk),
            rows,
            P(every),
            P(blk, head),
            P(every, None, None),
            P(blk, None, head),
            P(blk, head),
            rows,
            P(head),
            P(head),
            P(head),
            P(blk, head),
            P(blk, head),
            P(every),
            P(blk, None, head),
            P(blk, head),
        ),
        out_specs=(
            rows,
            rows,
            P(every),
            P(blk, head),
            P(every, None, None),
            P(blk, None, head),
            P(blk, head),
            rows,
            P(head),
            P(head),
            P(head),
            P(blk, head),
            P(blk, head),
            P(every),
            P(blk, None, head),
            P(blk, head),
        ),
        check_vma=False,
    )
```

```python
import functools
import math

import jax
import jax.numpy as jnp
from jax import lax
from jax.experimental import pallas as pl
from jax.experimental.pallas import tpu as pltpu
from jax.sharding import Mesh
from jax.sharding import PartitionSpec as P

QH = 8
KVH = 2
HD = 128
MP = 64
CHUNK = 256
KEYS = 512
EPS = 1e-05
THETA = 100000000000.0
NEGATIVE = -1e30
EXACT = lax.Precision.HIGHEST
F32 = jnp.float32
BF16 = jnp.bfloat16
VMEM_BYTES = 56 * 1024 * 1024
SWAP = [(0, 1), (1, 0)]


def mm(a, b, ca, cb, precision=None):
    return lax.dot_general(
        a, b, (((ca,), (cb,)), ((), ())), preferred_element_type=F32, precision=precision
    )


def scoped(function):
    def named(name, *args, **kwargs):
        with jax.named_scope(name):
            return function(*args, **kwargs)

    return named


def swap(a, axis):
    return lax.ppermute(a, axis, SWAP)


def after(value, *earlier):
    return lax.optimization_barrier((value,) + earlier)[0]


@scoped
def from_below(values):
    count = lax.axis_size("z")
    return [
        lax.ppermute(values[far], "z", [(i, i + far) for i in range(count - far)])
        for far in range(1, count)
    ]


@scoped
def from_above(values):
    count = lax.axis_size("z")
    return [
        lax.ppermute(values[far], "z", [(i + far, i) for i in range(count - far)])
        for far in range(1, count)
    ]


@scoped
def from_ring(value):
    count = lax.axis_size("z")
    return [
        lax.ppermute(value, "z", [(i, (i + far) % count) for i in range(count)])
        for far in range(1, count)
    ]


def spots(dx, dy, dc):
    x, y, c = (lax.axis_index(name) for name in "xyc")
    return ((x ^ dx) * 2 + (y ^ dy)) * 2 + (c ^ dc)


@scoped
def cube_gather(piece, split=0, gate=None):
    by_x, by_y = swap(piece, "x"), swap(piece, "y")
    if gate is not None:
        by_x, by_y = after(by_x, gate), after(by_y, gate)
    low = swap(jnp.split(by_x, 2, split)[0], "y")
    high = swap(jnp.split(by_y, 2, split)[1], "x")
    far = [low, high] if split == 0 else [jnp.concatenate([low, high], axis=split)]
    own = jnp.concatenate([piece, by_y, by_x] + far, axis=0)
    return own, swap(own, "c"), by_x, low


@scoped
def cube_scatter(mine, other, gate=None):
    mine = mine + swap(other, "c")
    if gate is not None:
        mine = after(mine, gate)
    here, to_y, to_x, far = mine[0], mine[1], mine[2], mine[3]
    half = far.shape[0] // 2
    from_x, from_y = swap(far[:half], "x"), swap(far[half:], "y")
    x_low, y_high = swap(to_x[:half], "x"), swap(to_y[half:], "y")
    x_high = swap(to_x[half:] + from_y, "x")
    y_low = swap(to_y[:half] + from_x, "y")
    by_x = jnp.concatenate([x_low, x_high], 0).astype(F32)
    by_y = jnp.concatenate([y_low, y_high], 0).astype(F32)
    return here.astype(F32) + by_x + by_y, from_x


def place_ref():
    x, y, c = (lax.axis_index(name) for name in "xyc")
    return jnp.stack([x * 2 + y, c]).astype(jnp.int32)


def core_order(place, own, other):
    first = place[1] == 0
    return jnp.concatenate([jnp.where(first, own, other), jnp.where(first, other, own)], axis=0)


def core_split(place, values):
    half = values.shape[0] // 2
    first = place[1] == 0
    low, high = values[:half], values[half:]
    return jnp.where(first, low, high), jnp.where(first, high, low)


def near_spec(rows, cols):
    return pl.BlockSpec((rows, cols), lambda i, place: (i ^ place[0], 0))


def here_spec(rows, cols):
    return pl.BlockSpec((rows, cols), lambda i, place: (i, 0))


def settle_kernel(place, own_ref, other_ref, *out_refs):
    values = core_order(place, own_ref[...], other_ref[...])
    start = 0
    for out_ref in out_refs:
        out_ref[...] = values[:, start : start + out_ref.shape[1]]
        start += out_ref.shape[1]


def settle(own, other, rows, cuts):
    cols = own.shape[1]
    return call(
        settle_kernel,
        tuple(shape((8 * rows, n), own.dtype) for n in cuts),
        (4,),
        [near_spec(rows, cols)] * 2,
        tuple(here_spec(2 * rows, n) for n in cuts),
        prefetch=1,
    )(place_ref(), own, other)


def unsettle_kernel(place, *refs):
    values = jnp.concatenate([ref[...].astype(BF16) for ref in refs[:-2]], axis=1)
    refs[-2][...], refs[-1][...] = core_split(place, values)


def unsettle(parts, rows):
    cols = sum(a.shape[1] for a in parts)
    return call(
        unsettle_kernel,
        (shape((4 * rows, cols), BF16),) * 2,
        (4,),
        [near_spec(2 * rows, a.shape[1]) for a in parts],
        (here_spec(rows, cols),) * 2,
        prefetch=1,
    )(place_ref(), *parts)


def settle_groups_kernel(place, own_ref, other_ref, main_ref, misc_ref):
    groups, rows = own_ref.shape[1], own_ref.shape[2]
    first = place[1] == 0
    main = main_ref.shape[-1]
    for far in range(groups):
        own, other = own_ref[0, far], other_ref[0, far]
        at = lax.rem(place[2] - far + groups, groups)
        for core in range(2):
            values = jnp.where(first, own, other) if core == 0 else jnp.where(first, other, own)
            main_ref[pl.ds(at, 1), core] = values[None, :, :main]
            misc_ref[pl.ds(at, 1), core] = values[None, :, main:]


def settle_groups(own, other, main):
    _, groups, rows, cols = own.shape
    spec = pl.BlockSpec((1, groups, rows, cols), lambda i, place: (i ^ place[0], 0, 0, 0))
    outs = call(
        settle_groups_kernel,
        tuple(shape((groups, 8, rows, n), own.dtype) for n in (main, cols - main)),
        (4,),
        [spec, spec],
        tuple(
            pl.BlockSpec((groups, 2, rows, n), lambda i, place: (0, i, 0, 0))
            for n in (main, cols - main)
        ),
        prefetch=1,
    )(jnp.concatenate([place_ref(), lax.axis_index("z")[None]]), own, other)
    return tuple(out.reshape(groups * 8 * rows, -1) for out in outs)


def project_kernel(
    place, own_ref, other_ref, gain_ref, one_ref, two_ref, step_ref, cos_ref, sin_ref,
    normed_ref, q_ref, x_ref, kv_ref, bc_ref, dt_ref,
):
    rows = own_ref.shape[0] // 2
    flip = (place[0] & 1) == 1
    pieces = []
    own_low, own_high = own_ref[:rows], own_ref[rows:]
    other_low, other_high = other_ref[:rows], other_ref[rows:]
    pieces.append(
        core_order(
            place, jnp.where(flip, own_high, own_low), jnp.where(flip, other_high, other_low)
        )
    )
    pieces.append(
        core_order(
            place, jnp.where(flip, own_low, own_high), jnp.where(flip, other_low, other_high)
        )
    )
    values = jnp.concatenate(pieces, axis=0).astype(F32)
    scale = lax.rsqrt(jnp.mean(values * values, axis=1, keepdims=True) + EPS)
    normed = (values * scale * gain_ref[...]).astype(BF16)
    normed_ref[...] = normed
    cosine, sine = cos_ref[...], sin_ref[...]

    def turned(v):
        return (v * cosine + pltpu.roll(v, HD // 2, 1) * sine).astype(BF16)

    one = mm(normed, one_ref[...], 1, 0)
    q_ref[...] = turned(one[:, :HD])
    x_ref[...] = one[:, HD:].astype(BF16)
    at = pl.multiple_of(place[2] * HD, HD)
    lead = KVH * HD
    kv_w = jnp.concatenate([two_ref[:, pl.ds(at, HD)], two_ref[:, pl.ds(lead + at, HD)]], axis=1)
    kv = mm(normed, kv_w, 1, 0)
    kv_ref[:, :HD] = turned(kv[:, :HD])
    kv_ref[:, HD:] = kv[:, HD:].astype(BF16)
    bc_ref[...] = mm(normed, two_ref[:, 2 * lead :], 1, 0).astype(BF16)
    dt_ref[...] = mm(normed, step_ref[...], 1, 0).astype(BF16)


def project(kv_head, own, other, gain, w_one, w_two, w_dt, tables, rows):
    total = 8 * rows
    width = own.shape[1]
    cut = total // 2
    widths = (width, HD, w_one.shape[1] - HD, 2 * HD, w_two.shape[1] - 2 * KVH * HD, 128)
    near = pl.BlockSpec((2 * rows, width), lambda i, place: (i ^ (place[0] // 2), 0))

    def fixed(a):
        return pl.BlockSpec(a.shape, lambda i, place: (0, 0))

    return call(
        project_kernel,
        tuple(shape((total, n), BF16) for n in widths),
        (2,),
        [near, near, fixed(gain), fixed(w_one), fixed(w_two), fixed(w_dt)]
        + [here_spec(cut, HD)] * 2,
        tuple(here_spec(cut, n) for n in widths),
        prefetch=1,
    )(
        jnp.concatenate([place_ref(), kv_head[None].astype(jnp.int32)]),
        own, other, gain, w_one, w_two, w_dt, *tables,
    )


def grad_early_kernel(normed_ref, q_ref, z_ref, w_ref, out_ref, gain_ref):
    grad = jnp.concatenate([q_ref[...], z_ref[...]], axis=1)
    grad = mm(normed_ref[...], grad, 0, 0)
    out_ref[...] = grad.astype(BF16)
    q_cols, z_cols = q_ref.shape[1], z_ref.shape[1]
    w = jnp.concatenate([w_ref[:, :q_cols], w_ref[:, w_ref.shape[1] - z_cols :]], axis=1)
    gain = jnp.sum(grad * w.astype(F32), axis=1, keepdims=True)
    gain_ref[...] = jnp.broadcast_to(gain, gain_ref.shape)


def grad_early(groups, normed, q, z, w_all):
    total, width = normed.shape
    rows = width // groups

    def fixed(a):
        return pl.BlockSpec(a.shape, lambda i: (0, 0))

    def flow(cols):
        return pl.BlockSpec((rows, cols), lambda i: (i, 0))

    cols = q.shape[1] + z.shape[1]
    return call(
        grad_early_kernel,
        (shape((width, cols), BF16), shape((width, 128))),
        (groups,),
        [pl.BlockSpec((total, rows), lambda i: (0, i)), fixed(q), fixed(z), flow(w_all.shape[1])],
        (flow(cols), flow(128)),
    )(normed, q, z, w_all)


def grad_late_kernel(
    place, normed_ref, x_ref, kv_ref, bc_ref, dt_ref, w_ref, gain_ref, gain_two_ref,
    x_out_ref, own_ref, other_ref,
):
    rows = own_ref.shape[2]
    head = place[2]
    first = place[1] == 0
    normed = normed_ref[...]
    x_cols, bc_cols = x_ref.shape[1], bc_ref.shape[1]
    lead = 2 * KVH * HD
    start = w_ref.shape[1] - x_cols - 128 - bc_cols - lead
    grad_x = mm(normed, x_ref[...], 0, 0)
    x_out_ref[...] = grad_x.astype(BF16)
    gain = jnp.sum(grad_x * w_ref[:, start - x_cols : start].astype(F32), axis=1, keepdims=True)
    kv = mm(normed, kv_ref[...], 0, 0)
    zero = jnp.zeros((kv.shape[0], HD), F32)
    parts = []
    for part in (kv[:, :HD], kv[:, HD:]):
        parts += [jnp.where(head == i, part, zero) for i in range(KVH)]
    two = jnp.concatenate(parts + [mm(normed, bc_ref[...], 0, 0)], axis=1)
    wide = lead + bc_cols
    gain = gain + jnp.sum(two * w_ref[:, start : start + wide].astype(F32), axis=1, keepdims=True)
    dt = mm(normed, dt_ref[...], 0, 0) * w_ref[:, start + wide : start + wide + 128].astype(F32)
    gain = gain + jnp.sum(dt, axis=1, keepdims=True) + gain_ref[:, 0:1]
    lane = lax.broadcasted_iota(jnp.int32, (gain.shape[0], 128), 1)
    gains = jnp.where(lane == 0, gain, jnp.where(lane == 1, gain_two_ref[...], 0.0))
    grad = jnp.concatenate([two.astype(BF16), gains.astype(BF16)], axis=1)
    for spot in range(4):
        low = grad[2 * spot * rows : (2 * spot + 1) * rows]
        high = grad[(2 * spot + 1) * rows : (2 * spot + 2) * rows]
        at = pl.ds(spot ^ place[0], 1)
        own_ref[at, 0] = jnp.where(first, low, high)[None]
        other_ref[at, 0] = jnp.where(first, high, low)[None]


def grad_late(kv_head, groups, normed, x, kv, bc, dt, w_all, gain, gain_two):
    total, width = normed.shape
    block = width // groups
    rows = block // 8
    cols = 2 * KVH * HD + bc.shape[1] + 128

    def fixed(a):
        return pl.BlockSpec(a.shape, lambda i, place: (0, 0))

    def flow(n):
        return pl.BlockSpec((block, n), lambda i, place: (i, 0))

    return call(
        grad_late_kernel,
        (shape((width, x.shape[1]), BF16),) + (shape((4, groups, rows, cols), BF16),) * 2,
        (groups,),
        [pl.BlockSpec((total, block), lambda i, place: (0, i))]
        + [fixed(a) for a in (x, kv, bc, dt)]
        + [flow(w_all.shape[1]), flow(128), flow(1)],
        (flow(x.shape[1]),)
        + (pl.BlockSpec((4, 1, rows, cols), lambda i, place: (0, i, 0, 0)),) * 2,
        prefetch=1,
    )(
        jnp.concatenate([place_ref(), kv_head[None].astype(jnp.int32)]),
        normed, x, kv, bc, dt, w_all, gain, gain_two,
    )


def assemble_kernel(place, q_ref, x_ref, kv_ref, bc_ref, dt_ref, z_ref, own_ref, other_ref):
    head = place[2]
    zero = jnp.zeros((kv_ref.shape[0], HD), BF16)
    parts = []
    for part in (kv_ref[:, :HD], kv_ref[:, HD:]):
        parts += [jnp.where(head == i, part, zero) for i in range(KVH)]
    wide = jnp.concatenate(
        [q_ref[...], x_ref[...]] + parts + [bc_ref[...], dt_ref[...], z_ref[...]], axis=1
    )
    own_ref[...], other_ref[...] = core_split(place, wide)


def assemble(kv_head, rows, *parts):
    total = parts[0].shape[0]
    wide = sum(a.shape[1] for a in parts) + 2 * (KVH - 1) * HD
    return call(
        assemble_kernel,
        (shape((total // 2, wide), BF16),) * 2,
        (4,),
        [near_spec(2 * rows, a.shape[1]) for a in parts],
        (here_spec(rows, wide),) * 2,
        prefetch=1,
    )(jnp.concatenate([place_ref(), kv_head[None].astype(jnp.int32)]), *parts)


def halves(pack):
    x = lax.axis_index("x")
    own = lax.dynamic_index_in_dim(pack, x, 0, False)
    return own, lax.dynamic_index_in_dim(pack, x ^ 1, 0, False)


@scoped
def weight_gather(own, got):
    x = lax.axis_index("x")
    both = jnp.concatenate([jnp.where(x == 0, own, got), jnp.where(x == 0, got, own)], axis=0)
    return lax.all_gather(both, "z", axis=0, tiled=True)


def halves_in_order(own, got, axis):
    x = lax.axis_index("x")
    return jnp.concatenate([jnp.where(x == 0, own, got), jnp.where(x == 0, got, own)], axis=axis)


def both_halves(own, got):
    return halves_in_order(own, got, 1)


@scoped
def line_scatter(grad):
    return lax.psum_scatter(grad, "z", scatter_dimension=0, tiled=True)


@scoped
def own_and_got(part):
    x = lax.axis_index("x")
    part = part.reshape(2, -1, part.shape[1])
    got = swap(lax.dynamic_index_in_dim(part, x ^ 1, 0, False), "x")
    return lax.dynamic_index_in_dim(part, x, 0, False).astype(F32), got.astype(F32)


def lanes_of(cols, heads):
    rows = cols.shape[0]
    low = lax.broadcasted_iota(jnp.int32, (rows, 2 * MP), 1) < MP
    return jnp.concatenate(
        [
            jnp.where(low, cols[:, 2 * j : 2 * j + 1], cols[:, 2 * j + 1 : 2 * j + 2])
            for j in range(heads // 2)
        ],
        axis=1,
    )


def head_sums(values):
    wide = values.shape[1]
    lane = lax.broadcasted_iota(jnp.int32, (wide, 128), 0) // MP
    pick = (lane == lax.broadcasted_iota(jnp.int32, (wide, 128), 1)).astype(F32)
    return mm(values, pick, 1, 0, EXACT)


def softplus(v):
    return jnp.maximum(v, 0.0) + jnp.log1p(jnp.exp(-jnp.abs(v)))


def sigmoid(v):
    return 1.0 / (1.0 + jnp.exp(-v))


def chunk_common(bc_ref, dt_in_ref, dt_row_ref, par_ref, par_col_ref, seg_col_ref, seg_row_ref, wide):
    heads = wide // MP
    states = bc_ref.shape[1] // 2
    b_val = bc_ref[:, :states]
    c_val = bc_ref[:, states:]
    raw = dt_in_ref[...].astype(F32) + par_ref[0:1, :]
    dt = softplus(raw)
    rate = par_ref[1:2, :]
    raw_row = dt_row_ref[...].astype(F32) + par_col_ref[:, 0:1]
    e_row = -softplus(raw_row) * par_col_ref[:, 1:2]
    first = lax.broadcasted_iota(jnp.int32, (CHUNK, CHUNK), 0)
    second = lax.broadcasted_iota(jnp.int32, (CHUNK, CHUNK), 1)
    lower = (first >= second).astype(F32)
    run = mm(lower, -dt * rate, 1, 0, EXACT)
    run_row = mm(e_row, lower, 1, 1, EXACT)
    bias = jnp.where((first >= second) & (seg_col_ref[...] == seg_row_ref[0]), 0.0, NEGATIVE)
    return heads, b_val, c_val, raw, dt, rate, run, run_row, bias, lower


def mamba_local_kernel(
    x_in_ref, bc_in_ref, dt_in_ref, dt_row_ref, par_ref, par_col_ref, skip_ref, seg_col_ref, seg_row_ref, marks_ref,
    y_ref, run_ref, held_ref, total_ref, starts_ref, state, base_run,
):
    step = pl.program_id(0)
    wide = skip_ref.shape[1]
    heads, b_val, c_val, raw, dt, rate, run, run_row, bias, _ = chunk_common(
        bc_in_ref, dt_in_ref, dt_row_ref, par_ref, par_col_ref, seg_col_ref, seg_row_ref, wide
    )

    @pl.when(step == 0)
    def _():
        state[...] = jnp.zeros_like(state)
        base_run[...] = jnp.zeros_like(base_run)

    x_val = x_in_ref[...].astype(F32)
    seg = seg_col_ref[...]
    label = marks_ref[step]
    final = marks_ref[step + 1]
    held = state[...]
    starts_ref[0] = held
    x_dt = x_val * lanes_of(dt, heads)
    x_dt_b = x_dt.astype(BF16)
    entry = jnp.where(seg == label, jnp.exp(run), 0.0)
    last = run[CHUNK - 1 : CHUNK, :]
    tail = jnp.where(seg == final, jnp.exp(last - run), 0.0)
    y_val = skip_ref[...] * x_val
    y_val = y_val + lanes_of(entry, heads) * mm(c_val, held.astype(BF16), 1, 0)
    gram = mm(c_val, b_val, 1, 1)
    low = lax.broadcasted_iota(jnp.int32, (CHUNK, 2 * MP), 1) < MP
    parts = []
    for pair in range(heads // 2):
        both = x_dt_b[:, pair * 2 * MP : (pair + 1) * 2 * MP]
        outs = []
        for h in (2 * pair, 2 * pair + 1):
            decay = jnp.exp(run[:, h : h + 1] - run_row[h : h + 1, :] + bias)
            outs.append(mm((decay * gram).astype(BF16), both, 1, 0))
        parts.append(jnp.where(low, outs[0], outs[1]))
    y_ref[...] = y_val + jnp.concatenate(parts, axis=1)
    fresh = mm(b_val, (x_dt * lanes_of(tail, heads)).astype(BF16), 0, 0)
    kept = jnp.where(label == final, jnp.exp(last), 0.0)
    new = lanes_of(jnp.broadcast_to(kept, (8, 128)), heads)[0:1] * held + fresh
    state[...] = new
    held_ref[...] = new
    run_all = run + base_run[0:1, :]
    run_ref[...] = run_all
    base_run[...] = jnp.broadcast_to(run_all[CHUNK - 1 : CHUNK, :], base_run.shape)
    total_ref[...] = jnp.exp(base_run[...])


def mamba_close_kernel(bc_in_ref, gate_ref, y_ref, run_ref, seg_col_ref, held_ref, marks_ref, out_ref, full_ref):
    wide = y_ref.shape[1]
    heads = wide // MP
    states = held_ref.shape[0]
    c_val = bc_in_ref[:, states:]
    entry = jnp.where(seg_col_ref[...] == marks_ref[0], jnp.exp(run_ref[...]), 0.0)
    y_val = y_ref[...] + lanes_of(entry, heads) * mm(c_val, held_ref[...].astype(BF16), 1, 0)
    full_ref[...] = y_val
    z_val = gate_ref[...].astype(F32)
    out_ref[...] = (y_val * z_val * sigmoid(z_val)).astype(BF16)


def mamba_grad_state_kernel(
    bc_in_ref, gate_ref, y_ref, grad_ref, run_ref, seg_col_ref, marks_ref, out_ref, gate_grad_ref
):
    wide = grad_ref.shape[1]
    heads = wide // MP
    states = out_ref.shape[0]
    c_val = bc_in_ref[:, states:]
    z_val = gate_ref[...].astype(F32)
    entry = jnp.where(seg_col_ref[...] == marks_ref[0], jnp.exp(run_ref[...]), 0.0)
    grad = grad_ref[...].astype(F32)
    sig = sigmoid(z_val)
    grad_y = grad * z_val * sig
    gate_grad_ref[...] = (grad * y_ref[...] * (sig * (1.0 + z_val * (1.0 - sig)))).astype(BF16)

    @pl.when(pl.program_id(0) == 0)
    def _():
        out_ref[...] = jnp.zeros_like(out_ref)

    out_ref[...] += mm(c_val, (grad_y * lanes_of(entry, heads)).astype(BF16), 0, 0)


def mamba_grad_near_kernel(
    x_in_ref, bc_in_ref, dt_in_ref, dt_row_ref, par_ref, par_col_ref, skip_ref, seg_col_ref, seg_row_ref, marks_ref,
    gate_ref, run_ref, starts_ref, held_ref, grad_ref,
    x_grad_ref, b_ref, c_ref, e_ref, carry_ref, skip_sum_ref,
):
    step = pl.program_id(0)
    wide = skip_ref.shape[1]
    heads, b_val, c_val, raw, dt, rate, run, run_row, bias, lower = chunk_common(
        bc_in_ref, dt_in_ref, dt_row_ref, par_ref, par_col_ref, seg_col_ref, seg_row_ref, wide
    )

    @pl.when(step == 0)
    def _():
        skip_sum_ref[...] = jnp.zeros_like(skip_sum_ref)

    z_val = gate_ref[...].astype(F32)
    x_val = x_in_ref[...].astype(F32)
    label = marks_ref[step]
    before = run_ref[0:1, :] - run[0:1, :]
    carry = jnp.where(label == marks_ref[0], jnp.exp(before), 0.0)
    held = starts_ref[0] + lanes_of(jnp.broadcast_to(carry, (8, 128)), heads)[0:1] * held_ref[...]
    held_b = held.astype(BF16)
    grad_y = grad_ref[...].astype(F32) * z_val * sigmoid(z_val)
    dt_wide = lanes_of(dt, heads)
    x_dt_b = (x_val * dt_wide).astype(BF16)
    entry = lanes_of(jnp.where(seg_col_ref[...] == label, jnp.exp(run), 0.0), heads)
    grad_in = (entry * grad_y).astype(BF16)
    run_grad = head_sums(grad_y * entry * mm(c_val, held_b, 1, 0))
    grad_c = mm(grad_in, held_b, 1, 1)
    carry_ref[0] = mm(c_val, grad_in, 0, 0)
    gram = mm(c_val, b_val, 1, 1)
    low = lax.broadcasted_iota(jnp.int32, (CHUNK, 2 * MP), 1) < MP
    lane = lax.broadcasted_iota(jnp.int32, (CHUNK, 128), 1)
    grad_y_b = grad_y.astype(BF16)
    none = jnp.zeros((CHUNK, 2 * MP), BF16)
    gram_grad = None
    parts, cols = [], []
    for pair in range(heads // 2):
        span = slice(pair * 2 * MP, (pair + 1) * 2 * MP)
        outs = []
        for h in (2 * pair, 2 * pair + 1):
            mask = low if h % 2 == 0 else ~low
            decay = jnp.exp(run[:, h : h + 1] - run_row[h : h + 1, :] + bias)
            mixing = (decay * gram).astype(BF16)
            outs.append(mm(mixing, grad_y_b[:, span], 0, 0))
            mixing_grad = mm(jnp.where(mask, grad_y_b[:, span], none), x_dt_b[:, span], 1, 1)
            weighted = mixing_grad * decay
            gram_grad = weighted if gram_grad is None else gram_grad + weighted
            weighted = weighted * gram
            run_grad = run_grad + jnp.where(
                lane == h, jnp.sum(weighted, axis=1, keepdims=True), 0.0
            )
            cols.append(jnp.sum(weighted, axis=0, keepdims=True))
        parts.append(jnp.where(low, outs[0], outs[1]))
    gram_grad_b = gram_grad.astype(BF16)
    c_ref[...] = (grad_c + mm(gram_grad_b, b_val, 1, 0)).astype(BF16)
    b_ref[...] = mm(gram_grad_b, c_val, 0, 0)
    x_grad_ref[...] = jnp.concatenate(parts, axis=1)
    col_grad = jnp.concatenate(cols + [jnp.zeros((128 - heads, CHUNK), F32)], axis=0)
    e_ref[...] = mm(lower, run_grad, 0, 0, EXACT) - mm(lower, col_grad, 0, 1, EXACT)
    skip_sum_ref[0:1, :] += jnp.sum(grad_y * x_val, axis=0, keepdims=True)


def mamba_grad_kernel(
    x_in_ref, bc_in_ref, dt_in_ref, dt_row_ref, par_ref, par_col_ref, skip_ref, seg_col_ref, seg_row_ref, marks_ref,
    gate_ref, run_ref, starts_ref, held_ref, grad_ref,
    x_grad_ref, b_grad_ref, c_grad_ref, e_grad_ref, carry_ref, deep_ref,
    x_ref, bc_ref, dt_ref, sums_ref, deep,
):
    step = pl.num_programs(0) - 1 - pl.program_id(0)
    wide = skip_ref.shape[1]
    heads = wide // MP
    states = b_grad_ref.shape[1]
    b_val = bc_in_ref[:, :states]
    raw = dt_in_ref[...].astype(F32) + par_ref[0:1, :]
    dt = softplus(raw)
    rate = par_ref[1:2, :]
    first = lax.broadcasted_iota(jnp.int32, (CHUNK, CHUNK), 0)
    second = lax.broadcasted_iota(jnp.int32, (CHUNK, CHUNK), 1)
    lower = (first >= second).astype(F32)
    run = run_ref[...]

    @pl.when(pl.program_id(0) == 0)
    def _():
        deep[...] = deep_ref[...]
        sums_ref[...] = jnp.zeros_like(sums_ref)

    z_val = gate_ref[...].astype(F32)
    x_val = x_in_ref[...].astype(F32)
    seg = seg_col_ref[...]
    label = marks_ref[step]
    final = marks_ref[step + 1]
    last = run[CHUNK - 1 : CHUNK, :]
    e_first = -dt[0:1, :] * rate
    before = run[0:1, :] - e_first
    carry = jnp.where(label == marks_ref[0], jnp.exp(before), 0.0)
    held = starts_ref[0] + lanes_of(jnp.broadcast_to(carry, (8, 128)), heads)[0:1] * held_ref[...]
    after_b = deep[...].astype(BF16)
    grad_y = grad_ref[...].astype(F32) * z_val * sigmoid(z_val)
    dt_wide = lanes_of(dt, heads)
    tail = lanes_of(jnp.where(seg == final, jnp.exp(last - run), 0.0), heads)
    x_tail = x_val * dt_wide * tail
    back = mm(b_val, after_b, 1, 0)
    bc_ref[:, :states] = (b_grad_ref[...] + mm(x_tail.astype(BF16), after_b, 1, 1)).astype(BF16)
    bc_ref[:, states:] = c_grad_ref[...]
    tail_grad = head_sums(x_tail * back)
    kept = jnp.where(label == final, jnp.exp(last - before), 0.0)
    kept_wide = lanes_of(jnp.broadcast_to(kept, (8, 128)), heads)[0:1]
    kept_grad = head_sums(
        jnp.broadcast_to(kept_wide * jnp.sum(deep[...] * held, axis=0, keepdims=True), (8, wide))
    )
    last_grad = jnp.sum(tail_grad, axis=0, keepdims=True) + kept_grad[0:1]
    deep[...] = kept_wide * deep[...] + carry_ref[0]
    x_dt_grad = x_grad_ref[...] + tail * back
    x_ref[...] = (x_dt_grad * dt_wide + skip_ref[...] * grad_y).astype(BF16)
    e_grad = e_grad_ref[...] - mm(lower, tail_grad, 0, 0, EXACT) + last_grad
    dt_grad = head_sums(x_dt_grad * x_val) - rate * e_grad
    raw_grad = dt_grad * sigmoid(raw)
    lane = lax.broadcasted_iota(jnp.int32, (CHUNK, 128), 1)
    dt_ref[...] = jnp.where(lane < heads, raw_grad, 0.0).astype(BF16)
    sums_ref[0:1, :] += jnp.sum(-rate * dt * e_grad, axis=0, keepdims=True)
    sums_ref[1:2, :] += jnp.sum(raw_grad, axis=0, keepdims=True)


def seen(kseg_ref, qseg, first_query, block):
    rows = qseg.shape[0]
    key_pos = block * KEYS + lax.broadcasted_iota(jnp.int32, (rows, KEYS), 1)
    query_pos = first_query + lax.broadcasted_iota(jnp.int32, (rows, KEYS), 0)
    return (key_pos <= query_pos) & (kseg_ref[pl.ds(block, 1), :] == qseg)


def key_span(block, where_ref, groups):
    far = where_ref[0] - block // 2
    at = jnp.where((block & 1) == where_ref[1], far, groups + far)
    return pl.ds(pl.multiple_of(at * KEYS, KEYS), KEYS)


def attend_kernel(low_ref, high_ref, start_ref, where_ref, q_ref, kv_ref, kseg_ref, qseg_ref, att_ref, log_ref):
    step = pl.program_id(0)
    rows = q_ref.shape[0]
    query = q_ref[...]
    qseg = qseg_ref[...]
    first_query = start_ref[0] + step * rows
    scale = HD**-0.5

    def visit(block, state):
        peak, total, acc = state
        span = key_span(block, where_ref, kv_ref.shape[0] // (2 * KEYS))
        scores = mm(query, kv_ref[span, :HD], 1, 1) * scale
        scores = jnp.where(seen(kseg_ref, qseg, first_query, block), scores, NEGATIVE)
        new_peak = jnp.maximum(peak, jnp.max(scores, axis=1, keepdims=True))
        weights = jnp.exp(scores - new_peak)
        rescale = jnp.exp(peak - new_peak)
        total = total * rescale + jnp.sum(weights, axis=1, keepdims=True)
        acc = acc * rescale + mm(weights.astype(BF16), kv_ref[span, HD:], 1, 0)
        return new_peak, total, acc

    peak, total, acc = lax.fori_loop(
        low_ref[step],
        high_ref[step],
        visit,
        (
            jnp.full((rows, 1), NEGATIVE, F32),
            jnp.zeros((rows, 1), F32),
            jnp.zeros((rows, HD), F32),
        ),
    )
    att_ref[...] = acc / total
    log_ref[...] = jnp.broadcast_to(peak + jnp.log(total), log_ref.shape)


def attend_grad_kernel(
    low_ref, high_ref, start_ref, where_ref, q_ref, kv_ref, kseg_ref, qseg_ref, att_ref, log_ref,
    grad_ref, dq_ref, dkv_ref, sums,
):
    step = pl.program_id(0)
    rows = q_ref.shape[0]
    query = q_ref[...]
    grad = grad_ref[...]
    qseg = qseg_ref[...]
    log_total = log_ref[:, 0:1]
    first_query = start_ref[0] + step * rows
    scale = HD**-0.5
    delta = jnp.sum(grad.astype(F32) * att_ref[...], axis=1, keepdims=True)

    @pl.when(step == 0)
    def _():
        sums[...] = jnp.zeros_like(sums)

    def visit(block, acc):
        span = key_span(block, where_ref, kv_ref.shape[0] // (2 * KEYS))
        keys = kv_ref[span, :HD]
        scores = mm(query, keys, 1, 1) * scale - log_total
        scores = jnp.where(seen(kseg_ref, qseg, first_query, block), scores, NEGATIVE)
        probs = jnp.exp(scores)
        probs_grad = mm(grad, kv_ref[span, HD:], 1, 1)
        scores_grad = (probs * (probs_grad - delta)).astype(BF16)
        sums[span, :HD] += mm(scores_grad, query, 0, 0)
        sums[span, HD:] += mm(probs.astype(BF16), grad, 0, 0)
        return acc + mm(scores_grad, keys, 1, 0)

    acc = lax.fori_loop(low_ref[step], high_ref[step], visit, jnp.zeros((rows, HD), F32))
    dq_ref[...] = acc * scale

    @pl.when(step == pl.num_programs(0) - 1)
    def _():
        dkv_ref[:, :HD] = (sums[:, :HD] * scale).astype(BF16)
        dkv_ref[:, HD:] = sums[:, HD:].astype(BF16)


def call(kernel, out_shape, grid, in_specs, out_specs, scratch=(), prefetch=0, cost=None):
    return pl.pallas_call(
        kernel,
        out_shape=out_shape,
        grid_spec=pltpu.PrefetchScalarGridSpec(
            num_scalar_prefetch=prefetch,
            grid=grid,
            in_specs=in_specs,
            out_specs=out_specs,
            scratch_shapes=list(scratch),
        ),
        compiler_params=pltpu.CompilerParams(
            vmem_limit_bytes=VMEM_BYTES, dimension_semantics=("arbitrary",) * len(grid)
        ),
        cost_estimate=cost,
        name=kernel.__name__,
    )


def shape(dims, dtype=F32):
    return jax.ShapeDtypeStruct(dims, dtype)


def rope_tables(positions):
    half = HD // 2
    frequency = jnp.exp(jnp.arange(half, dtype=F32) * (-2.0 * math.log(THETA) / HD))
    angle = positions.astype(F32)[:, None] * frequency[None, :]
    cosine, sine = jnp.cos(angle), jnp.sin(angle)
    return jnp.concatenate([cosine, cosine], 1), jnp.concatenate([-sine, sine], 1)


def rope(values, tables):
    cosine, sine = tables
    return values * cosine + jnp.concatenate([values[:, HD // 2 :], values[:, : HD // 2]], 1) * sine


def rope_back(values, tables):
    cosine, sine = tables
    return values * cosine - jnp.concatenate([values[:, HD // 2 :], values[:, : HD // 2]], 1) * sine


def unit(values):
    return values * lax.rsqrt(jnp.mean(values * values, axis=-1, keepdims=True) + EPS)


def norm_back(values, gain, grad):
    scale = lax.rsqrt(jnp.mean(values * values, axis=-1, keepdims=True) + EPS)
    u = values * scale
    inner = jnp.mean(grad * gain * u, axis=-1, keepdims=True)
    return scale * (grad * gain - u * inner), jnp.sum(grad * u, axis=0)


def shards(
    tokens, seg_ids, cotangent, gain_mix, q_w, kv_w, zx_w, dt_w, bc_w,
    a_log, dt_bias, skip, wo_w, wm_w, gain_ff, gu_w, down_w,
):
    groups = lax.axis_size("z")
    z, x, y, c = (lax.axis_index(name) for name in "zxyc")
    own_rows, width = tokens.shape
    group = 8 * own_rows
    rows_w = q_w.shape[0]
    part = kv_w.shape[0]
    ratio = rows_w // part
    heads = dt_w.shape[1] // 2
    wide = heads * MP
    states = bc_w.shape[1] // 2
    ff = gu_w.shape[2] // 2
    inner = q_w.shape[1] // 2
    steps = group // CHUNK

    zx_cut = zx_w.reshape(rows_w, 2, 2, wide).transpose(1, 2, 0, 3)
    pack_z = zx_cut[0]
    pack_one = jnp.concatenate([q_w.reshape(rows_w, 2, inner).transpose(1, 0, 2), zx_cut[1]], axis=2)
    pack_out = jnp.concatenate(
        [
            wo_w.reshape(rows_w, 2, inner).transpose(1, 0, 2),
            wm_w.reshape(rows_w, 2, wide).transpose(1, 0, 2),
        ],
        axis=2,
    )
    pack_gu = gu_w.reshape(rows_w, 2, 2, ff).transpose(2, 0, 1, 3).reshape(2, rows_w, 2 * ff)
    pack_down = down_w.reshape(rows_w, 2, ff).transpose(1, 0, 2)
    kv_cols = kv_w.shape[1] * kv_w.shape[2]
    bc_cols = bc_w.shape[1]
    lead = kv_cols + bc_cols
    dt_cols = dt_w.shape[1]
    dt_part = dt_w.reshape(ratio, part, dt_cols).transpose(1, 0, 2).reshape(part, ratio * dt_cols)
    pack_two = jnp.concatenate(
        [kv_w.reshape(part, kv_cols), bc_w, gain_mix[:, None], gain_ff[:, None], dt_part], axis=1
    )
    used = pack_two.shape[1]
    total_cols = -(-used // 128) * 128
    pack_two = jnp.pad(pack_two, ((0, 0), (0, total_cols - used)))

    def put_two(out, at, number, value):
        return lax.dynamic_update_slice(out, value[None], (at, 0, 0))

    own_one, give_one = halves(pack_one)
    own_out, give_out = halves(jnp.concatenate([pack_out, pack_z], axis=2))
    own_ff, give_ff = halves(jnp.concatenate([pack_gu, pack_down], axis=2))
    two_far = from_ring("whole_rows", pack_two)
    seg_pair = jnp.zeros((2, seg_ids.shape[0]), jnp.int32)
    seg_pair = lax.dynamic_update_index_in_dim(seg_pair, seg_ids, x, 0)
    seg_pair = lax.dynamic_update_index_in_dim(seg_pair, swap(seg_ids, "x"), x ^ 1, 0)
    seg_own = seg_pair.reshape(1, group)
    seg_far = from_ring("ids", seg_own)
    two = jnp.stack([pack_two] + two_far)[None]
    got_one = swap(give_one, "x")
    own_one, got_one, two, *seg_far = lax.optimization_barrier((own_one, got_one, two, *seg_far))
    seg_all = jnp.zeros((groups, group), jnp.int32)
    for far, got in enumerate([seg_own, *seg_far]):
        seg_all = lax.dynamic_update_slice(seg_all, got, ((z - far + groups) % groups, 0))
    w_one = weight_gather("w_one", own_one, got_one)
    two_own, two_other, _, two_low = cube_gather("whole_rows", two, 1)
    rows_own, rows_other, *_ = cube_gather("tokens", after(tokens, two_low))
    w_two, misc = settle_groups(two_own, two_other, lead)
    w_mix = weight_gather("w_mix", own_out, swap(after(give_out, rows_own), "x"))
    w_out, w_z = w_mix[:, : inner + wide], w_mix[:, inner + wide :]
    got_ff = swap(after(give_ff, rows_own), "x")
    w_ff = weight_gather("w_ff", own_ff, got_ff)
    w_gu, w_down = w_ff[:, : 2 * ff], w_ff[:, 2 * ff :]
    segment = seg_own.astype(F32)
    seg_col = segment.reshape(group, 1)
    seg_row = segment.reshape(steps, 1, CHUNK)
    previous = lax.dynamic_index_in_dim(seg_all, jnp.maximum(z - 1, 0), 0, False)[group - 1]
    in_label = jnp.where(z > 0, previous, -1).astype(F32)
    marks = jnp.concatenate([in_label[None], segment[0, CHUNK - 1 :: CHUNK]])

    gain_one = misc[:, 0].astype(F32)
    gain_two = misc[:, 1].astype(F32)
    dt_all = misc[:, 2 : 2 + ratio * dt_cols].reshape(
        groups, 2, 4, part, ratio, 2, heads
    )
    dt_own = lax.dynamic_index_in_dim(dt_all, y * 2 + c, 2, False)
    dt_own = lax.dynamic_index_in_dim(dt_own, x, 4, False)
    w_dt = dt_own.transpose(0, 1, 3, 2, 4).reshape(width, heads)
    kv_head = ((y * 2 + c) * 2 + x) * (inner // HD) // (QH // KVH)
    w_dt = jnp.pad(w_dt, ((0, 0), (0, 128 - heads)))

    positions = z * group + jnp.arange(group, dtype=jnp.int32)
    tables = rope_tables(positions)
    normed, query, x_in, kv_own, bc_in, dt_in = project(
        kv_head, rows_own, rows_other, gain_one[None, :], w_one, w_two, w_dt, tables, own_rows
    )
    half, quarter = group // 2, group // 4
    kv_half = lax.dynamic_slice_in_dim(kv_own, c * half, half, 0)
    kv_quarter = lax.dynamic_slice_in_dim(kv_own, c * half + x * quarter, quarter, 0)
    kv_far = from_below("kv", [kv_quarter] * groups)
    x_in = after(x_in, got_ff)
    gate_in = mm(normed, w_z, 1, 0).astype(BF16)

    dt_row = jnp.pad(dt_in[:, :8].T, ((0, 8), (0, 0)))
    pad = ((0, 128 - heads),)

    def pick(values):
        return lax.dynamic_slice_in_dim(values, x * heads, heads, 0)

    rates = jnp.exp(pick(a_log))
    params = jnp.stack([jnp.pad(pick(dt_bias), pad), jnp.pad(rates, pad)])
    params = jnp.pad(params, ((0, 6), (0, 0)))
    params_col = jnp.pad(
        jnp.stack([pick(dt_bias), rates], axis=1), ((0, 16 - heads), (0, 126))
    )
    skip_wide = jnp.repeat(pick(skip), MP)[None, :]

    def flow(cols, back=False):
        at = (lambda i: (steps - 1 - i, 0)) if back else (lambda i: (i, 0))
        return pl.BlockSpec((CHUNK, cols), at)

    def chunk_specs(back=False):
        def turn(i):
            return steps - 1 - i if back else i

        return [
            flow(wide, back),
            flow(2 * states, back),
            flow(128, back),
            pl.BlockSpec((16, CHUNK), lambda i: (0, turn(i))),
            pl.BlockSpec((8, 128), lambda i: (0, 0)),
            pl.BlockSpec((16, 128), lambda i: (0, 0)),
            pl.BlockSpec((1, wide), lambda i: (0, 0)),
            flow(1, back),
            pl.BlockSpec((1, 1, CHUNK), lambda i: (turn(i), 0, 0)),
            pl.BlockSpec(memory_space=pltpu.SMEM),
        ]

    whole = pl.BlockSpec((states, wide), lambda i: (0, 0))
    smem = pl.BlockSpec(memory_space=pltpu.SMEM)
    chunk_args = (x_in, bc_in, dt_in, dt_row, params, params_col, skip_wide, seg_col, seg_row, marks)
    y_local, run, held_own, total, starts = call(
        mamba_local_kernel,
        (
            shape((group, wide)),
            shape((group, 128)),
            shape((states, wide)),
            shape((8, 128)),
            shape((steps, states, wide)),
        ),
        (steps,),
        chunk_specs(),
        (
            flow(wide),
            flow(128),
            whole,
            pl.BlockSpec((8, 128), lambda i: (0, 0)),
            pl.BlockSpec((1, states, wide), lambda i: (i, 0, 0)),
        ),
        [pltpu.VMEM((states, wide), F32), pltpu.VMEM((8, 128), F32)],
    )(*chunk_args)
    joined = jnp.where(in_label == segment[0, group - 1], 1.0, 0.0)
    factor = jnp.repeat(total[0, :heads] * joined, MP)[None, :]
    factor_rows = jnp.broadcast_to(factor, (16, wide))
    held_sent = jnp.concatenate([held_own, factor_rows], axis=0).astype(BF16)
    held_sent, *kv_far = lax.optimization_barrier((held_sent, *kv_far))
    held_far = from_below("held", [held_sent] * groups)
    kv_far = jnp.stack(kv_far)
    kv_far = halves_in_order(kv_far, swap(kv_far, "x"), 1).reshape(-1, 2 * HD)
    kv_near = jnp.concatenate([kv_half, kv_far], axis=0)
    cot_own, cot_other, *_ = cube_gather("cotangent", after(cotangent, kv_near))
    kv_all = jnp.concatenate([kv_near, swap(kv_near, "c")], axis=0)
    w_all = jnp.concatenate([w_one, w_two, w_dt, w_z], axis=1)
    query, w_all, *held_far = lax.optimization_barrier((query, w_all, *held_far))
    in_held = jnp.zeros((states, wide), F32)
    for got in reversed(held_far):
        got = got.astype(F32)
        in_held = got[:states] + got[states : states + 1] * in_held

    q_rows = CHUNK
    blocks = group // q_rows
    first_rows = z * group + q_rows * jnp.arange(blocks, dtype=jnp.int32)
    first_seg = seg_own[0, ::q_rows]
    reached = jnp.arange(groups * group, dtype=jnp.int32)[None, :] < (z + 1) * group
    earlier = (seg_all.reshape(1, -1) < first_seg[:, None]) & reached
    low = jnp.sum(earlier, axis=1, dtype=jnp.int32) // KEYS
    high = (first_rows + q_rows - 1) // KEYS + 1
    start = (z * group)[None].astype(jnp.int32)
    where = jnp.stack([z, c]).astype(jnp.int32)
    key_seg = seg_all.astype(F32).reshape(groups * group // KEYS, KEYS)

    def rows_spec(cols):
        return pl.BlockSpec((q_rows, cols), lambda i, *_: (i, 0))

    def full_spec(a):
        return pl.BlockSpec(a.shape, lambda i, *_: (0, 0))

    att_full, log_total = call(
        attend_kernel,
        (shape((group, HD)), shape((group, 128))),
        (blocks,),
        [rows_spec(HD), full_spec(kv_all), full_spec(key_seg), rows_spec(1)],
        (rows_spec(HD), rows_spec(128)),
        prefetch=4,
    )(low, high, start, where, query, kv_all, key_seg, seg_col)

    ssm_out, y_full = call(
        mamba_close_kernel,
        (shape((group, wide), BF16), shape((group, wide))),
        (steps,),
        [flow(2 * states), flow(wide), flow(wide), flow(128), flow(1), whole, smem],
        (flow(wide), flow(wide)),
    )(bc_in, gate_in, y_local, run, seg_col, after(in_held, att_full), marks)

    def row_term(a, w):
        return mm(a, w, 1, 1).astype(BF16).reshape(4, own_rows, width)

    def weight_grad(pairs):
        total = None
        for a, g in pairs:
            value = mm(a, g, 0, 0)
            total = value if total is None else total + value
        return total.astype(BF16)

    stream_own = tokens.astype(F32)
    ssm_out, cot_own, cot_other = lax.optimization_barrier((ssm_out, cot_own, cot_other))
    mixer_own, mixer_other = unsettle([att_full, ssm_out], own_rows)
    term_other = row_term(mixer_other, w_out)
    middle = stream_own + cube_scatter("mixed", row_term(mixer_own, w_out), term_other)[0]
    normed_two = (unit(middle) * gain_two).astype(BF16)
    two_rows = cube_gather("normed_two", normed_two)[:2]

    def forward(rows):
        gate_up = mm(rows, w_gu, 1, 0).astype(BF16)
        gate = gate_up[:, :ff].astype(F32)
        up = gate_up[:, ff:].astype(F32)
        sig = jax.nn.sigmoid(gate)
        return gate, up, sig, (gate * sig * up).astype(BF16)

    def backward(rows, gate, up, sig):
        grad_hidden = mm(rows, w_down, 1, 0).astype(BF16).astype(F32)
        grad_gate = grad_hidden * up * (sig * (1.0 + gate * (1.0 - sig)))
        return jnp.concatenate([grad_gate, grad_hidden * gate * sig], axis=1).astype(BF16)

    *kept_own, hidden_own = forward(two_rows[0])
    *kept_other, hidden_other = forward(two_rows[1])
    gu_other = backward(cot_other, *kept_other)
    gu_own = backward(cot_own, *kept_own)
    term_other = row_term(gu_other, w_gu)
    down_w = weight_grad(
        [(after(cot_own, term_other), hidden_own), (after(cot_other, term_other), hidden_other)]
    )
    down_part = line_scatter("down", down_w)
    term, down_w = lax.optimization_barrier((row_term(gu_own, w_gu), down_w))
    grad_normed_two, far = cube_scatter("grad_normed_two", term, term_other)
    gu_w = weight_grad([(after(two_rows[0], far), gu_own), (after(two_rows[1], far), gu_other)])
    middle_part, gain_two_part = norm_back(middle, gain_two, grad_normed_two)
    grad_middle = cotangent.astype(F32) + middle_part
    mixed_own, mixed_other, *_ = cube_gather("grad_middle", grad_middle.astype(BF16))
    mixed_own, gu_w = lax.optimization_barrier((mixed_own, gu_w))
    gu_part = line_scatter("gu", gu_w)
    grad_att, grad_ssm = settle(
        mm(mixed_own, w_out, 1, 0).astype(BF16),
        mm(mixed_other, w_out, 1, 0).astype(BF16),
        own_rows,
        (inner, wide),
    )

    state_grad, grad_z = call(
        mamba_grad_state_kernel,
        (shape((states, wide)), shape((group, wide), BF16)),
        (steps,),
        [flow(2 * states), flow(wide), flow(wide), flow(wide), flow(128), flow(1), smem],
        (whole, flow(wide)),
    )(bc_in, gate_in, y_full, grad_ssm, run, seg_col, marks)
    grad_sent = jnp.concatenate([state_grad, factor_rows], axis=0).astype(BF16)
    grad_att, grad_sent, down_part = lax.optimization_barrier((grad_att, grad_sent, down_part))
    held_far = from_above("grad_held", [grad_sent] * groups)
    grad_query, grad_kv_all = call(
        attend_grad_kernel,
        (shape((group, HD)), shape((groups * group, 2 * HD), BF16)),
        (blocks,),
        [
            rows_spec(HD), full_spec(kv_all), full_spec(key_seg), rows_spec(1),
            rows_spec(HD), rows_spec(128), rows_spec(HD),
        ],
        (rows_spec(HD), full_spec(kv_all)),
        [pltpu.VMEM((groups * group, 2 * HD), F32)],
        prefetch=4,
    )(low, high, start, where, query, kv_all, key_seg, seg_col, att_full, log_total, grad_att)
    kv_terms = grad_kv_all.reshape(2, groups, half, 2 * HD)
    kv_terms = (kv_terms[0] + swap(kv_terms[1], "c")).reshape(groups, 2, quarter, 2 * HD)
    kv_terms = lax.dynamic_index_in_dim(kv_terms, x, 1, False) + swap(
        lax.dynamic_index_in_dim(kv_terms, x ^ 1, 1, False), "x"
    )
    kv_terms, *held_far = lax.optimization_barrier((kv_terms, *held_far))
    kv_far = from_above("grad_kv", kv_terms)
    grad_q = rope_back(grad_query, tables).astype(BF16)
    chunk_more = (gate_in, run, starts, in_held, after(grad_ssm, kv_terms))

    def more_specs(back=False):
        return [
            flow(wide, back),
            flow(128, back),
            pl.BlockSpec((1, states, wide), lambda i: (steps - 1 - i if back else i, 0, 0)),
            whole,
            flow(wide, back),
        ]

    near_out = call(
        mamba_grad_near_kernel,
        (
            shape((group, wide)),
            shape((group, states)),
            shape((group, states), BF16),
            shape((group, 128)),
            shape((steps, states, wide)),
            shape((8, wide)),
        ),
        (steps,),
        chunk_specs() + more_specs(),
        (
            flow(wide),
            flow(states),
            flow(states),
            flow(128),
            pl.BlockSpec((1, states, wide), lambda i: (i, 0, 0)),
            pl.BlockSpec((8, wide), lambda i: (0, 0)),
        ),
    )(*chunk_args, *chunk_more)
    skip_sums = near_out[5]
    near, *kv_far = lax.optimization_barrier((near_out[3], *kv_far))
    qz_w, gain_early = grad_early(groups, normed, after(grad_q, near), grad_z, w_all)
    qz_part = line_scatter("qz", qz_w)
    out_w = weight_grad([(after(mixed_own, near), mixer_own), (mixed_other, mixer_other)])
    out_part = line_scatter("out", out_w)
    hidden_own, hidden_other = after(hidden_own, near), after(hidden_other, near)
    layer_other = row_term(hidden_other, w_down)
    layer_own = row_term(hidden_own, w_down)
    layer_out = middle + cube_scatter("layer_out", layer_own, layer_other)[0]
    layer_out = layer_out.astype(BF16)
    deep = jnp.zeros((states, wide), F32)
    for got in reversed(held_far):
        got = got.astype(F32)
        deep = got[:states] + got[states : states + 1] * deep
    grad_kv_part = kv_terms[0].astype(F32)
    for got in kv_far:
        grad_kv_part = grad_kv_part + got.astype(F32)
    down_own, down_got = own_and_got("down", down_part)
    deep = after(deep, grad_kv_part, down_got, layer_out)
    part_tables = tuple(
        lax.dynamic_slice_in_dim(table, c * half + x * quarter, quarter, 0) for table in tables
    )
    grad_kv_part = jnp.concatenate(
        [rope_back(grad_kv_part[:, :HD], part_tables), grad_kv_part[:, HD:]], axis=1
    ).astype(BF16)
    grad_kv = lax.dynamic_update_slice(
        jnp.zeros((group, 2 * HD), BF16), grad_kv_part, (c * half + x * quarter, 0)
    )
    grad_x, grad_bc, grad_dt, sums = call(
        mamba_grad_kernel,
        (
            shape((group, wide), BF16),
            shape((group, 2 * states), BF16),
            shape((group, 128), BF16),
            shape((8, 128)),
        ),
        (steps,),
        chunk_specs(True)
        + more_specs(True)
        + [
            flow(wide, True),
            flow(states, True),
            flow(states, True),
            flow(128, True),
            pl.BlockSpec((1, states, wide), lambda i: (steps - 1 - i, 0, 0)),
            whole,
        ],
        (
            flow(wide, True),
            flow(2 * states, True),
            flow(128, True),
            pl.BlockSpec((8, 128), lambda i: (0, 0)),
        ),
        [pltpu.VMEM((states, wide), F32)],
    )(*chunk_args, *chunk_more, *near_out[:5], deep)

    gu_own, gu_got = own_and_got("gu", gu_part)
    grad_x, gu_got = lax.optimization_barrier((grad_x, gu_got))
    x_w, two_own, two_other = grad_late(
        kv_head, groups, normed, grad_x, grad_kv, grad_bc, grad_dt, w_all, gain_early,
        gain_two_part[:, None],
    )
    x_part = line_scatter("x", x_w)
    grad_own, grad_other = assemble(
        kv_head, own_rows, grad_q, after(grad_x, x_w), grad_kv, grad_bc, grad_dt, grad_z
    )
    in_other = row_term(grad_other, w_all)
    grad_own, out_part = lax.optimization_barrier((after(grad_own, in_other), out_part))
    in_own = row_term(grad_own, w_all)
    two_part, two_far = cube_scatter("grad_two", two_own, two_other)
    in_grad, in_far = cube_scatter("grad_in", in_own, in_other, gate=two_far)
    in_grad, qz_part = lax.optimization_barrier((in_grad, qz_part))
    qz_own, qz_got = own_and_got("qz", after(qz_part, in_grad))
    out_own, out_got = own_and_got("out", after(out_part, in_grad))
    input_part, _ = norm_back(stream_own, gain_one, in_grad)
    input_grad = grad_middle + input_part
    two_part = after(two_part.astype(BF16), in_grad)
    ahead = [lax.dynamic_index_in_dim(two_part, (z + i) % groups, 0, False) for i in range(groups)]
    back = [lax.dynamic_index_in_dim(two_part, (z - i) % groups, 0, False) for i in range(groups)]
    from_others = from_above("grad_two", back) + from_below("grad_two", ahead)
    two_part = lax.dynamic_index_in_dim(two_part, z, 0, False).astype(F32)
    for got in from_others:
        two_part = two_part + got.astype(F32)
    kv_grad = two_part[:, :kv_cols].reshape(kv_w.shape)
    bc_grad = two_part[:, kv_cols:lead]
    small = jnp.concatenate(
        [sums[0, :heads], sums[1, :heads], jnp.sum(skip_sums[0].reshape(heads, MP), axis=1)]
    )
    small = jnp.pad(small, (0, width - small.shape[0]))
    dt_w_grad = mm(after(grad_dt, in_own), normed, 0, 0)[:heads]
    tiny = jnp.concatenate([dt_w_grad, small[None]], axis=0)
    for got in from_ring("tiny", tiny):
        tiny = tiny + got
    tiny_other = swap(tiny, "x")
    dt_grad = both_halves(
        *(
            lax.dynamic_slice_in_dim(a[:heads], (z * 2 + x) * rows_w, rows_w, 1).T
            for a in (tiny, tiny_other)
        )
    )
    small_sum = both_halves(*(a[heads, : 3 * heads].reshape(3, heads) for a in (tiny, tiny_other)))
    return (
        layer_out,
        input_grad,
        two_part[:, lead] / gain_mix.astype(F32),
        both_halves(qz_own[:, :inner], qz_got[:, :inner]),
        kv_grad,
        jnp.stack(
            [both_halves(qz_own[:, inner:], qz_got[:, inner:]), both_halves(*own_and_got("x", x_part))],
            axis=1,
        ),
        dt_grad,
        bc_grad,
        small_sum[0],
        small_sum[1],
        small_sum[2],
        both_halves(out_own[:, :inner], out_got[:, :inner]),
        both_halves(out_own[:, inner:], out_got[:, inner:]),
        two_part[:, lead + 1],
        jnp.stack(
            [both_halves(gu_own[:, :ff], gu_got[:, :ff]), both_halves(gu_own[:, ff:], gu_got[:, ff:])],
            axis=1,
        ),
        both_halves(down_own, down_got),
    )


def solution(mesh):
    groups = mesh.shape["blk"] // 2
    fine = Mesh(mesh.devices.reshape(groups, 2, 2, mesh.shape["head"] // 2), ("z", "x", "y", "c"))
    blk, head = ("z", "x"), ("y", "c")
    every = blk + head
    rows = P(every, None)
    return jax.shard_map(
        shards,
        mesh=fine,
        in_specs=(
            rows,
            P(blk),
            rows,
            P(every),
            P(blk, head),
            P(every, None, None),
            P(blk, None, head),
            P(blk, head),
            rows,
            P(head),
            P(head),
            P(head),
            P(blk, head),
            P(blk, head),
            P(every),
            P(blk, None, head),
            P(blk, head),
        ),
        out_specs=(
            rows,
            rows,
            P(every),
            P(blk, head),
            P(every, None, None),
            P(blk, None, head),
            P(blk, head),
            rows,
            P(head),
            P(head),
            P(head),
            P(blk, head),
            P(blk, head),
            P(every),
            P(blk, None, head),
            P(blk, head),
        ),
        check_vma=False,
    )
```

```python
import functools
import math

import jax
import jax.numpy as jnp
from jax import lax
from jax.experimental import pallas as pl
from jax.experimental.pallas import tpu as pltpu
from jax.sharding import Mesh
from jax.sharding import PartitionSpec as P

QH = 8
KVH = 2
HD = 128
MP = 64
CHUNK = 256
KEYS = 512
EPS = 1e-05
THETA = 100000000000.0
NEGATIVE = -1e30
EXACT = lax.Precision.HIGHEST
F32 = jnp.float32
BF16 = jnp.bfloat16
VMEM_BYTES = 56 * 1024 * 1024
SWAP = [(0, 1), (1, 0)]


def mm(a, b, ca, cb, precision=None):
    return lax.dot_general(
        a, b, (((ca,), (cb,)), ((), ())), preferred_element_type=F32, precision=precision
    )


def scoped(function):
    def named(name, *args, **kwargs):
        with jax.named_scope(name):
            return function(*args, **kwargs)

    return named


def swap(a, axis):
    return lax.ppermute(a, axis, SWAP)


def after(value, *earlier):
    return lax.optimization_barrier((value,) + earlier)[0]


@scoped
def from_below(values):
    count = lax.axis_size("z")
    return [
        lax.ppermute(values[far], "z", [(i, i + far) for i in range(count - far)])
        for far in range(1, count)
    ]


@scoped
def from_above(values):
    count = lax.axis_size("z")
    return [
        lax.ppermute(values[far], "z", [(i + far, i) for i in range(count - far)])
        for far in range(1, count)
    ]


@scoped
def from_ring(value):
    count = lax.axis_size("z")
    return [
        lax.ppermute(value, "z", [(i, (i + far) % count) for i in range(count)])
        for far in range(1, count)
    ]


def spots(dx, dy, dc):
    x, y, c = (lax.axis_index(name) for name in "xyc")
    return ((x ^ dx) * 2 + (y ^ dy)) * 2 + (c ^ dc)


@scoped
def cube_gather(piece, split=0, gate=None, last_gate=None):
    by_x, by_y = swap(piece, "x"), swap(piece, "y")
    if gate is not None:
        by_x, by_y = after(by_x, gate), after(by_y, gate)
    low = swap(jnp.split(by_x, 2, split)[0], "y")
    high = swap(jnp.split(by_y, 2, split)[1], "x")
    if last_gate is not None:
        low, high = after(low, last_gate), after(high, last_gate)
    far = [low, high] if split == 0 else [jnp.concatenate([low, high], axis=split)]
    own = jnp.concatenate([piece, by_y, by_x] + far, axis=0)
    return own, swap(own, "c"), by_x, low


@scoped
def cube_scatter(mine, other=None, gate=None, far_gate=None):
    if other is not None:
        mine = mine + swap(other, "c")
    if gate is not None:
        mine = after(mine, gate)
    here, to_y, to_x, far = mine[0], mine[1], mine[2], mine[3]
    half = far.shape[0] // 2
    from_x, from_y = swap(far[:half], "x"), swap(far[half:], "y")
    x_low, y_high = swap(to_x[:half], "x"), swap(to_y[half:], "y")
    if far_gate is not None:
        to_x, to_y = after(to_x, far_gate), after(to_y, far_gate)
    last = to_x[half:] + from_y
    x_high = swap(last, "x")
    y_low = swap(to_y[:half] + from_x, "y")
    by_x = jnp.concatenate([x_low, x_high], 0).astype(F32)
    by_y = jnp.concatenate([y_low, y_high], 0).astype(F32)
    return here.astype(F32) + by_x + by_y, from_x, last


@scoped
def cube_scatter_direct(mine, other, gate):
    if other is not None:
        mine = mine + swap(other, "c")
    if gate is not None:
        mine = after(mine, gate)
    across = [(0, 3), (1, 2), (2, 1), (3, 0)]
    by_y, by_x = swap(mine[1], "y"), swap(mine[2], "x")
    by_both = lax.ppermute(mine[3], ("x", "y"), across)
    return mine[0], by_y, by_x, by_both


def place_ref():
    x, y, c = (lax.axis_index(name) for name in "xyc")
    return jnp.stack([x * 2 + y, c]).astype(jnp.int32)


def core_order(place, own, other):
    first = place[1] == 0
    return jnp.concatenate([jnp.where(first, own, other), jnp.where(first, other, own)], axis=0)


def core_split(place, values):
    half = values.shape[0] // 2
    first = place[1] == 0
    low, high = values[:half], values[half:]
    return jnp.where(first, low, high), jnp.where(first, high, low)


def near_spec(rows, cols):
    return pl.BlockSpec((rows, cols), lambda i, place: (i ^ place[0], 0))


def here_spec(rows, cols):
    return pl.BlockSpec((rows, cols), lambda i, place: (i, 0))


def settle_kernel(place, own_ref, other_ref, *out_refs):
    values = core_order(place, own_ref[...], other_ref[...])
    start = 0
    for out_ref in out_refs:
        out_ref[...] = values[:, start : start + out_ref.shape[1]]
        start += out_ref.shape[1]


def settle(own, other, rows, cuts):
    cols = own.shape[1]
    return call(
        settle_kernel,
        tuple(shape((8 * rows, n), own.dtype) for n in cuts),
        (4,),
        [near_spec(rows, cols)] * 2,
        tuple(here_spec(2 * rows, n) for n in cuts),
        prefetch=1,
    )(place_ref(), own, other)


def unsettle_kernel(place, *refs):
    values = jnp.concatenate([ref[...].astype(BF16) for ref in refs[:-2]], axis=1)
    refs[-2][...], refs[-1][...] = core_split(place, values)


def unsettle(parts, rows):
    cols = sum(a.shape[1] for a in parts)
    return call(
        unsettle_kernel,
        (shape((4 * rows, cols), BF16),) * 2,
        (4,),
        [near_spec(2 * rows, a.shape[1]) for a in parts],
        (here_spec(rows, cols),) * 2,
        prefetch=1,
    )(place_ref(), *parts)


def settle_groups_kernel(place, own_ref, other_ref, main_ref, misc_ref):
    groups, rows = own_ref.shape[1], own_ref.shape[2]
    first = place[1] == 0
    main = main_ref.shape[-1]
    for far in range(groups):
        own, other = own_ref[0, far], other_ref[0, far]
        at = lax.rem(place[2] - far + groups, groups)
        for core in range(2):
            values = jnp.where(first, own, other) if core == 0 else jnp.where(first, other, own)
            main_ref[pl.ds(at, 1), core] = values[None, :, :main]
            misc_ref[pl.ds(at, 1), core] = values[None, :, main:]


def settle_groups(own, other, main):
    _, groups, rows, cols = own.shape
    spec = pl.BlockSpec((1, groups, rows, cols), lambda i, place: (i ^ place[0], 0, 0, 0))
    outs = call(
        settle_groups_kernel,
        tuple(shape((groups, 8, rows, n), own.dtype) for n in (main, cols - main)),
        (4,),
        [spec, spec],
        tuple(
            pl.BlockSpec((groups, 2, rows, n), lambda i, place: (0, i, 0, 0))
            for n in (main, cols - main)
        ),
        prefetch=1,
    )(jnp.concatenate([place_ref(), lax.axis_index("z")[None]]), own, other)
    return tuple(out.reshape(groups * 8 * rows, -1) for out in outs)


def project_kernel(
    place, own_ref, other_ref, gain_ref, one_ref, two_ref, step_ref, cos_ref, sin_ref,
    normed_ref, q_ref, x_ref, kv_ref, bc_ref, dt_ref,
):
    rows = own_ref.shape[0] // 2
    flip = (place[0] & 1) == 1
    pieces = []
    own_low, own_high = own_ref[:rows], own_ref[rows:]
    other_low, other_high = other_ref[:rows], other_ref[rows:]
    pieces.append(
        core_order(
            place, jnp.where(flip, own_high, own_low), jnp.where(flip, other_high, other_low)
        )
    )
    pieces.append(
        core_order(
            place, jnp.where(flip, own_low, own_high), jnp.where(flip, other_low, other_high)
        )
    )
    values = jnp.concatenate(pieces, axis=0).astype(F32)
    scale = lax.rsqrt(jnp.mean(values * values, axis=1, keepdims=True) + EPS)
    normed = (values * scale * gain_ref[...]).astype(BF16)
    normed_ref[...] = normed
    cosine, sine = cos_ref[...], sin_ref[...]

    def turned(v):
        return (v * cosine + pltpu.roll(v, HD // 2, 1) * sine).astype(BF16)

    one = mm(normed, one_ref[...], 1, 0)
    q_ref[...] = turned(one[:, :HD])
    x_ref[...] = one[:, HD:].astype(BF16)
    at = pl.multiple_of(place[2] * HD, HD)
    lead = KVH * HD
    kv_w = jnp.concatenate([two_ref[:, pl.ds(at, HD)], two_ref[:, pl.ds(lead + at, HD)]], axis=1)
    kv = mm(normed, kv_w, 1, 0)
    kv_ref[:, :HD] = turned(kv[:, :HD])
    kv_ref[:, HD:] = kv[:, HD:].astype(BF16)
    bc_ref[...] = mm(normed, two_ref[:, 2 * lead :], 1, 0).astype(BF16)
    dt_ref[...] = mm(normed, step_ref[...], 1, 0).astype(BF16)


def project(kv_head, own, other, gain, w_one, w_two, w_dt, tables, rows):
    total = 8 * rows
    width = own.shape[1]
    cut = total // 2
    widths = (width, HD, w_one.shape[1] - HD, 2 * HD, w_two.shape[1] - 2 * KVH * HD, 128)
    near = pl.BlockSpec((2 * rows, width), lambda i, place: (i ^ (place[0] // 2), 0))

    def fixed(a):
        return pl.BlockSpec(a.shape, lambda i, place: (0, 0))

    return call(
        project_kernel,
        tuple(shape((total, n), BF16) for n in widths),
        (2,),
        [near, near, fixed(gain), fixed(w_one), fixed(w_two), fixed(w_dt)]
        + [here_spec(cut, HD)] * 2,
        tuple(here_spec(cut, n) for n in widths),
        prefetch=1,
    )(
        jnp.concatenate([place_ref(), kv_head[None].astype(jnp.int32)]),
        own, other, gain, w_one, w_two, w_dt, *tables,
    )


def grad_early_kernel(normed_ref, q_ref, z_ref, w_ref, out_ref, gain_ref):
    grad = jnp.concatenate([q_ref[...], z_ref[...]], axis=1)
    grad = mm(normed_ref[...], grad, 0, 0)
    out_ref[...] = grad.astype(BF16)
    q_cols, z_cols = q_ref.shape[1], z_ref.shape[1]
    w = jnp.concatenate([w_ref[:, :q_cols], w_ref[:, w_ref.shape[1] - z_cols :]], axis=1)
    gain = jnp.sum(grad * w.astype(F32), axis=1, keepdims=True)
    gain_ref[...] = jnp.broadcast_to(gain, gain_ref.shape)


def grad_early(groups, normed, q, z, w_all):
    total, width = normed.shape
    rows = width // groups

    def fixed(a):
        return pl.BlockSpec(a.shape, lambda i: (0, 0))

    def flow(cols):
        return pl.BlockSpec((rows, cols), lambda i: (i, 0))

    cols = q.shape[1] + z.shape[1]
    return call(
        grad_early_kernel,
        (shape((width, cols), BF16), shape((width, 128))),
        (groups,),
        [pl.BlockSpec((total, rows), lambda i: (0, i)), fixed(q), fixed(z), flow(w_all.shape[1])],
        (flow(cols), flow(128)),
    )(normed, q, z, w_all)


def grad_late_kernel(
    place, normed_ref, x_ref, kv_ref, bc_ref, dt_ref, w_ref, gain_ref, gain_two_ref,
    x_out_ref, own_ref, other_ref,
):
    rows = own_ref.shape[2]
    head = place[2]
    first = place[1] == 0
    normed = normed_ref[...]
    x_cols, bc_cols = x_ref.shape[1], bc_ref.shape[1]
    lead = 2 * KVH * HD
    start = w_ref.shape[1] - x_cols - 128 - bc_cols - lead
    grad_x = mm(normed, x_ref[...], 0, 0)
    x_out_ref[...] = grad_x.astype(BF16)
    gain = jnp.sum(grad_x * w_ref[:, start - x_cols : start].astype(F32), axis=1, keepdims=True)
    kv = mm(normed, kv_ref[...], 0, 0)
    zero = jnp.zeros((kv.shape[0], HD), F32)
    parts = []
    for part in (kv[:, :HD], kv[:, HD:]):
        parts += [jnp.where(head == i, part, zero) for i in range(KVH)]
    two = jnp.concatenate(parts + [mm(normed, bc_ref[...], 0, 0)], axis=1)
    wide = lead + bc_cols
    gain = gain + jnp.sum(two * w_ref[:, start : start + wide].astype(F32), axis=1, keepdims=True)
    dt = mm(normed, dt_ref[...], 0, 0) * w_ref[:, start + wide : start + wide + 128].astype(F32)
    gain = gain + jnp.sum(dt, axis=1, keepdims=True) + gain_ref[:, 0:1]
    lane = lax.broadcasted_iota(jnp.int32, (gain.shape[0], 128), 1)
    gains = jnp.where(lane == 0, gain, jnp.where(lane == 1, gain_two_ref[...], 0.0))
    grad = jnp.concatenate([two.astype(BF16), gains.astype(BF16)], axis=1)
    for spot in range(4):
        low = grad[2 * spot * rows : (2 * spot + 1) * rows]
        high = grad[(2 * spot + 1) * rows : (2 * spot + 2) * rows]
        at = pl.ds(spot ^ place[0], 1)
        own_ref[at, 0] = jnp.where(first, low, high)[None]
        other_ref[at, 0] = jnp.where(first, high, low)[None]


def grad_late(kv_head, groups, normed, x, kv, bc, dt, w_all, gain, gain_two):
    total, width = normed.shape
    block = width // groups
    rows = block // 8
    cols = 2 * KVH * HD + bc.shape[1] + 128

    def fixed(a):
        return pl.BlockSpec(a.shape, lambda i, place: (0, 0))

    def flow(n):
        return pl.BlockSpec((block, n), lambda i, place: (i, 0))

    return call(
        grad_late_kernel,
        (shape((width, x.shape[1]), BF16),) + (shape((4, groups, rows, cols), BF16),) * 2,
        (groups,),
        [pl.BlockSpec((total, block), lambda i, place: (0, i))]
        + [fixed(a) for a in (x, kv, bc, dt)]
        + [flow(w_all.shape[1]), flow(128), flow(1)],
        (flow(x.shape[1]),)
        + (pl.BlockSpec((4, 1, rows, cols), lambda i, place: (0, i, 0, 0)),) * 2,
        prefetch=1,
    )(
        jnp.concatenate([place_ref(), kv_head[None].astype(jnp.int32)]),
        normed, x, kv, bc, dt, w_all, gain, gain_two,
    )


def assemble_kernel(place, q_ref, x_ref, kv_ref, bc_ref, dt_ref, z_ref, own_ref, other_ref):
    head = place[2]
    zero = jnp.zeros((kv_ref.shape[0], HD), BF16)
    parts = []
    for part in (kv_ref[:, :HD], kv_ref[:, HD:]):
        parts += [jnp.where(head == i, part, zero) for i in range(KVH)]
    wide = jnp.concatenate(
        [q_ref[...], x_ref[...]] + parts + [bc_ref[...], dt_ref[...], z_ref[...]], axis=1
    )
    own_ref[...], other_ref[...] = core_split(place, wide)


def assemble(kv_head, rows, *parts):
    total = parts[0].shape[0]
    wide = sum(a.shape[1] for a in parts) + 2 * (KVH - 1) * HD
    return call(
        assemble_kernel,
        (shape((total // 2, wide), BF16),) * 2,
        (4,),
        [near_spec(2 * rows, a.shape[1]) for a in parts],
        (here_spec(rows, wide),) * 2,
        prefetch=1,
    )(jnp.concatenate([place_ref(), kv_head[None].astype(jnp.int32)]), *parts)


def halves(pack):
    x = lax.axis_index("x")
    own = lax.dynamic_index_in_dim(pack, x, 0, False)
    return own, lax.dynamic_index_in_dim(pack, x ^ 1, 0, False)


@scoped
def weight_gather(own, got):
    x = lax.axis_index("x")
    both = jnp.concatenate([jnp.where(x == 0, own, got), jnp.where(x == 0, got, own)], axis=0)
    return lax.all_gather(both, "z", axis=0, tiled=True)


def halves_in_order(own, got, axis):
    x = lax.axis_index("x")
    return jnp.concatenate([jnp.where(x == 0, own, got), jnp.where(x == 0, got, own)], axis=axis)


def both_halves(own, got):
    return halves_in_order(own, got, 1).astype(F32)


@scoped
def line_scatter(grad):
    return lax.psum_scatter(grad, "z", scatter_dimension=0, tiled=True)


@scoped
def own_and_got(part):
    x = lax.axis_index("x")
    part = part.reshape(2, -1, part.shape[1])
    got = swap(lax.dynamic_index_in_dim(part, x ^ 1, 0, False), "x")
    return lax.dynamic_index_in_dim(part, x, 0, False), got


def lanes_of(cols, heads):
    rows = cols.shape[0]
    low = lax.broadcasted_iota(jnp.int32, (rows, 2 * MP), 1) < MP
    return jnp.concatenate(
        [
            jnp.where(low, cols[:, 2 * j : 2 * j + 1], cols[:, 2 * j + 1 : 2 * j + 2])
            for j in range(heads // 2)
        ],
        axis=1,
    )


def head_sums(values):
    wide = values.shape[1]
    lane = lax.broadcasted_iota(jnp.int32, (wide, 128), 0) // MP
    pick = (lane == lax.broadcasted_iota(jnp.int32, (wide, 128), 1)).astype(F32)
    return mm(values, pick, 1, 0, EXACT)


def softplus(v):
    return jnp.maximum(v, 0.0) + jnp.log1p(jnp.exp(-jnp.abs(v)))


def sigmoid(v):
    return 1.0 / (1.0 + jnp.exp(-v))


def chunk_common(bc_ref, dt_in_ref, dt_row_ref, par_ref, par_col_ref, seg_col_ref, seg_row_ref, wide):
    heads = wide // MP
    states = bc_ref.shape[1] // 2
    b_val = bc_ref[:, :states]
    c_val = bc_ref[:, states:]
    raw = dt_in_ref[...].astype(F32) + par_ref[0:1, :]
    dt = softplus(raw)
    rate = par_ref[1:2, :]
    raw_row = dt_row_ref[...].astype(F32) + par_col_ref[:, 0:1]
    e_row = -softplus(raw_row) * par_col_ref[:, 1:2]
    first = lax.broadcasted_iota(jnp.int32, (CHUNK, CHUNK), 0)
    second = lax.broadcasted_iota(jnp.int32, (CHUNK, CHUNK), 1)
    lower = (first >= second).astype(F32)
    run = mm(lower, -dt * rate, 1, 0, EXACT)
    run_row = mm(e_row, lower, 1, 1, EXACT)
    bias = jnp.where((first >= second) & (seg_col_ref[...] == seg_row_ref[0]), 0.0, NEGATIVE)
    return heads, b_val, c_val, raw, dt, rate, run, run_row, bias, lower


def mamba_local_kernel(
    x_in_ref, bc_in_ref, dt_in_ref, dt_row_ref, par_ref, par_col_ref, skip_ref, seg_col_ref, seg_row_ref, marks_ref,
    y_ref, run_ref, held_ref, total_ref, starts_ref, state, base_run,
):
    step = pl.program_id(0)
    wide = skip_ref.shape[1]
    heads, b_val, c_val, raw, dt, rate, run, run_row, bias, _ = chunk_common(
        bc_in_ref, dt_in_ref, dt_row_ref, par_ref, par_col_ref, seg_col_ref, seg_row_ref, wide
    )

    @pl.when(step == 0)
    def _():
        state[...] = jnp.zeros_like(state)
        base_run[...] = jnp.zeros_like(base_run)

    x_val = x_in_ref[...].astype(F32)
    seg = seg_col_ref[...]
    label = marks_ref[step]
    final = marks_ref[step + 1]
    held = state[...]
    starts_ref[0] = held
    x_dt = x_val * lanes_of(dt, heads)
    x_dt_b = x_dt.astype(BF16)
    entry = jnp.where(seg == label, jnp.exp(run), 0.0)
    last = run[CHUNK - 1 : CHUNK, :]
    tail = jnp.where(seg == final, jnp.exp(last - run), 0.0)
    y_val = skip_ref[...] * x_val
    y_val = y_val + lanes_of(entry, heads) * mm(c_val, held.astype(BF16), 1, 0)
    gram = mm(c_val, b_val, 1, 1)
    low = lax.broadcasted_iota(jnp.int32, (CHUNK, 2 * MP), 1) < MP
    parts = []
    for pair in range(heads // 2):
        both = x_dt_b[:, pair * 2 * MP : (pair + 1) * 2 * MP]
        outs = []
        for h in (2 * pair, 2 * pair + 1):
            decay = jnp.exp(run[:, h : h + 1] - run_row[h : h + 1, :] + bias)
            outs.append(mm((decay * gram).astype(BF16), both, 1, 0))
        parts.append(jnp.where(low, outs[0], outs[1]))
    y_ref[...] = y_val + jnp.concatenate(parts, axis=1)
    fresh = mm(b_val, (x_dt * lanes_of(tail, heads)).astype(BF16), 0, 0)
    kept = jnp.where(label == final, jnp.exp(last), 0.0)
    new = lanes_of(jnp.broadcast_to(kept, (8, 128)), heads)[0:1] * held + fresh
    state[...] = new
    held_ref[...] = new
    run_all = run + base_run[0:1, :]
    run_ref[...] = run_all
    base_run[...] = jnp.broadcast_to(run_all[CHUNK - 1 : CHUNK, :], base_run.shape)
    total_ref[...] = jnp.exp(base_run[...])


def mamba_close_kernel(bc_in_ref, gate_ref, y_ref, run_ref, seg_col_ref, held_ref, marks_ref, out_ref, full_ref):
    wide = y_ref.shape[1]
    heads = wide // MP
    states = held_ref.shape[0]
    c_val = bc_in_ref[:, states:]
    entry = jnp.where(seg_col_ref[...] == marks_ref[0], jnp.exp(run_ref[...]), 0.0)
    y_val = y_ref[...] + lanes_of(entry, heads) * mm(c_val, held_ref[...].astype(BF16), 1, 0)
    full_ref[...] = y_val
    z_val = gate_ref[...].astype(F32)
    out_ref[...] = (y_val * z_val * sigmoid(z_val)).astype(BF16)


def mamba_grad_state_kernel(
    bc_in_ref, gate_ref, y_ref, grad_ref, run_ref, seg_col_ref, marks_ref, out_ref, gate_grad_ref
):
    wide = grad_ref.shape[1]
    heads = wide // MP
    states = out_ref.shape[0]
    c_val = bc_in_ref[:, states:]
    z_val = gate_ref[...].astype(F32)
    entry = jnp.where(seg_col_ref[...] == marks_ref[0], jnp.exp(run_ref[...]), 0.0)
    grad = grad_ref[...].astype(F32)
    sig = sigmoid(z_val)
    grad_y = grad * z_val * sig
    gate_grad_ref[...] = (grad * y_ref[...] * (sig * (1.0 + z_val * (1.0 - sig)))).astype(BF16)

    @pl.when(pl.program_id(0) == 0)
    def _():
        out_ref[...] = jnp.zeros_like(out_ref)

    out_ref[...] += mm(c_val, (grad_y * lanes_of(entry, heads)).astype(BF16), 0, 0)


def mamba_grad_near_kernel(
    x_in_ref, bc_in_ref, dt_in_ref, dt_row_ref, par_ref, par_col_ref, skip_ref, seg_col_ref, seg_row_ref, marks_ref,
    gate_ref, run_ref, starts_ref, held_ref, grad_ref,
    x_grad_ref, b_ref, c_ref, e_ref, carry_ref, skip_sum_ref,
):
    step = pl.program_id(0)
    wide = skip_ref.shape[1]
    heads, b_val, c_val, raw, dt, rate, run, run_row, bias, lower = chunk_common(
        bc_in_ref, dt_in_ref, dt_row_ref, par_ref, par_col_ref, seg_col_ref, seg_row_ref, wide
    )

    @pl.when(step == 0)
    def _():
        skip_sum_ref[...] = jnp.zeros_like(skip_sum_ref)

    z_val = gate_ref[...].astype(F32)
    x_val = x_in_ref[...].astype(F32)
    label = marks_ref[step]
    before = run_ref[0:1, :] - run[0:1, :]
    carry = jnp.where(label == marks_ref[0], jnp.exp(before), 0.0)
    held = starts_ref[0] + lanes_of(jnp.broadcast_to(carry, (8, 128)), heads)[0:1] * held_ref[...]
    held_b = held.astype(BF16)
    grad_y = grad_ref[...].astype(F32) * z_val * sigmoid(z_val)
    dt_wide = lanes_of(dt, heads)
    x_dt_b = (x_val * dt_wide).astype(BF16)
    entry = lanes_of(jnp.where(seg_col_ref[...] == label, jnp.exp(run), 0.0), heads)
    grad_in = (entry * grad_y).astype(BF16)
    run_grad = head_sums(grad_y * entry * mm(c_val, held_b, 1, 0))
    grad_c = mm(grad_in, held_b, 1, 1)
    carry_ref[0] = mm(c_val, grad_in, 0, 0)
    gram = mm(c_val, b_val, 1, 1)
    low = lax.broadcasted_iota(jnp.int32, (CHUNK, 2 * MP), 1) < MP
    lane = lax.broadcasted_iota(jnp.int32, (CHUNK, 128), 1)
    grad_y_b = grad_y.astype(BF16)
    none = jnp.zeros((CHUNK, 2 * MP), BF16)
    gram_grad = None
    parts, cols = [], []
    for pair in range(heads // 2):
        span = slice(pair * 2 * MP, (pair + 1) * 2 * MP)
        outs = []
        for h in (2 * pair, 2 * pair + 1):
            mask = low if h % 2 == 0 else ~low
            decay = jnp.exp(run[:, h : h + 1] - run_row[h : h + 1, :] + bias)
            mixing = (decay * gram).astype(BF16)
            outs.append(mm(mixing, grad_y_b[:, span], 0, 0))
            mixing_grad = mm(jnp.where(mask, grad_y_b[:, span], none), x_dt_b[:, span], 1, 1)
            weighted = mixing_grad * decay
            gram_grad = weighted if gram_grad is None else gram_grad + weighted
            weighted = weighted * gram
            run_grad = run_grad + jnp.where(
                lane == h, jnp.sum(weighted, axis=1, keepdims=True), 0.0
            )
            cols.append(jnp.sum(weighted, axis=0, keepdims=True))
        parts.append(jnp.where(low, outs[0], outs[1]))
    gram_grad_b = gram_grad.astype(BF16)
    c_ref[...] = (grad_c + mm(gram_grad_b, b_val, 1, 0)).astype(BF16)
    b_ref[...] = mm(gram_grad_b, c_val, 0, 0)
    x_grad_ref[...] = jnp.concatenate(parts, axis=1)
    col_grad = jnp.concatenate(cols + [jnp.zeros((128 - heads, CHUNK), F32)], axis=0)
    e_ref[...] = mm(lower, run_grad, 0, 0, EXACT) - mm(lower, col_grad, 0, 1, EXACT)
    skip_sum_ref[0:1, :] += jnp.sum(grad_y * x_val, axis=0, keepdims=True)


def mamba_grad_kernel(
    x_in_ref, bc_in_ref, dt_in_ref, dt_row_ref, par_ref, par_col_ref, skip_ref, seg_col_ref, seg_row_ref, marks_ref,
    gate_ref, run_ref, starts_ref, held_ref, grad_ref,
    x_grad_ref, b_grad_ref, c_grad_ref, e_grad_ref, carry_ref, deep_ref,
    x_ref, bc_ref, dt_ref, sums_ref, deep,
):
    step = pl.num_programs(0) - 1 - pl.program_id(0)
    wide = skip_ref.shape[1]
    heads = wide // MP
    states = b_grad_ref.shape[1]
    b_val = bc_in_ref[:, :states]
    raw = dt_in_ref[...].astype(F32) + par_ref[0:1, :]
    dt = softplus(raw)
    rate = par_ref[1:2, :]
    first = lax.broadcasted_iota(jnp.int32, (CHUNK, CHUNK), 0)
    second = lax.broadcasted_iota(jnp.int32, (CHUNK, CHUNK), 1)
    lower = (first >= second).astype(F32)
    run = run_ref[...]

    @pl.when(pl.program_id(0) == 0)
    def _():
        deep[...] = deep_ref[...]
        sums_ref[...] = jnp.zeros_like(sums_ref)

    z_val = gate_ref[...].astype(F32)
    x_val = x_in_ref[...].astype(F32)
    seg = seg_col_ref[...]
    label = marks_ref[step]
    final = marks_ref[step + 1]
    last = run[CHUNK - 1 : CHUNK, :]
    e_first = -dt[0:1, :] * rate
    before = run[0:1, :] - e_first
    carry = jnp.where(label == marks_ref[0], jnp.exp(before), 0.0)
    held = starts_ref[0] + lanes_of(jnp.broadcast_to(carry, (8, 128)), heads)[0:1] * held_ref[...]
    after_b = deep[...].astype(BF16)
    grad_y = grad_ref[...].astype(F32) * z_val * sigmoid(z_val)
    dt_wide = lanes_of(dt, heads)
    tail = lanes_of(jnp.where(seg == final, jnp.exp(last - run), 0.0), heads)
    x_tail = x_val * dt_wide * tail
    back = mm(b_val, after_b, 1, 0)
    bc_ref[:, :states] = (b_grad_ref[...] + mm(x_tail.astype(BF16), after_b, 1, 1)).astype(BF16)
    bc_ref[:, states:] = c_grad_ref[...]
    tail_grad = head_sums(x_tail * back)
    kept = jnp.where(label == final, jnp.exp(last - before), 0.0)
    kept_wide = lanes_of(jnp.broadcast_to(kept, (8, 128)), heads)[0:1]
    kept_grad = head_sums(
        jnp.broadcast_to(kept_wide * jnp.sum(deep[...] * held, axis=0, keepdims=True), (8, wide))
    )
    last_grad = jnp.sum(tail_grad, axis=0, keepdims=True) + kept_grad[0:1]
    deep[...] = kept_wide * deep[...] + carry_ref[0]
    x_dt_grad = x_grad_ref[...] + tail * back
    x_ref[...] = (x_dt_grad * dt_wide + skip_ref[...] * grad_y).astype(BF16)
    e_grad = e_grad_ref[...] - mm(lower, tail_grad, 0, 0, EXACT) + last_grad
    dt_grad = head_sums(x_dt_grad * x_val) - rate * e_grad
    raw_grad = dt_grad * sigmoid(raw)
    lane = lax.broadcasted_iota(jnp.int32, (CHUNK, 128), 1)
    dt_ref[...] = jnp.where(lane < heads, raw_grad, 0.0).astype(BF16)
    sums_ref[0:1, :] += jnp.sum(-rate * dt * e_grad, axis=0, keepdims=True)
    sums_ref[1:2, :] += jnp.sum(raw_grad, axis=0, keepdims=True)


def seen(kseg_ref, qseg, first_query, block):
    rows = qseg.shape[0]
    key_pos = block * KEYS + lax.broadcasted_iota(jnp.int32, (rows, KEYS), 1)
    query_pos = first_query + lax.broadcasted_iota(jnp.int32, (rows, KEYS), 0)
    return (key_pos <= query_pos) & (kseg_ref[pl.ds(block, 1), :] == qseg)


def key_span(block, where_ref, groups):
    far = where_ref[0] - block // 2
    at = jnp.where((block & 1) == where_ref[1], far, groups + far)
    return pl.ds(pl.multiple_of(at * KEYS, KEYS), KEYS)


def attend_kernel(low_ref, high_ref, start_ref, where_ref, q_ref, kv_ref, kseg_ref, qseg_ref, att_ref, log_ref):
    step = pl.program_id(0)
    rows = q_ref.shape[0]
    query = q_ref[...]
    qseg = qseg_ref[...]
    first_query = start_ref[0] + step * rows
    scale = HD**-0.5

    def visit(block, state):
        peak, total, acc = state
        span = key_span(block, where_ref, kv_ref.shape[0] // (2 * KEYS))
        scores = mm(query, kv_ref[span, :HD], 1, 1) * scale
        scores = jnp.where(seen(kseg_ref, qseg, first_query, block), scores, NEGATIVE)
        new_peak = jnp.maximum(peak, jnp.max(scores, axis=1, keepdims=True))
        weights = jnp.exp(scores - new_peak)
        rescale = jnp.exp(peak - new_peak)
        total = total * rescale + jnp.sum(weights, axis=1, keepdims=True)
        acc = acc * rescale + mm(weights.astype(BF16), kv_ref[span, HD:], 1, 0)
        return new_peak, total, acc

    peak, total, acc = lax.fori_loop(
        low_ref[step],
        high_ref[step],
        visit,
        (
            jnp.full((rows, 1), NEGATIVE, F32),
            jnp.zeros((rows, 1), F32),
            jnp.zeros((rows, HD), F32),
        ),
    )
    att_ref[...] = acc / total
    log_ref[...] = jnp.broadcast_to(peak + jnp.log(total), log_ref.shape)


def attend_grad_kernel(
    low_ref, high_ref, start_ref, where_ref, q_ref, kv_ref, kseg_ref, qseg_ref, att_ref, log_ref,
    grad_ref, dq_ref, dkv_ref, sums,
):
    step = pl.program_id(0)
    rows = q_ref.shape[0]
    query = q_ref[...]
    grad = grad_ref[...]
    qseg = qseg_ref[...]
    log_total = log_ref[:, 0:1]
    first_query = start_ref[0] + step * rows
    scale = HD**-0.5
    delta = jnp.sum(grad.astype(F32) * att_ref[...], axis=1, keepdims=True)

    @pl.when(step == 0)
    def _():
        sums[...] = jnp.zeros_like(sums)

    def visit(block, acc):
        span = key_span(block, where_ref, kv_ref.shape[0] // (2 * KEYS))
        keys = kv_ref[span, :HD]
        scores = mm(query, keys, 1, 1) * scale - log_total
        scores = jnp.where(seen(kseg_ref, qseg, first_query, block), scores, NEGATIVE)
        probs = jnp.exp(scores)
        probs_grad = mm(grad, kv_ref[span, HD:], 1, 1)
        scores_grad = (probs * (probs_grad - delta)).astype(BF16)
        sums[span, :HD] += mm(scores_grad, query, 0, 0)
        sums[span, HD:] += mm(probs.astype(BF16), grad, 0, 0)
        return acc + mm(scores_grad, keys, 1, 0)

    acc = lax.fori_loop(low_ref[step], high_ref[step], visit, jnp.zeros((rows, HD), F32))
    dq_ref[...] = acc * scale

    @pl.when(step == pl.num_programs(0) - 1)
    def _():
        dkv_ref[:, :HD] = (sums[:, :HD] * scale).astype(BF16)
        dkv_ref[:, HD:] = sums[:, HD:].astype(BF16)


def call(kernel, out_shape, grid, in_specs, out_specs, scratch=(), prefetch=0, cost=None):
    return pl.pallas_call(
        kernel,
        out_shape=out_shape,
        grid_spec=pltpu.PrefetchScalarGridSpec(
            num_scalar_prefetch=prefetch,
            grid=grid,
            in_specs=in_specs,
            out_specs=out_specs,
            scratch_shapes=list(scratch),
        ),
        compiler_params=pltpu.CompilerParams(
            vmem_limit_bytes=VMEM_BYTES, dimension_semantics=("arbitrary",) * len(grid)
        ),
        cost_estimate=cost,
        name=kernel.__name__,
    )


def shape(dims, dtype=F32):
    return jax.ShapeDtypeStruct(dims, dtype)


def rope_tables(positions):
    half = HD // 2
    frequency = jnp.exp(jnp.arange(half, dtype=F32) * (-2.0 * math.log(THETA) / HD))
    angle = positions.astype(F32)[:, None] * frequency[None, :]
    cosine, sine = jnp.cos(angle), jnp.sin(angle)
    return jnp.concatenate([cosine, cosine], 1), jnp.concatenate([-sine, sine], 1)


def rope(values, tables):
    cosine, sine = tables
    return values * cosine + jnp.concatenate([values[:, HD // 2 :], values[:, : HD // 2]], 1) * sine


def rope_back(values, tables):
    cosine, sine = tables
    return values * cosine - jnp.concatenate([values[:, HD // 2 :], values[:, : HD // 2]], 1) * sine


def unit(values):
    return values * lax.rsqrt(jnp.mean(values * values, axis=-1, keepdims=True) + EPS)


def norm_back(values, gain, grad):
    scale = lax.rsqrt(jnp.mean(values * values, axis=-1, keepdims=True) + EPS)
    u = values * scale
    inner = jnp.mean(grad * gain * u, axis=-1, keepdims=True)
    return scale * (grad * gain - u * inner), jnp.sum(grad * u, axis=0)


def shards(
    tokens, seg_ids, cotangent, gain_mix, q_w, kv_w, zx_w, dt_w, bc_w,
    a_log, dt_bias, skip, wo_w, wm_w, gain_ff, gu_w, down_w,
):
    groups = lax.axis_size("z")
    z, x, y, c = (lax.axis_index(name) for name in "zxyc")
    own_rows, width = tokens.shape
    group = 8 * own_rows
    rows_w = q_w.shape[0]
    part = kv_w.shape[0]
    ratio = rows_w // part
    heads = dt_w.shape[1] // 2
    wide = heads * MP
    states = bc_w.shape[1] // 2
    ff = gu_w.shape[2] // 2
    inner = q_w.shape[1] // 2
    steps = group // CHUNK

    zx_cut = zx_w.reshape(rows_w, 2, 2, wide).transpose(1, 2, 0, 3)
    pack_z = zx_cut[0]
    pack_one = jnp.concatenate([q_w.reshape(rows_w, 2, inner).transpose(1, 0, 2), zx_cut[1]], axis=2)
    pack_out = jnp.concatenate(
        [
            wo_w.reshape(rows_w, 2, inner).transpose(1, 0, 2),
            wm_w.reshape(rows_w, 2, wide).transpose(1, 0, 2),
        ],
        axis=2,
    )
    pack_gu = gu_w.reshape(rows_w, 2, 2, ff).transpose(2, 0, 1, 3).reshape(2, rows_w, 2 * ff)
    pack_down = down_w.reshape(rows_w, 2, ff).transpose(1, 0, 2)
    kv_cols = kv_w.shape[1] * kv_w.shape[2]
    bc_cols = bc_w.shape[1]
    lead = kv_cols + bc_cols
    dt_cols = dt_w.shape[1]
    dt_part = dt_w.reshape(ratio, part, dt_cols).transpose(1, 0, 2).reshape(part, ratio * dt_cols)
    pack_two = jnp.concatenate(
        [kv_w.reshape(part, kv_cols), bc_w, gain_mix[:, None], gain_ff[:, None], dt_part], axis=1
    )
    used = pack_two.shape[1]
    total_cols = -(-used // 128) * 128
    pack_two = jnp.pad(pack_two, ((0, 0), (0, total_cols - used)))

    def put_two(out, at, number, value):
        return lax.dynamic_update_slice(out, value[None], (at, 0, 0))

    own_one, give_one = halves(pack_one)
    own_out, give_out = halves(jnp.concatenate([pack_out, pack_z], axis=2))
    own_ff, give_ff = halves(jnp.concatenate([pack_gu, pack_down], axis=2))
    two_far = from_ring("whole_rows", pack_two)
    seg_pair = jnp.zeros((2, seg_ids.shape[0]), jnp.int32)
    seg_pair = lax.dynamic_update_index_in_dim(seg_pair, seg_ids, x, 0)
    seg_pair = lax.dynamic_update_index_in_dim(seg_pair, swap(seg_ids, "x"), x ^ 1, 0)
    seg_own = seg_pair.reshape(1, group)
    seg_far = from_ring("ids", seg_own)
    two = jnp.stack([pack_two] + two_far)[None]
    got_one = swap(give_one, "x")
    own_one, got_one, two, *seg_far = lax.optimization_barrier((own_one, got_one, two, *seg_far))
    seg_all = jnp.zeros((groups, group), jnp.int32)
    for far, got in enumerate([seg_own, *seg_far]):
        seg_all = lax.dynamic_update_slice(seg_all, got, ((z - far + groups) % groups, 0))
    w_one = weight_gather("w_one", own_one, got_one)
    two_own, two_other, _, two_low = cube_gather("whole_rows", two, 1)
    rows_own, rows_other, *_ = cube_gather("tokens", after(tokens, two_low))
    w_two, misc = settle_groups(two_own, two_other, lead)
    w_mix = weight_gather("w_mix", own_out, swap(after(give_out, rows_own), "x"))
    w_out, w_z = w_mix[:, : inner + wide], w_mix[:, inner + wide :]
    segment = seg_own.astype(F32)
    seg_col = segment.reshape(group, 1)
    seg_row = segment.reshape(steps, 1, CHUNK)
    previous = lax.dynamic_index_in_dim(seg_all, jnp.maximum(z - 1, 0), 0, False)[group - 1]
    in_label = jnp.where(z > 0, previous, -1).astype(F32)
    marks = jnp.concatenate([in_label[None], segment[0, CHUNK - 1 :: CHUNK]])

    gain_one = misc[:, 0].astype(F32)
    gain_two = misc[:, 1].astype(F32)
    dt_all = misc[:, 2 : 2 + ratio * dt_cols].reshape(
        groups, 2, 4, part, ratio, 2, heads
    )
    dt_own = lax.dynamic_index_in_dim(dt_all, y * 2 + c, 2, False)
    dt_own = lax.dynamic_index_in_dim(dt_own, x, 4, False)
    w_dt = dt_own.transpose(0, 1, 3, 2, 4).reshape(width, heads)
    kv_head = ((y * 2 + c) * 2 + x) * (inner // HD) // (QH // KVH)
    w_dt = jnp.pad(w_dt, ((0, 0), (0, 128 - heads)))

    positions = z * group + jnp.arange(group, dtype=jnp.int32)
    tables = rope_tables(positions)
    normed, query, x_in, kv_own, bc_in, dt_in = project(
        kv_head, rows_own, rows_other, gain_one[None, :], w_one, w_two, w_dt, tables, own_rows
    )
    half, quarter = group // 2, group // 4
    kv_half = lax.dynamic_slice_in_dim(kv_own, c * half, half, 0)
    kv_quarter = lax.dynamic_slice_in_dim(kv_own, c * half + x * quarter, quarter, 0)
    kv_far = from_below("kv", [kv_quarter] * groups)
    gate_in = mm(normed, w_z, 1, 0).astype(BF16)

    dt_row = jnp.pad(dt_in[:, :8].T, ((0, 8), (0, 0)))
    pad = ((0, 128 - heads),)

    def pick(values):
        return lax.dynamic_slice_in_dim(values, x * heads, heads, 0)

    rates = jnp.exp(pick(a_log))
    params = jnp.stack([jnp.pad(pick(dt_bias), pad), jnp.pad(rates, pad)])
    params = jnp.pad(params, ((0, 6), (0, 0)))
    params_col = jnp.pad(
        jnp.stack([pick(dt_bias), rates], axis=1), ((0, 16 - heads), (0, 126))
    )
    skip_wide = jnp.repeat(pick(skip), MP)[None, :]

    def flow(cols, back=False):
        at = (lambda i: (steps - 1 - i, 0)) if back else (lambda i: (i, 0))
        return pl.BlockSpec((CHUNK, cols), at)

    def chunk_specs(back=False):
        def turn(i):
            return steps - 1 - i if back else i

        return [
            flow(wide, back),
            flow(2 * states, back),
            flow(128, back),
            pl.BlockSpec((16, CHUNK), lambda i: (0, turn(i))),
            pl.BlockSpec((8, 128), lambda i: (0, 0)),
            pl.BlockSpec((16, 128), lambda i: (0, 0)),
            pl.BlockSpec((1, wide), lambda i: (0, 0)),
            flow(1, back),
            pl.BlockSpec((1, 1, CHUNK), lambda i: (turn(i), 0, 0)),
            pl.BlockSpec(memory_space=pltpu.SMEM),
        ]

    whole = pl.BlockSpec((states, wide), lambda i: (0, 0))
    smem = pl.BlockSpec(memory_space=pltpu.SMEM)
    chunk_args = (x_in, bc_in, dt_in, dt_row, params, params_col, skip_wide, seg_col, seg_row, marks)
    y_local, run, held_own, total, starts = call(
        mamba_local_kernel,
        (
            shape((group, wide)),
            shape((group, 128)),
            shape((states, wide)),
            shape((8, 128)),
            shape((steps, states, wide)),
        ),
        (steps,),
        chunk_specs(),
        (
            flow(wide),
            flow(128),
            whole,
            pl.BlockSpec((8, 128), lambda i: (0, 0)),
            pl.BlockSpec((1, states, wide), lambda i: (i, 0, 0)),
        ),
        [pltpu.VMEM((states, wide), F32), pltpu.VMEM((8, 128), F32)],
    )(*chunk_args)
    joined = jnp.where(in_label == segment[0, group - 1], 1.0, 0.0)
    factor = jnp.repeat(total[0, :heads] * joined, MP)[None, :]
    factor_rows = jnp.broadcast_to(factor, (16, wide))
    held_sent = jnp.concatenate([held_own, factor_rows], axis=0).astype(BF16)
    held_sent, *kv_far = lax.optimization_barrier((held_sent, *kv_far))
    w_ff = weight_gather("w_ff", own_ff, swap(after(give_ff, held_sent), "x"))
    w_gu, w_down = w_ff[:, : 2 * ff], w_ff[:, 2 * ff :]
    held_far = from_below("held", [held_sent] * groups)
    kv_far = jnp.stack(kv_far)
    kv_far = halves_in_order(kv_far, swap(kv_far, "x"), 1).reshape(-1, 2 * HD)
    kv_near = jnp.concatenate([kv_half, kv_far], axis=0)
    kv_near, *held_far = lax.optimization_barrier((kv_near, *held_far))
    kv_all = jnp.concatenate([kv_near, swap(kv_near, "c")], axis=0)
    w_all = jnp.concatenate([w_one, w_two, w_dt, w_z], axis=1)
    query, w_all = lax.optimization_barrier((query, w_all))
    in_held = jnp.zeros((states, wide), F32)
    for got in reversed(held_far):
        got = got.astype(F32)
        in_held = got[:states] + got[states : states + 1] * in_held

    q_rows = CHUNK
    blocks = group // q_rows
    first_rows = z * group + q_rows * jnp.arange(blocks, dtype=jnp.int32)
    first_seg = seg_own[0, ::q_rows]
    reached = jnp.arange(groups * group, dtype=jnp.int32)[None, :] < (z + 1) * group
    earlier = (seg_all.reshape(1, -1) < first_seg[:, None]) & reached
    low = jnp.sum(earlier, axis=1, dtype=jnp.int32) // KEYS
    high = (first_rows + q_rows - 1) // KEYS + 1
    start = (z * group)[None].astype(jnp.int32)
    where = jnp.stack([z, c]).astype(jnp.int32)
    key_seg = seg_all.astype(F32).reshape(groups * group // KEYS, KEYS)

    def rows_spec(cols):
        return pl.BlockSpec((q_rows, cols), lambda i, *_: (i, 0))

    def full_spec(a):
        return pl.BlockSpec(a.shape, lambda i, *_: (0, 0))

    att_full, log_total = call(
        attend_kernel,
        (shape((group, HD)), shape((group, 128))),
        (blocks,),
        [rows_spec(HD), full_spec(kv_all), full_spec(key_seg), rows_spec(1)],
        (rows_spec(HD), rows_spec(128)),
        prefetch=4,
    )(low, high, start, where, query, kv_all, key_seg, seg_col)

    ssm_out, y_full = call(
        mamba_close_kernel,
        (shape((group, wide), BF16), shape((group, wide))),
        (steps,),
        [flow(2 * states), flow(wide), flow(wide), flow(128), flow(1), whole, smem],
        (flow(wide), flow(wide)),
    )(bc_in, gate_in, y_local, run, seg_col, after(in_held, att_full), marks)

    def row_term(a, w):
        return mm(a, w, 1, 1).astype(BF16).reshape(4, own_rows, width)

    def weight_grad(pairs):
        total = None
        for a, g in pairs:
            value = mm(a, g, 0, 0)
            total = value if total is None else total + value
        return total.astype(BF16)

    stream_own = tokens.astype(F32)
    mixer_own, mixer_other = unsettle([att_full, ssm_out], own_rows)
    term_other = row_term(mixer_other, w_out)
    middle = stream_own + cube_scatter("mixed", row_term(mixer_own, w_out), term_other)[0]
    normed_two = (unit(middle) * gain_two).astype(BF16)
    two_rows = cube_gather("normed_two", normed_two)[:2]
    cot_own, cot_other, *_ = cube_gather("cotangent", after(cotangent, two_rows[0]))

    def forward(rows):
        gate_up = mm(rows, w_gu, 1, 0).astype(BF16)
        gate = gate_up[:, :ff].astype(F32)
        up = gate_up[:, ff:].astype(F32)
        sig = jax.nn.sigmoid(gate)
        return gate, up, sig, (gate * sig * up).astype(BF16)

    def backward(rows, gate, up, sig):
        grad_hidden = mm(rows, w_down, 1, 0).astype(BF16).astype(F32)
        grad_gate = grad_hidden * up * (sig * (1.0 + gate * (1.0 - sig)))
        return jnp.concatenate([grad_gate, grad_hidden * gate * sig], axis=1).astype(BF16)

    *kept_own, hidden_own = forward(two_rows[0])
    *kept_other, hidden_other = forward(two_rows[1])
    gu_other = backward(cot_other, *kept_other)
    gu_own = backward(cot_own, *kept_own)
    term_other = row_term(gu_other, w_gu)
    down_w = weight_grad(
        [(after(cot_own, term_other), hidden_own), (after(cot_other, term_other), hidden_other)]
    )
    down_part = line_scatter("down", down_w)
    term, down_w = lax.optimization_barrier((row_term(gu_own, w_gu), down_w))
    grad_normed_two, far, _ = cube_scatter("grad_normed_two", term, term_other)
    gu_w = weight_grad([(after(two_rows[0], far), gu_own), (after(two_rows[1], far), gu_other)])
    middle_part, gain_two_part = norm_back(middle, gain_two, grad_normed_two)
    grad_middle = cotangent.astype(F32) + middle_part
    grad_middle, gu_w = lax.optimization_barrier((grad_middle, gu_w))
    hidden_own, hidden_other = after(hidden_own, grad_middle), after(hidden_other, grad_middle)
    layer_other = row_term(hidden_other, w_down)
    layer_own = row_term(hidden_own, w_down)
    mixed_own, mixed_other, *_ = cube_gather(
        "grad_middle", grad_middle.astype(BF16), gate=layer_other, last_gate=layer_own
    )
    layer_terms = cube_scatter_direct("layer_out", layer_own, layer_other, mixed_own)
    layer_out = middle + sum(a.astype(F32) for a in layer_terms)
    layer_out = layer_out.astype(BF16)
    gu_part = line_scatter("gu", gu_w)
    grad_att, grad_ssm = settle(
        mm(mixed_own, w_out, 1, 0).astype(BF16),
        mm(mixed_other, w_out, 1, 0).astype(BF16),
        own_rows,
        (inner, wide),
    )

    grad_att, down_part = lax.optimization_barrier((grad_att, down_part))
    grad_query, grad_kv_all = call(
        attend_grad_kernel,
        (shape((group, HD)), shape((groups * group, 2 * HD), BF16)),
        (blocks,),
        [
            rows_spec(HD), full_spec(kv_all), full_spec(key_seg), rows_spec(1),
            rows_spec(HD), rows_spec(128), rows_spec(HD),
        ],
        (rows_spec(HD), full_spec(kv_all)),
        [pltpu.VMEM((groups * group, 2 * HD), F32)],
        prefetch=4,
    )(low, high, start, where, query, kv_all, key_seg, seg_col, att_full, log_total, grad_att)
    grad_ssm = after(grad_ssm, grad_query, layer_out)
    state_grad, grad_z = call(
        mamba_grad_state_kernel,
        (shape((states, wide)), shape((group, wide), BF16)),
        (steps,),
        [flow(2 * states), flow(wide), flow(wide), flow(wide), flow(128), flow(1), smem],
        (whole, flow(wide)),
    )(bc_in, gate_in, y_full, grad_ssm, run, seg_col, marks)
    grad_sent = jnp.concatenate([state_grad, factor_rows], axis=0).astype(BF16)
    held_far = from_above("grad_held", [grad_sent] * groups)
    grad_q = rope_back(grad_query, tables).astype(BF16)
    chunk_more = (gate_in, run, starts, in_held, after(grad_ssm, grad_sent))

    def more_specs(back=False):
        return [
            flow(wide, back),
            flow(128, back),
            pl.BlockSpec((1, states, wide), lambda i: (steps - 1 - i if back else i, 0, 0)),
            whole,
            flow(wide, back),
        ]

    near_out = call(
        mamba_grad_near_kernel,
        (
            shape((group, wide)),
            shape((group, states)),
            shape((group, states), BF16),
            shape((group, 128)),
            shape((steps, states, wide)),
            shape((8, wide)),
        ),
        (steps,),
        chunk_specs() + more_specs(),
        (
            flow(wide),
            flow(states),
            flow(states),
            flow(128),
            pl.BlockSpec((1, states, wide), lambda i: (i, 0, 0)),
            pl.BlockSpec((8, wide), lambda i: (0, 0)),
        ),
    )(*chunk_args, *chunk_more)
    kv_terms = grad_kv_all.reshape(2, groups, half, 2 * HD)
    kv_mine, *held_far = lax.optimization_barrier(
        (after(kv_terms[0], near_out[0]), *held_far)
    )
    kv_both = kv_mine + swap(kv_terms[1], "c")
    kv_terms = kv_both.reshape(groups, 2, quarter, 2 * HD)
    kv_terms = lax.dynamic_index_in_dim(kv_terms, x, 1, False) + swap(
        lax.dynamic_index_in_dim(kv_terms, x ^ 1, 1, False), "x"
    )
    kv_far = from_above("grad_kv", kv_terms)
    skip_sums = near_out[5]
    down_own, down_got = own_and_got("down", after(down_part, kv_terms))
    grad_q, gu_part, *kv_far = lax.optimization_barrier((grad_q, gu_part, *kv_far))
    qz_w, gain_early = grad_early(groups, normed, grad_q, grad_z, w_all)
    qz_part = line_scatter("qz", qz_w)
    out_w = weight_grad([(after(mixed_own, kv_both), mixer_own), (mixed_other, mixer_other)])
    out_part = line_scatter("out", out_w)
    deep = jnp.zeros((states, wide), F32)
    for got in reversed(held_far):
        got = got.astype(F32)
        deep = got[:states] + got[states : states + 1] * deep
    grad_kv_part = kv_terms[0].astype(F32)
    for got in kv_far:
        grad_kv_part = grad_kv_part + got.astype(F32)
    deep = after(deep, grad_kv_part, qz_w, down_got)
    part_tables = tuple(
        lax.dynamic_slice_in_dim(table, c * half + x * quarter, quarter, 0) for table in tables
    )
    grad_kv_part = jnp.concatenate(
        [rope_back(grad_kv_part[:, :HD], part_tables), grad_kv_part[:, HD:]], axis=1
    ).astype(BF16)
    grad_kv = lax.dynamic_update_slice(
        jnp.zeros((group, 2 * HD), BF16), grad_kv_part, (c * half + x * quarter, 0)
    )
    grad_x, grad_bc, grad_dt, sums = call(
        mamba_grad_kernel,
        (
            shape((group, wide), BF16),
            shape((group, 2 * states), BF16),
            shape((group, 128), BF16),
            shape((8, 128)),
        ),
        (steps,),
        chunk_specs(True)
        + more_specs(True)
        + [
            flow(wide, True),
            flow(states, True),
            flow(states, True),
            flow(128, True),
            pl.BlockSpec((1, states, wide), lambda i: (steps - 1 - i, 0, 0)),
            whole,
        ],
        (
            flow(wide, True),
            flow(2 * states, True),
            flow(128, True),
            pl.BlockSpec((8, 128), lambda i: (0, 0)),
        ),
        [pltpu.VMEM((states, wide), F32)],
    )(*chunk_args, *chunk_more, *near_out[:5], deep)

    grad_x, out_part = lax.optimization_barrier((grad_x, out_part))
    x_w, two_own, two_other = grad_late(
        kv_head, groups, normed, grad_x, grad_kv, grad_bc, grad_dt, w_all, gain_early,
        gain_two_part[:, None],
    )
    x_part = line_scatter("x", x_w)
    grad_own, grad_other = assemble(
        kv_head, own_rows, grad_q, after(grad_x, x_w), grad_kv, grad_bc, grad_dt, grad_z
    )
    two_mine = two_own + swap(two_other, "c")
    grad_other = after(grad_other, two_mine)
    in_other = row_term(grad_other, w_all)
    two_terms = cube_scatter_direct("grad_two", two_mine, None, None)
    grad_own, qz_part = lax.optimization_barrier((after(grad_own, in_other), qz_part))
    in_own = row_term(grad_own, w_all)
    in_sum, in_far, in_last = cube_scatter("grad_in", in_own, in_other)
    two_terms = lax.optimization_barrier((*two_terms, in_far))[:4]
    two_part = sum(a.astype(F32) for a in two_terms)
    out_own, out_got = own_and_got("out", after(out_part, in_sum))
    gu_own, gu_got = own_and_got("gu", after(gu_part, in_sum))
    qz_own, qz_got = own_and_got("qz", after(qz_part, in_sum))
    in_grad = in_sum
    input_part, _ = norm_back(stream_own, gain_one, in_grad)
    input_grad = grad_middle + input_part
    two_part = lax.psum_scatter(two_part.astype(BF16), "z", scatter_dimension=0).astype(F32)
    kv_grad = two_part[:, :kv_cols].reshape(kv_w.shape)
    bc_grad = two_part[:, kv_cols:lead]
    small = jnp.concatenate(
        [sums[0, :heads], sums[1, :heads], jnp.sum(skip_sums[0].reshape(heads, MP), axis=1)]
    )
    small = jnp.pad(small, (0, width - small.shape[0]))
    dt_w_grad = mm(after(grad_dt, in_other), normed, 0, 0)[:heads]
    tiny = jnp.concatenate([dt_w_grad, small[None]], axis=0)
    tiny = after(tiny, in_sum)
    for got in from_ring("tiny", tiny):
        tiny = tiny + got
    tiny_other = swap(tiny, "x")
    dt_grad = both_halves(
        *(
            lax.dynamic_slice_in_dim(a[:heads], (z * 2 + x) * rows_w, rows_w, 1).T
            for a in (tiny, tiny_other)
        )
    )
    small_sum = both_halves(*(a[heads, : 3 * heads].reshape(3, heads) for a in (tiny, tiny_other)))
    return (
        layer_out,
        input_grad,
        two_part[:, lead] / gain_mix.astype(F32),
        both_halves(qz_own[:, :inner], qz_got[:, :inner]),
        kv_grad,
        jnp.stack(
            [both_halves(qz_own[:, inner:], qz_got[:, inner:]), both_halves(*own_and_got("x", after(x_part, in_sum)))],
            axis=1,
        ),
        dt_grad,
        bc_grad,
        small_sum[0],
        small_sum[1],
        small_sum[2],
        both_halves(out_own[:, :inner], out_got[:, :inner]),
        both_halves(out_own[:, inner:], out_got[:, inner:]),
        two_part[:, lead + 1],
        jnp.stack(
            [both_halves(gu_own[:, :ff], gu_got[:, :ff]), both_halves(gu_own[:, ff:], gu_got[:, ff:])],
            axis=1,
        ),
        both_halves(down_own, down_got),
    )


def solution(mesh):
    groups = mesh.shape["blk"] // 2
    fine = Mesh(mesh.devices.reshape(groups, 2, 2, mesh.shape["head"] // 2), ("z", "x", "y", "c"))
    blk, head = ("z", "x"), ("y", "c")
    every = blk + head
    rows = P(every, None)
    return jax.shard_map(
        shards,
        mesh=fine,
        in_specs=(
            rows,
            P(blk),
            rows,
            P(every),
            P(blk, head),
            P(every, None, None),
            P(blk, None, head),
            P(blk, head),
            rows,
            P(head),
            P(head),
            P(head),
            P(blk, head),
            P(blk, head),
            P(every),
            P(blk, None, head),
            P(blk, head),
        ),
        out_specs=(
            rows,
            rows,
            P(every),
            P(blk, head),
            P(every, None, None),
            P(blk, None, head),
            P(blk, head),
            rows,
            P(head),
            P(head),
            P(head),
            P(blk, head),
            P(blk, head),
            P(every),
            P(blk, None, head),
            P(blk, head),
        ),
        check_vma=False,
    )
```

```python
import functools
import math

import jax
import jax.numpy as jnp
from jax import lax
from jax.experimental import pallas as pl
from jax.experimental.pallas import tpu as pltpu
from jax.sharding import Mesh
from jax.sharding import PartitionSpec as P

QH = 8
KVH = 2
HD = 128
MP = 64
CHUNK = 256
KEYS = 512
EPS = 1e-05
THETA = 100000000000.0
NEGATIVE = -1e30
EXACT = lax.Precision.HIGHEST
F32 = jnp.float32
BF16 = jnp.bfloat16
VMEM_BYTES = 56 * 1024 * 1024
SWAP = [(0, 1), (1, 0)]


def mm(a, b, ca, cb, precision=None):
    return lax.dot_general(
        a, b, (((ca,), (cb,)), ((), ())), preferred_element_type=F32, precision=precision
    )


def scoped(function):
    def named(name, *args, **kwargs):
        with jax.named_scope(name):
            return function(*args, **kwargs)

    return named


def swap(a, axis):
    return lax.ppermute(a, axis, SWAP)


def after(value, *earlier):
    return lax.optimization_barrier((value,) + earlier)[0]


@scoped
def from_below(values):
    count = lax.axis_size("z")
    return [
        lax.ppermute(values[far], "z", [(i, i + far) for i in range(count - far)])
        for far in range(1, count)
    ]


@scoped
def from_above(values):
    count = lax.axis_size("z")
    return [
        lax.ppermute(values[far], "z", [(i + far, i) for i in range(count - far)])
        for far in range(1, count)
    ]


@scoped
def from_ring(value):
    count = lax.axis_size("z")
    return [
        lax.ppermute(value, "z", [(i, (i + far) % count) for i in range(count)])
        for far in range(1, count)
    ]


def spots(dx, dy, dc):
    x, y, c = (lax.axis_index(name) for name in "xyc")
    return ((x ^ dx) * 2 + (y ^ dy)) * 2 + (c ^ dc)


@scoped
def cube_gather(piece, split=0, gate=None, last_gate=None):
    by_x, by_y = swap(piece, "x"), swap(piece, "y")
    if gate is not None:
        by_x, by_y = after(by_x, gate), after(by_y, gate)
    low = swap(jnp.split(by_x, 2, split)[0], "y")
    high = swap(jnp.split(by_y, 2, split)[1], "x")
    if last_gate is not None:
        low, high = after(low, last_gate), after(high, last_gate)
    far = [low, high] if split == 0 else [jnp.concatenate([low, high], axis=split)]
    own = jnp.concatenate([piece, by_y, by_x] + far, axis=0)
    return own, swap(own, "c"), by_x, low


@scoped
def cube_scatter(mine, other=None, gate=None, far_gate=None):
    if other is not None:
        mine = mine + swap(other, "c")
    if gate is not None:
        mine = after(mine, gate)
    here, to_y, to_x, far = mine[0], mine[1], mine[2], mine[3]
    half = far.shape[0] // 2
    from_x, from_y = swap(far[:half], "x"), swap(far[half:], "y")
    x_low, y_high = swap(to_x[:half], "x"), swap(to_y[half:], "y")
    if far_gate is not None:
        to_x, to_y = after(to_x, far_gate), after(to_y, far_gate)
    last = to_x[half:] + from_y
    x_high = swap(last, "x")
    y_low = swap(to_y[:half] + from_x, "y")
    by_x = jnp.concatenate([x_low, x_high], 0).astype(F32)
    by_y = jnp.concatenate([y_low, y_high], 0).astype(F32)
    return here.astype(F32) + by_x + by_y, from_x, last


@scoped
def cube_scatter_direct(mine, other, gate):
    if other is not None:
        mine = mine + swap(other, "c")
    if gate is not None:
        mine = after(mine, gate)
    across = [(0, 3), (1, 2), (2, 1), (3, 0)]
    by_y, by_x = swap(mine[1], "y"), swap(mine[2], "x")
    by_both = lax.ppermute(mine[3], ("x", "y"), across)
    return mine[0], by_y, by_x, by_both


def place_ref():
    x, y, c = (lax.axis_index(name) for name in "xyc")
    return jnp.stack([x * 2 + y, c]).astype(jnp.int32)


def core_order(place, own, other):
    first = place[1] == 0
    return jnp.concatenate([jnp.where(first, own, other), jnp.where(first, other, own)], axis=0)


def core_split(place, values):
    half = values.shape[0] // 2
    first = place[1] == 0
    low, high = values[:half], values[half:]
    return jnp.where(first, low, high), jnp.where(first, high, low)


def near_spec(rows, cols):
    return pl.BlockSpec((rows, cols), lambda i, place: (i ^ place[0], 0))


def here_spec(rows, cols):
    return pl.BlockSpec((rows, cols), lambda i, place: (i, 0))


def settle_kernel(place, own_ref, other_ref, *out_refs):
    values = core_order(place, own_ref[...], other_ref[...])
    start = 0
    for out_ref in out_refs:
        out_ref[...] = values[:, start : start + out_ref.shape[1]]
        start += out_ref.shape[1]


def settle(own, other, rows, cuts):
    cols = own.shape[1]
    return call(
        settle_kernel,
        tuple(shape((8 * rows, n), own.dtype) for n in cuts),
        (4,),
        [near_spec(rows, cols)] * 2,
        tuple(here_spec(2 * rows, n) for n in cuts),
        prefetch=1,
    )(place_ref(), own, other)


def unsettle_kernel(place, *refs):
    values = jnp.concatenate([ref[...].astype(BF16) for ref in refs[:-2]], axis=1)
    refs[-2][...], refs[-1][...] = core_split(place, values)


def unsettle(parts, rows):
    cols = sum(a.shape[1] for a in parts)
    return call(
        unsettle_kernel,
        (shape((4 * rows, cols), BF16),) * 2,
        (4,),
        [near_spec(2 * rows, a.shape[1]) for a in parts],
        (here_spec(rows, cols),) * 2,
        prefetch=1,
    )(place_ref(), *parts)


def settle_groups_kernel(place, own_ref, other_ref, main_ref, misc_ref):
    groups, rows = own_ref.shape[1], own_ref.shape[2]
    first = place[1] == 0
    main = main_ref.shape[-1]
    for far in range(groups):
        own, other = own_ref[0, far], other_ref[0, far]
        at = lax.rem(place[2] - far + groups, groups)
        for core in range(2):
            values = jnp.where(first, own, other) if core == 0 else jnp.where(first, other, own)
            main_ref[pl.ds(at, 1), core] = values[None, :, :main]
            misc_ref[pl.ds(at, 1), core] = values[None, :, main:]


def settle_groups(own, other, main):
    _, groups, rows, cols = own.shape
    spec = pl.BlockSpec((1, groups, rows, cols), lambda i, place: (i ^ place[0], 0, 0, 0))
    outs = call(
        settle_groups_kernel,
        tuple(shape((groups, 8, rows, n), own.dtype) for n in (main, cols - main)),
        (4,),
        [spec, spec],
        tuple(
            pl.BlockSpec((groups, 2, rows, n), lambda i, place: (0, i, 0, 0))
            for n in (main, cols - main)
        ),
        prefetch=1,
    )(jnp.concatenate([place_ref(), lax.axis_index("z")[None]]), own, other)
    return tuple(out.reshape(groups * 8 * rows, -1) for out in outs)


def project_kernel(
    place, own_ref, other_ref, gain_ref, one_ref, two_ref, step_ref, cos_ref, sin_ref,
    normed_ref, q_ref, x_ref, kv_ref, bc_ref, dt_ref,
):
    rows = own_ref.shape[0] // 2
    flip = (place[0] & 1) == 1
    pieces = []
    own_low, own_high = own_ref[:rows], own_ref[rows:]
    other_low, other_high = other_ref[:rows], other_ref[rows:]
    pieces.append(
        core_order(
            place, jnp.where(flip, own_high, own_low), jnp.where(flip, other_high, other_low)
        )
    )
    pieces.append(
        core_order(
            place, jnp.where(flip, own_low, own_high), jnp.where(flip, other_low, other_high)
        )
    )
    values = jnp.concatenate(pieces, axis=0).astype(F32)
    scale = lax.rsqrt(jnp.mean(values * values, axis=1, keepdims=True) + EPS)
    normed = (values * scale * gain_ref[...]).astype(BF16)
    normed_ref[...] = normed
    cosine, sine = cos_ref[...], sin_ref[...]

    def turned(v):
        return (v * cosine + pltpu.roll(v, HD // 2, 1) * sine).astype(BF16)

    one = mm(normed, one_ref[...], 1, 0)
    q_ref[...] = turned(one[:, :HD])
    x_ref[...] = one[:, HD:].astype(BF16)
    at = pl.multiple_of(place[2] * HD, HD)
    lead = KVH * HD
    kv_w = jnp.concatenate([two_ref[:, pl.ds(at, HD)], two_ref[:, pl.ds(lead + at, HD)]], axis=1)
    kv = mm(normed, kv_w, 1, 0)
    kv_ref[:, :HD] = turned(kv[:, :HD])
    kv_ref[:, HD:] = kv[:, HD:].astype(BF16)
    bc_ref[...] = mm(normed, two_ref[:, 2 * lead :], 1, 0).astype(BF16)
    dt_ref[...] = mm(normed, step_ref[...], 1, 0).astype(BF16)


def project(kv_head, own, other, gain, w_one, w_two, w_dt, tables, rows):
    total = 8 * rows
    width = own.shape[1]
    cut = total // 2
    widths = (width, HD, w_one.shape[1] - HD, 2 * HD, w_two.shape[1] - 2 * KVH * HD, 128)
    near = pl.BlockSpec((2 * rows, width), lambda i, place: (i ^ (place[0] // 2), 0))

    def fixed(a):
        return pl.BlockSpec(a.shape, lambda i, place: (0, 0))

    return call(
        project_kernel,
        tuple(shape((total, n), BF16) for n in widths),
        (2,),
        [near, near, fixed(gain), fixed(w_one), fixed(w_two), fixed(w_dt)]
        + [here_spec(cut, HD)] * 2,
        tuple(here_spec(cut, n) for n in widths),
        prefetch=1,
    )(
        jnp.concatenate([place_ref(), kv_head[None].astype(jnp.int32)]),
        own, other, gain, w_one, w_two, w_dt, *tables,
    )


def grad_early_kernel(normed_ref, q_ref, z_ref, w_ref, out_ref, gain_ref):
    grad = jnp.concatenate([q_ref[...], z_ref[...]], axis=1)
    grad = mm(normed_ref[...], grad, 0, 0)
    out_ref[...] = grad.astype(BF16)
    q_cols, z_cols = q_ref.shape[1], z_ref.shape[1]
    w = jnp.concatenate([w_ref[:, :q_cols], w_ref[:, w_ref.shape[1] - z_cols :]], axis=1)
    gain = jnp.sum(grad * w.astype(F32), axis=1, keepdims=True)
    gain_ref[...] = jnp.broadcast_to(gain, gain_ref.shape)


def grad_early(groups, normed, q, z, w_all):
    total, width = normed.shape
    rows = width // groups

    def fixed(a):
        return pl.BlockSpec(a.shape, lambda i: (0, 0))

    def flow(cols):
        return pl.BlockSpec((rows, cols), lambda i: (i, 0))

    cols = q.shape[1] + z.shape[1]
    return call(
        grad_early_kernel,
        (shape((width, cols), BF16), shape((width, 128))),
        (groups,),
        [pl.BlockSpec((total, rows), lambda i: (0, i)), fixed(q), fixed(z), flow(w_all.shape[1])],
        (flow(cols), flow(128)),
    )(normed, q, z, w_all)


def grad_late_kernel(
    place, normed_ref, x_ref, kv_ref, bc_ref, dt_ref, w_ref, gain_ref, gain_two_ref,
    x_out_ref, own_ref, other_ref,
):
    rows = own_ref.shape[2]
    head = place[2]
    first = place[1] == 0
    normed = normed_ref[...]
    x_cols, bc_cols = x_ref.shape[1], bc_ref.shape[1]
    lead = 2 * KVH * HD
    start = w_ref.shape[1] - x_cols - 128 - bc_cols - lead
    grad_x = mm(normed, x_ref[...], 0, 0)
    x_out_ref[...] = grad_x.astype(BF16)
    gain = jnp.sum(grad_x * w_ref[:, start - x_cols : start].astype(F32), axis=1, keepdims=True)
    kv = mm(normed, kv_ref[...], 0, 0)
    zero = jnp.zeros((kv.shape[0], HD), F32)
    parts = []
    for part in (kv[:, :HD], kv[:, HD:]):
        parts += [jnp.where(head == i, part, zero) for i in range(KVH)]
    two = jnp.concatenate(parts + [mm(normed, bc_ref[...], 0, 0)], axis=1)
    wide = lead + bc_cols
    gain = gain + jnp.sum(two * w_ref[:, start : start + wide].astype(F32), axis=1, keepdims=True)
    dt = mm(normed, dt_ref[...], 0, 0) * w_ref[:, start + wide : start + wide + 128].astype(F32)
    gain = gain + jnp.sum(dt, axis=1, keepdims=True) + gain_ref[:, 0:1]
    lane = lax.broadcasted_iota(jnp.int32, (gain.shape[0], 128), 1)
    gains = jnp.where(lane == 0, gain, jnp.where(lane == 1, gain_two_ref[...], 0.0))
    grad = jnp.concatenate([two.astype(BF16), gains.astype(BF16)], axis=1)
    for spot in range(4):
        low = grad[2 * spot * rows : (2 * spot + 1) * rows]
        high = grad[(2 * spot + 1) * rows : (2 * spot + 2) * rows]
        at = pl.ds(spot ^ place[0], 1)
        own_ref[at, 0] = jnp.where(first, low, high)[None]
        other_ref[at, 0] = jnp.where(first, high, low)[None]


def grad_late(kv_head, groups, normed, x, kv, bc, dt, w_all, gain, gain_two):
    total, width = normed.shape
    block = width // groups
    rows = block // 8
    cols = 2 * KVH * HD + bc.shape[1] + 128

    def fixed(a):
        return pl.BlockSpec(a.shape, lambda i, place: (0, 0))

    def flow(n):
        return pl.BlockSpec((block, n), lambda i, place: (i, 0))

    return call(
        grad_late_kernel,
        (shape((width, x.shape[1]), BF16),) + (shape((4, groups, rows, cols), BF16),) * 2,
        (groups,),
        [pl.BlockSpec((total, block), lambda i, place: (0, i))]
        + [fixed(a) for a in (x, kv, bc, dt)]
        + [flow(w_all.shape[1]), flow(128), flow(1)],
        (flow(x.shape[1]),)
        + (pl.BlockSpec((4, 1, rows, cols), lambda i, place: (0, i, 0, 0)),) * 2,
        prefetch=1,
    )(
        jnp.concatenate([place_ref(), kv_head[None].astype(jnp.int32)]),
        normed, x, kv, bc, dt, w_all, gain, gain_two,
    )


def assemble_kernel(place, q_ref, x_ref, kv_ref, bc_ref, dt_ref, z_ref, own_ref, other_ref):
    head = place[2]
    zero = jnp.zeros((kv_ref.shape[0], HD), BF16)
    parts = []
    for part in (kv_ref[:, :HD], kv_ref[:, HD:]):
        parts += [jnp.where(head == i, part, zero) for i in range(KVH)]
    wide = jnp.concatenate(
        [q_ref[...], x_ref[...]] + parts + [bc_ref[...], dt_ref[...], z_ref[...]], axis=1
    )
    own_ref[...], other_ref[...] = core_split(place, wide)


def assemble(kv_head, rows, *parts):
    total = parts[0].shape[0]
    wide = sum(a.shape[1] for a in parts) + 2 * (KVH - 1) * HD
    return call(
        assemble_kernel,
        (shape((total // 2, wide), BF16),) * 2,
        (4,),
        [near_spec(2 * rows, a.shape[1]) for a in parts],
        (here_spec(rows, wide),) * 2,
        prefetch=1,
    )(jnp.concatenate([place_ref(), kv_head[None].astype(jnp.int32)]), *parts)


def halves(pack):
    x = lax.axis_index("x")
    own = lax.dynamic_index_in_dim(pack, x, 0, False)
    return own, lax.dynamic_index_in_dim(pack, x ^ 1, 0, False)


@scoped
def weight_gather(own, got):
    x = lax.axis_index("x")
    both = jnp.concatenate([jnp.where(x == 0, own, got), jnp.where(x == 0, got, own)], axis=0)
    return lax.all_gather(both, "z", axis=0, tiled=True)


def halves_in_order(own, got, axis):
    x = lax.axis_index("x")
    return jnp.concatenate([jnp.where(x == 0, own, got), jnp.where(x == 0, got, own)], axis=axis)


def both_halves(own, got):
    return halves_in_order(own, got, 1).astype(F32)


@scoped
def line_scatter(grad):
    return lax.psum_scatter(grad, "z", scatter_dimension=0, tiled=True)


@scoped
def own_and_got(part):
    x = lax.axis_index("x")
    part = part.reshape(2, -1, part.shape[1])
    got = swap(lax.dynamic_index_in_dim(part, x ^ 1, 0, False), "x")
    return lax.dynamic_index_in_dim(part, x, 0, False), got


def lanes_of(cols, heads):
    rows = cols.shape[0]
    low = lax.broadcasted_iota(jnp.int32, (rows, 2 * MP), 1) < MP
    return jnp.concatenate(
        [
            jnp.where(low, cols[:, 2 * j : 2 * j + 1], cols[:, 2 * j + 1 : 2 * j + 2])
            for j in range(heads // 2)
        ],
        axis=1,
    )


def head_sums(values):
    wide = values.shape[1]
    lane = lax.broadcasted_iota(jnp.int32, (wide, 128), 0) // MP
    pick = (lane == lax.broadcasted_iota(jnp.int32, (wide, 128), 1)).astype(F32)
    return mm(values, pick, 1, 0, EXACT)


def softplus(v):
    return jnp.maximum(v, 0.0) + jnp.log1p(jnp.exp(-jnp.abs(v)))


def sigmoid(v):
    return 1.0 / (1.0 + jnp.exp(-v))


def chunk_common(bc_ref, dt_in_ref, dt_row_ref, par_ref, par_col_ref, seg_col_ref, seg_row_ref, wide):
    heads = wide // MP
    states = bc_ref.shape[1] // 2
    b_val = bc_ref[:, :states]
    c_val = bc_ref[:, states:]
    raw = dt_in_ref[...].astype(F32) + par_ref[0:1, :]
    dt = softplus(raw)
    rate = par_ref[1:2, :]
    raw_row = dt_row_ref[...].astype(F32) + par_col_ref[:, 0:1]
    e_row = -softplus(raw_row) * par_col_ref[:, 1:2]
    first = lax.broadcasted_iota(jnp.int32, (CHUNK, CHUNK), 0)
    second = lax.broadcasted_iota(jnp.int32, (CHUNK, CHUNK), 1)
    lower = (first >= second).astype(F32)
    run = mm(lower, -dt * rate, 1, 0, EXACT)
    run_row = mm(e_row, lower, 1, 1, EXACT)
    bias = jnp.where((first >= second) & (seg_col_ref[...] == seg_row_ref[0]), 0.0, NEGATIVE)
    return heads, b_val, c_val, raw, dt, rate, run, run_row, bias, lower


def mamba_local_kernel(
    x_in_ref, bc_in_ref, dt_in_ref, dt_row_ref, par_ref, par_col_ref, skip_ref, seg_col_ref, seg_row_ref, marks_ref,
    y_ref, run_ref, held_ref, total_ref, starts_ref, state, base_run,
):
    step = pl.program_id(0)
    wide = skip_ref.shape[1]
    heads, b_val, c_val, raw, dt, rate, run, run_row, bias, _ = chunk_common(
        bc_in_ref, dt_in_ref, dt_row_ref, par_ref, par_col_ref, seg_col_ref, seg_row_ref, wide
    )

    @pl.when(step == 0)
    def _():
        state[...] = jnp.zeros_like(state)
        base_run[...] = jnp.zeros_like(base_run)

    x_val = x_in_ref[...].astype(F32)
    seg = seg_col_ref[...]
    label = marks_ref[step]
    final = marks_ref[step + 1]
    held = state[...]
    starts_ref[0] = held
    x_dt = x_val * lanes_of(dt, heads)
    x_dt_b = x_dt.astype(BF16)
    entry = jnp.where(seg == label, jnp.exp(run), 0.0)
    last = run[CHUNK - 1 : CHUNK, :]
    tail = jnp.where(seg == final, jnp.exp(last - run), 0.0)
    y_val = skip_ref[...] * x_val
    y_val = y_val + lanes_of(entry, heads) * mm(c_val, held.astype(BF16), 1, 0)
    gram = mm(c_val, b_val, 1, 1)
    low = lax.broadcasted_iota(jnp.int32, (CHUNK, 2 * MP), 1) < MP
    parts = []
    for pair in range(heads // 2):
        both = x_dt_b[:, pair * 2 * MP : (pair + 1) * 2 * MP]
        outs = []
        for h in (2 * pair, 2 * pair + 1):
            decay = jnp.exp(run[:, h : h + 1] - run_row[h : h + 1, :] + bias)
            outs.append(mm((decay * gram).astype(BF16), both, 1, 0))
        parts.append(jnp.where(low, outs[0], outs[1]))
    y_ref[...] = y_val + jnp.concatenate(parts, axis=1)
    fresh = mm(b_val, (x_dt * lanes_of(tail, heads)).astype(BF16), 0, 0)
    kept = jnp.where(label == final, jnp.exp(last), 0.0)
    new = lanes_of(jnp.broadcast_to(kept, (8, 128)), heads)[0:1] * held + fresh
    state[...] = new
    held_ref[...] = new
    run_all = run + base_run[0:1, :]
    run_ref[...] = run_all
    base_run[...] = jnp.broadcast_to(run_all[CHUNK - 1 : CHUNK, :], base_run.shape)
    total_ref[...] = jnp.exp(base_run[...])


def mamba_close_kernel(bc_in_ref, gate_ref, y_ref, run_ref, seg_col_ref, held_ref, marks_ref, out_ref, full_ref):
    wide = y_ref.shape[1]
    heads = wide // MP
    states = held_ref.shape[0]
    c_val = bc_in_ref[:, states:]
    entry = jnp.where(seg_col_ref[...] == marks_ref[0], jnp.exp(run_ref[...]), 0.0)
    y_val = y_ref[...] + lanes_of(entry, heads) * mm(c_val, held_ref[...].astype(BF16), 1, 0)
    full_ref[...] = y_val
    z_val = gate_ref[...].astype(F32)
    out_ref[...] = (y_val * z_val * sigmoid(z_val)).astype(BF16)


def mamba_grad_state_kernel(
    bc_in_ref, gate_ref, y_ref, grad_ref, run_ref, seg_col_ref, marks_ref, out_ref, gate_grad_ref
):
    wide = grad_ref.shape[1]
    heads = wide // MP
    states = out_ref.shape[0]
    c_val = bc_in_ref[:, states:]
    z_val = gate_ref[...].astype(F32)
    entry = jnp.where(seg_col_ref[...] == marks_ref[0], jnp.exp(run_ref[...]), 0.0)
    grad = grad_ref[...].astype(F32)
    sig = sigmoid(z_val)
    grad_y = grad * z_val * sig
    gate_grad_ref[...] = (grad * y_ref[...] * (sig * (1.0 + z_val * (1.0 - sig)))).astype(BF16)

    @pl.when(pl.program_id(0) == 0)
    def _():
        out_ref[...] = jnp.zeros_like(out_ref)

    out_ref[...] += mm(c_val, (grad_y * lanes_of(entry, heads)).astype(BF16), 0, 0)


def mamba_grad_near_kernel(
    x_in_ref, bc_in_ref, dt_in_ref, dt_row_ref, par_ref, par_col_ref, skip_ref, seg_col_ref, seg_row_ref, marks_ref,
    gate_ref, run_ref, starts_ref, held_ref, grad_ref,
    x_grad_ref, b_ref, c_ref, e_ref, carry_ref, skip_sum_ref,
):
    step = pl.program_id(0)
    wide = skip_ref.shape[1]
    heads, b_val, c_val, raw, dt, rate, run, run_row, bias, lower = chunk_common(
        bc_in_ref, dt_in_ref, dt_row_ref, par_ref, par_col_ref, seg_col_ref, seg_row_ref, wide
    )

    @pl.when(step == 0)
    def _():
        skip_sum_ref[...] = jnp.zeros_like(skip_sum_ref)

    z_val = gate_ref[...].astype(F32)
    x_val = x_in_ref[...].astype(F32)
    label = marks_ref[step]
    before = run_ref[0:1, :] - run[0:1, :]
    carry = jnp.where(label == marks_ref[0], jnp.exp(before), 0.0)
    held = starts_ref[0] + lanes_of(jnp.broadcast_to(carry, (8, 128)), heads)[0:1] * held_ref[...]
    held_b = held.astype(BF16)
    grad_y = grad_ref[...].astype(F32) * z_val * sigmoid(z_val)
    dt_wide = lanes_of(dt, heads)
    x_dt_b = (x_val * dt_wide).astype(BF16)
    entry = lanes_of(jnp.where(seg_col_ref[...] == label, jnp.exp(run), 0.0), heads)
    grad_in = (entry * grad_y).astype(BF16)
    run_grad = head_sums(grad_y * entry * mm(c_val, held_b, 1, 0))
    grad_c = mm(grad_in, held_b, 1, 1)
    carry_ref[0] = mm(c_val, grad_in, 0, 0)
    gram = mm(c_val, b_val, 1, 1)
    low = lax.broadcasted_iota(jnp.int32, (CHUNK, 2 * MP), 1) < MP
    lane = lax.broadcasted_iota(jnp.int32, (CHUNK, 128), 1)
    grad_y_b = grad_y.astype(BF16)
    none = jnp.zeros((CHUNK, 2 * MP), BF16)
    gram_grad = None
    parts, cols = [], []
    for pair in range(heads // 2):
        span = slice(pair * 2 * MP, (pair + 1) * 2 * MP)
        outs = []
        for h in (2 * pair, 2 * pair + 1):
            mask = low if h % 2 == 0 else ~low
            decay = jnp.exp(run[:, h : h + 1] - run_row[h : h + 1, :] + bias)
            mixing = (decay * gram).astype(BF16)
            outs.append(mm(mixing, grad_y_b[:, span], 0, 0))
            mixing_grad = mm(jnp.where(mask, grad_y_b[:, span], none), x_dt_b[:, span], 1, 1)
            weighted = mixing_grad * decay
            gram_grad = weighted if gram_grad is None else gram_grad + weighted
            weighted = weighted * gram
            run_grad = run_grad + jnp.where(
                lane == h, jnp.sum(weighted, axis=1, keepdims=True), 0.0
            )
            cols.append(jnp.sum(weighted, axis=0, keepdims=True))
        parts.append(jnp.where(low, outs[0], outs[1]))
    gram_grad_b = gram_grad.astype(BF16)
    c_ref[...] = (grad_c + mm(gram_grad_b, b_val, 1, 0)).astype(BF16)
    b_ref[...] = mm(gram_grad_b, c_val, 0, 0)
    x_grad_ref[...] = jnp.concatenate(parts, axis=1)
    col_grad = jnp.concatenate(cols + [jnp.zeros((128 - heads, CHUNK), F32)], axis=0)
    e_ref[...] = mm(lower, run_grad, 0, 0, EXACT) - mm(lower, col_grad, 0, 1, EXACT)
    skip_sum_ref[0:1, :] += jnp.sum(grad_y * x_val, axis=0, keepdims=True)


def mamba_grad_kernel(
    x_in_ref, bc_in_ref, dt_in_ref, dt_row_ref, par_ref, par_col_ref, skip_ref, seg_col_ref, seg_row_ref, marks_ref,
    gate_ref, run_ref, starts_ref, held_ref, grad_ref,
    x_grad_ref, b_grad_ref, c_grad_ref, e_grad_ref, carry_ref, deep_ref,
    x_ref, bc_ref, dt_ref, sums_ref, deep,
):
    step = pl.num_programs(0) - 1 - pl.program_id(0)
    wide = skip_ref.shape[1]
    heads = wide // MP
    states = b_grad_ref.shape[1]
    b_val = bc_in_ref[:, :states]
    raw = dt_in_ref[...].astype(F32) + par_ref[0:1, :]
    dt = softplus(raw)
    rate = par_ref[1:2, :]
    first = lax.broadcasted_iota(jnp.int32, (CHUNK, CHUNK), 0)
    second = lax.broadcasted_iota(jnp.int32, (CHUNK, CHUNK), 1)
    lower = (first >= second).astype(F32)
    run = run_ref[...]

    @pl.when(pl.program_id(0) == 0)
    def _():
        deep[...] = deep_ref[...]
        sums_ref[...] = jnp.zeros_like(sums_ref)

    z_val = gate_ref[...].astype(F32)
    x_val = x_in_ref[...].astype(F32)
    seg = seg_col_ref[...]
    label = marks_ref[step]
    final = marks_ref[step + 1]
    last = run[CHUNK - 1 : CHUNK, :]
    e_first = -dt[0:1, :] * rate
    before = run[0:1, :] - e_first
    carry = jnp.where(label == marks_ref[0], jnp.exp(before), 0.0)
    held = starts_ref[0] + lanes_of(jnp.broadcast_to(carry, (8, 128)), heads)[0:1] * held_ref[...]
    after_b = deep[...].astype(BF16)
    grad_y = grad_ref[...].astype(F32) * z_val * sigmoid(z_val)
    dt_wide = lanes_of(dt, heads)
    tail = lanes_of(jnp.where(seg == final, jnp.exp(last - run), 0.0), heads)
    x_tail = x_val * dt_wide * tail
    back = mm(b_val, after_b, 1, 0)
    bc_ref[:, :states] = (b_grad_ref[...] + mm(x_tail.astype(BF16), after_b, 1, 1)).astype(BF16)
    bc_ref[:, states:] = c_grad_ref[...]
    tail_grad = head_sums(x_tail * back)
    kept = jnp.where(label == final, jnp.exp(last - before), 0.0)
    kept_wide = lanes_of(jnp.broadcast_to(kept, (8, 128)), heads)[0:1]
    kept_grad = head_sums(
        jnp.broadcast_to(kept_wide * jnp.sum(deep[...] * held, axis=0, keepdims=True), (8, wide))
    )
    last_grad = jnp.sum(tail_grad, axis=0, keepdims=True) + kept_grad[0:1]
    deep[...] = kept_wide * deep[...] + carry_ref[0]
    x_dt_grad = x_grad_ref[...] + tail * back
    x_ref[...] = (x_dt_grad * dt_wide + skip_ref[...] * grad_y).astype(BF16)
    e_grad = e_grad_ref[...] - mm(lower, tail_grad, 0, 0, EXACT) + last_grad
    dt_grad = head_sums(x_dt_grad * x_val) - rate * e_grad
    raw_grad = dt_grad * sigmoid(raw)
    lane = lax.broadcasted_iota(jnp.int32, (CHUNK, 128), 1)
    dt_ref[...] = jnp.where(lane < heads, raw_grad, 0.0).astype(BF16)
    sums_ref[0:1, :] += jnp.sum(-rate * dt * e_grad, axis=0, keepdims=True)
    sums_ref[1:2, :] += jnp.sum(raw_grad, axis=0, keepdims=True)


def seen(kseg_ref, qseg, first_query, block):
    rows = qseg.shape[0]
    key_pos = block * KEYS + lax.broadcasted_iota(jnp.int32, (rows, KEYS), 1)
    query_pos = first_query + lax.broadcasted_iota(jnp.int32, (rows, KEYS), 0)
    return (key_pos <= query_pos) & (kseg_ref[pl.ds(block, 1), :] == qseg)


def key_span(block, where_ref, groups):
    far = where_ref[0] - block // 2
    at = jnp.where((block & 1) == where_ref[1], far, groups + far)
    return pl.ds(pl.multiple_of(at * KEYS, KEYS), KEYS)


def attend_kernel(low_ref, high_ref, start_ref, where_ref, q_ref, kv_ref, kseg_ref, qseg_ref, att_ref, log_ref):
    step = pl.program_id(0)
    rows = q_ref.shape[0]
    query = q_ref[...]
    qseg = qseg_ref[...]
    first_query = start_ref[0] + step * rows
    scale = HD**-0.5

    def visit(block, state):
        peak, total, acc = state
        span = key_span(block, where_ref, kv_ref.shape[0] // (2 * KEYS))
        scores = mm(query, kv_ref[span, :HD], 1, 1) * scale
        scores = jnp.where(seen(kseg_ref, qseg, first_query, block), scores, NEGATIVE)
        new_peak = jnp.maximum(peak, jnp.max(scores, axis=1, keepdims=True))
        weights = jnp.exp(scores - new_peak)
        rescale = jnp.exp(peak - new_peak)
        total = total * rescale + jnp.sum(weights, axis=1, keepdims=True)
        acc = acc * rescale + mm(weights.astype(BF16), kv_ref[span, HD:], 1, 0)
        return new_peak, total, acc

    peak, total, acc = lax.fori_loop(
        low_ref[step],
        high_ref[step],
        visit,
        (
            jnp.full((rows, 1), NEGATIVE, F32),
            jnp.zeros((rows, 1), F32),
            jnp.zeros((rows, HD), F32),
        ),
    )
    att_ref[...] = acc / total
    log_ref[...] = jnp.broadcast_to(peak + jnp.log(total), log_ref.shape)


def attend_grad_kernel(
    low_ref, high_ref, start_ref, where_ref, q_ref, kv_ref, kseg_ref, qseg_ref, att_ref, log_ref,
    grad_ref, dq_ref, dkv_ref, sums,
):
    step = pl.program_id(0)
    rows = q_ref.shape[0]
    query = q_ref[...]
    grad = grad_ref[...]
    qseg = qseg_ref[...]
    log_total = log_ref[:, 0:1]
    first_query = start_ref[0] + step * rows
    scale = HD**-0.5
    delta = jnp.sum(grad.astype(F32) * att_ref[...], axis=1, keepdims=True)

    @pl.when(step == 0)
    def _():
        sums[...] = jnp.zeros_like(sums)

    def visit(block, acc):
        span = key_span(block, where_ref, kv_ref.shape[0] // (2 * KEYS))
        keys = kv_ref[span, :HD]
        scores = mm(query, keys, 1, 1) * scale - log_total
        scores = jnp.where(seen(kseg_ref, qseg, first_query, block), scores, NEGATIVE)
        probs = jnp.exp(scores)
        probs_grad = mm(grad, kv_ref[span, HD:], 1, 1)
        scores_grad = (probs * (probs_grad - delta)).astype(BF16)
        sums[span, :HD] += mm(scores_grad, query, 0, 0)
        sums[span, HD:] += mm(probs.astype(BF16), grad, 0, 0)
        return acc + mm(scores_grad, keys, 1, 0)

    acc = lax.fori_loop(low_ref[step], high_ref[step], visit, jnp.zeros((rows, HD), F32))
    dq_ref[...] = acc * scale

    @pl.when(step == pl.num_programs(0) - 1)
    def _():
        dkv_ref[:, :HD] = (sums[:, :HD] * scale).astype(BF16)
        dkv_ref[:, HD:] = sums[:, HD:].astype(BF16)


def call(kernel, out_shape, grid, in_specs, out_specs, scratch=(), prefetch=0, cost=None):
    return pl.pallas_call(
        kernel,
        out_shape=out_shape,
        grid_spec=pltpu.PrefetchScalarGridSpec(
            num_scalar_prefetch=prefetch,
            grid=grid,
            in_specs=in_specs,
            out_specs=out_specs,
            scratch_shapes=list(scratch),
        ),
        compiler_params=pltpu.CompilerParams(
            vmem_limit_bytes=VMEM_BYTES, dimension_semantics=("arbitrary",) * len(grid)
        ),
        cost_estimate=cost,
        name=kernel.__name__,
    )


def shape(dims, dtype=F32):
    return jax.ShapeDtypeStruct(dims, dtype)


def rope_tables(positions):
    half = HD // 2
    frequency = jnp.exp(jnp.arange(half, dtype=F32) * (-2.0 * math.log(THETA) / HD))
    angle = positions.astype(F32)[:, None] * frequency[None, :]
    cosine, sine = jnp.cos(angle), jnp.sin(angle)
    return jnp.concatenate([cosine, cosine], 1), jnp.concatenate([-sine, sine], 1)


def rope(values, tables):
    cosine, sine = tables
    return values * cosine + jnp.concatenate([values[:, HD // 2 :], values[:, : HD // 2]], 1) * sine


def rope_back(values, tables):
    cosine, sine = tables
    return values * cosine - jnp.concatenate([values[:, HD // 2 :], values[:, : HD // 2]], 1) * sine


def unit(values):
    return values * lax.rsqrt(jnp.mean(values * values, axis=-1, keepdims=True) + EPS)


def norm_back(values, gain, grad):
    scale = lax.rsqrt(jnp.mean(values * values, axis=-1, keepdims=True) + EPS)
    u = values * scale
    inner = jnp.mean(grad * gain * u, axis=-1, keepdims=True)
    return scale * (grad * gain - u * inner), jnp.sum(grad * u, axis=0)


def shards(
    tokens, seg_ids, cotangent, gain_mix, q_w, kv_w, zx_w, dt_w, bc_w,
    a_log, dt_bias, skip, wo_w, wm_w, gain_ff, gu_w, down_w,
):
    groups = lax.axis_size("z")
    z, x, y, c = (lax.axis_index(name) for name in "zxyc")
    own_rows, width = tokens.shape
    group = 8 * own_rows
    rows_w = q_w.shape[0]
    part = kv_w.shape[0]
    ratio = rows_w // part
    heads = dt_w.shape[1] // 2
    wide = heads * MP
    states = bc_w.shape[1] // 2
    ff = gu_w.shape[2] // 2
    inner = q_w.shape[1] // 2
    steps = group // CHUNK

    zx_cut = zx_w.reshape(rows_w, 2, 2, wide).transpose(1, 2, 0, 3)
    pack_z = zx_cut[0]
    pack_one = jnp.concatenate([q_w.reshape(rows_w, 2, inner).transpose(1, 0, 2), zx_cut[1]], axis=2)
    pack_out = jnp.concatenate(
        [
            wo_w.reshape(rows_w, 2, inner).transpose(1, 0, 2),
            wm_w.reshape(rows_w, 2, wide).transpose(1, 0, 2),
        ],
        axis=2,
    )
    pack_gu = gu_w.reshape(rows_w, 2, 2, ff).transpose(2, 0, 1, 3).reshape(2, rows_w, 2 * ff)
    pack_down = down_w.reshape(rows_w, 2, ff).transpose(1, 0, 2)
    kv_cols = kv_w.shape[1] * kv_w.shape[2]
    bc_cols = bc_w.shape[1]
    lead = kv_cols + bc_cols
    dt_cols = dt_w.shape[1]
    dt_part = dt_w.reshape(ratio, part, dt_cols).transpose(1, 0, 2).reshape(part, ratio * dt_cols)
    pack_two = jnp.concatenate(
        [kv_w.reshape(part, kv_cols), bc_w, gain_mix[:, None], gain_ff[:, None], dt_part], axis=1
    )
    used = pack_two.shape[1]
    total_cols = -(-used // 128) * 128
    pack_two = jnp.pad(pack_two, ((0, 0), (0, total_cols - used)))

    def put_two(out, at, number, value):
        return lax.dynamic_update_slice(out, value[None], (at, 0, 0))

    own_one, give_one = halves(pack_one)
    own_out, give_out = halves(jnp.concatenate([pack_out, pack_z], axis=2))
    own_ff, give_ff = halves(jnp.concatenate([pack_gu, pack_down], axis=2))
    two_far = from_ring("whole_rows", pack_two)
    seg_pair = jnp.zeros((2, seg_ids.shape[0]), jnp.int32)
    seg_pair = lax.dynamic_update_index_in_dim(seg_pair, seg_ids, x, 0)
    seg_pair = lax.dynamic_update_index_in_dim(seg_pair, swap(seg_ids, "x"), x ^ 1, 0)
    seg_own = seg_pair.reshape(1, group)
    seg_far = from_ring("ids", seg_own)
    two = jnp.stack([pack_two] + two_far)[None]
    got_one = swap(give_one, "x")
    own_one, got_one, two, *seg_far = lax.optimization_barrier((own_one, got_one, two, *seg_far))
    seg_all = jnp.zeros((groups, group), jnp.int32)
    for far, got in enumerate([seg_own, *seg_far]):
        seg_all = lax.dynamic_update_slice(seg_all, got, ((z - far + groups) % groups, 0))
    w_one = weight_gather("w_one", own_one, got_one)
    two_own, two_other, _, two_low = cube_gather("whole_rows", two, 1)
    rows_own, rows_other, *_ = cube_gather("tokens", after(tokens, two_low))
    w_two, misc = settle_groups(two_own, two_other, lead)
    w_mix = weight_gather("w_mix", own_out, swap(after(give_out, rows_own), "x"))
    w_out, w_z = w_mix[:, : inner + wide], w_mix[:, inner + wide :]
    segment = seg_own.astype(F32)
    seg_col = segment.reshape(group, 1)
    seg_row = segment.reshape(steps, 1, CHUNK)
    previous = lax.dynamic_index_in_dim(seg_all, jnp.maximum(z - 1, 0), 0, False)[group - 1]
    in_label = jnp.where(z > 0, previous, -1).astype(F32)
    marks = jnp.concatenate([in_label[None], segment[0, CHUNK - 1 :: CHUNK]])

    gain_one = misc[:, 0].astype(F32)
    gain_two = misc[:, 1].astype(F32)
    dt_all = misc[:, 2 : 2 + ratio * dt_cols].reshape(
        groups, 2, 4, part, ratio, 2, heads
    )
    dt_own = lax.dynamic_index_in_dim(dt_all, y * 2 + c, 2, False)
    dt_own = lax.dynamic_index_in_dim(dt_own, x, 4, False)
    w_dt = dt_own.transpose(0, 1, 3, 2, 4).reshape(width, heads)
    kv_head = ((y * 2 + c) * 2 + x) * (inner // HD) // (QH // KVH)
    w_dt = jnp.pad(w_dt, ((0, 0), (0, 128 - heads)))

    positions = z * group + jnp.arange(group, dtype=jnp.int32)
    tables = rope_tables(positions)
    normed, query, x_in, kv_own, bc_in, dt_in = project(
        kv_head, rows_own, rows_other, gain_one[None, :], w_one, w_two, w_dt, tables, own_rows
    )
    half, quarter = group // 2, group // 4
    kv_half = lax.dynamic_slice_in_dim(kv_own, c * half, half, 0)
    kv_quarter = lax.dynamic_slice_in_dim(kv_own, c * half + x * quarter, quarter, 0)
    kv_far = from_below("kv", [kv_quarter] * groups)
    gate_in = mm(normed, w_z, 1, 0).astype(BF16)

    dt_row = jnp.pad(dt_in[:, :8].T, ((0, 8), (0, 0)))
    pad = ((0, 128 - heads),)

    def pick(values):
        return lax.dynamic_slice_in_dim(values, x * heads, heads, 0)

    rates = jnp.exp(pick(a_log))
    params = jnp.stack([jnp.pad(pick(dt_bias), pad), jnp.pad(rates, pad)])
    params = jnp.pad(params, ((0, 6), (0, 0)))
    params_col = jnp.pad(
        jnp.stack([pick(dt_bias), rates], axis=1), ((0, 16 - heads), (0, 126))
    )
    skip_wide = jnp.repeat(pick(skip), MP)[None, :]

    def flow(cols, back=False):
        at = (lambda i: (steps - 1 - i, 0)) if back else (lambda i: (i, 0))
        return pl.BlockSpec((CHUNK, cols), at)

    def chunk_specs(back=False):
        def turn(i):
            return steps - 1 - i if back else i

        return [
            flow(wide, back),
            flow(2 * states, back),
            flow(128, back),
            pl.BlockSpec((16, CHUNK), lambda i: (0, turn(i))),
            pl.BlockSpec((8, 128), lambda i: (0, 0)),
            pl.BlockSpec((16, 128), lambda i: (0, 0)),
            pl.BlockSpec((1, wide), lambda i: (0, 0)),
            flow(1, back),
            pl.BlockSpec((1, 1, CHUNK), lambda i: (turn(i), 0, 0)),
            pl.BlockSpec(memory_space=pltpu.SMEM),
        ]

    whole = pl.BlockSpec((states, wide), lambda i: (0, 0))
    smem = pl.BlockSpec(memory_space=pltpu.SMEM)
    chunk_args = (x_in, bc_in, dt_in, dt_row, params, params_col, skip_wide, seg_col, seg_row, marks)
    y_local, run, held_own, total, starts = call(
        mamba_local_kernel,
        (
            shape((group, wide)),
            shape((group, 128)),
            shape((states, wide)),
            shape((8, 128)),
            shape((steps, states, wide)),
        ),
        (steps,),
        chunk_specs(),
        (
            flow(wide),
            flow(128),
            whole,
            pl.BlockSpec((8, 128), lambda i: (0, 0)),
            pl.BlockSpec((1, states, wide), lambda i: (i, 0, 0)),
        ),
        [pltpu.VMEM((states, wide), F32), pltpu.VMEM((8, 128), F32)],
    )(*chunk_args)
    joined = jnp.where(in_label == segment[0, group - 1], 1.0, 0.0)
    factor = jnp.repeat(total[0, :heads] * joined, MP)[None, :]
    factor_rows = jnp.broadcast_to(factor, (16, wide))
    held_sent = jnp.concatenate([held_own, factor_rows], axis=0).astype(BF16)
    held_sent, *kv_far = lax.optimization_barrier((held_sent, *kv_far))
    w_ff = weight_gather("w_ff", own_ff, swap(after(give_ff, held_sent), "x"))
    w_gu, w_down = w_ff[:, : 2 * ff], w_ff[:, 2 * ff :]
    held_far = from_below("held", [held_sent] * groups)
    kv_far = jnp.stack(kv_far)
    kv_far = halves_in_order(kv_far, swap(kv_far, "x"), 1).reshape(-1, 2 * HD)
    kv_near = jnp.concatenate([kv_half, kv_far], axis=0)
    kv_near, *held_far = lax.optimization_barrier((kv_near, *held_far))
    kv_all = jnp.concatenate([kv_near, swap(kv_near, "c")], axis=0)
    w_all = jnp.concatenate([w_one, w_two, w_dt, w_z], axis=1)
    query, w_all = lax.optimization_barrier((query, w_all))
    in_held = jnp.zeros((states, wide), F32)
    for got in reversed(held_far):
        got = got.astype(F32)
        in_held = got[:states] + got[states : states + 1] * in_held

    q_rows = CHUNK
    blocks = group // q_rows
    first_rows = z * group + q_rows * jnp.arange(blocks, dtype=jnp.int32)
    first_seg = seg_own[0, ::q_rows]
    reached = jnp.arange(groups * group, dtype=jnp.int32)[None, :] < (z + 1) * group
    earlier = (seg_all.reshape(1, -1) < first_seg[:, None]) & reached
    low = jnp.sum(earlier, axis=1, dtype=jnp.int32) // KEYS
    high = (first_rows + q_rows - 1) // KEYS + 1
    start = (z * group)[None].astype(jnp.int32)
    where = jnp.stack([z, c]).astype(jnp.int32)
    key_seg = seg_all.astype(F32).reshape(groups * group // KEYS, KEYS)

    def rows_spec(cols):
        return pl.BlockSpec((q_rows, cols), lambda i, *_: (i, 0))

    def full_spec(a):
        return pl.BlockSpec(a.shape, lambda i, *_: (0, 0))

    att_full, log_total = call(
        attend_kernel,
        (shape((group, HD)), shape((group, 128))),
        (blocks,),
        [rows_spec(HD), full_spec(kv_all), full_spec(key_seg), rows_spec(1)],
        (rows_spec(HD), rows_spec(128)),
        prefetch=4,
    )(low, high, start, where, query, kv_all, key_seg, seg_col)

    ssm_out, y_full = call(
        mamba_close_kernel,
        (shape((group, wide), BF16), shape((group, wide))),
        (steps,),
        [flow(2 * states), flow(wide), flow(wide), flow(128), flow(1), whole, smem],
        (flow(wide), flow(wide)),
    )(bc_in, gate_in, y_local, run, seg_col, after(in_held, att_full), marks)

    def row_term(a, w):
        return mm(a, w, 1, 1).astype(BF16).reshape(4, own_rows, width)

    def weight_grad(pairs):
        total = None
        for a, g in pairs:
            value = mm(a, g, 0, 0)
            total = value if total is None else total + value
        return total.astype(BF16)

    stream_own = tokens.astype(F32)
    mixer_own, mixer_other = unsettle([att_full, ssm_out], own_rows)
    term_other = row_term(mixer_other, w_out)
    middle = stream_own + cube_scatter("mixed", row_term(mixer_own, w_out), term_other)[0]
    normed_two = (unit(middle) * gain_two).astype(BF16)
    two_rows = cube_gather("normed_two", normed_two)[:2]
    cot_own, cot_other, *_ = cube_gather("cotangent", after(cotangent, two_rows[0]))

    def forward(rows):
        gate_up = mm(rows, w_gu, 1, 0).astype(BF16)
        gate = gate_up[:, :ff].astype(F32)
        up = gate_up[:, ff:].astype(F32)
        sig = jax.nn.sigmoid(gate)
        return gate, up, sig, (gate * sig * up).astype(BF16)

    def backward(rows, gate, up, sig):
        grad_hidden = mm(rows, w_down, 1, 0).astype(BF16).astype(F32)
        grad_gate = grad_hidden * up * (sig * (1.0 + gate * (1.0 - sig)))
        return jnp.concatenate([grad_gate, grad_hidden * gate * sig], axis=1).astype(BF16)

    *kept_own, hidden_own = forward(two_rows[0])
    *kept_other, hidden_other = forward(two_rows[1])
    gu_other = backward(cot_other, *kept_other)
    gu_own = backward(cot_own, *kept_own)
    term_other = row_term(gu_other, w_gu)
    down_w = weight_grad(
        [(after(cot_own, term_other), hidden_own), (after(cot_other, term_other), hidden_other)]
    )
    down_part = line_scatter("down", down_w)
    term, down_w = lax.optimization_barrier((row_term(gu_own, w_gu), down_w))
    grad_normed_two, far, _ = cube_scatter("grad_normed_two", term, term_other)
    gu_w = weight_grad([(after(two_rows[0], far), gu_own), (after(two_rows[1], far), gu_other)])
    middle_part, gain_two_part = norm_back(middle, gain_two, grad_normed_two)
    grad_middle = cotangent.astype(F32) + middle_part
    grad_middle, gu_w = lax.optimization_barrier((grad_middle, gu_w))
    hidden_own, hidden_other = after(hidden_own, grad_middle), after(hidden_other, grad_middle)
    layer_other = row_term(hidden_other, w_down)
    layer_own = row_term(hidden_own, w_down)
    mixed_own, mixed_other, *_ = cube_gather(
        "grad_middle", grad_middle.astype(BF16), gate=layer_other, last_gate=layer_own
    )
    layer_terms = cube_scatter_direct("layer_out", layer_own, layer_other, mixed_own)
    layer_out = middle + sum(a.astype(F32) for a in layer_terms)
    layer_out = layer_out.astype(BF16)
    gu_part = line_scatter("gu", gu_w)
    grad_att, grad_ssm = settle(
        mm(mixed_own, w_out, 1, 0).astype(BF16),
        mm(mixed_other, w_out, 1, 0).astype(BF16),
        own_rows,
        (inner, wide),
    )

    grad_att, down_part = lax.optimization_barrier((grad_att, down_part))
    grad_query, grad_kv_all = call(
        attend_grad_kernel,
        (shape((group, HD)), shape((groups * group, 2 * HD), BF16)),
        (blocks,),
        [
            rows_spec(HD), full_spec(kv_all), full_spec(key_seg), rows_spec(1),
            rows_spec(HD), rows_spec(128), rows_spec(HD),
        ],
        (rows_spec(HD), full_spec(kv_all)),
        [pltpu.VMEM((groups * group, 2 * HD), F32)],
        prefetch=4,
    )(low, high, start, where, query, kv_all, key_seg, seg_col, att_full, log_total, grad_att)
    grad_ssm = after(grad_ssm, grad_query, layer_out)
    state_grad, grad_z = call(
        mamba_grad_state_kernel,
        (shape((states, wide)), shape((group, wide), BF16)),
        (steps,),
        [flow(2 * states), flow(wide), flow(wide), flow(wide), flow(128), flow(1), smem],
        (whole, flow(wide)),
    )(bc_in, gate_in, y_full, grad_ssm, run, seg_col, marks)
    grad_sent = jnp.concatenate([state_grad, factor_rows], axis=0).astype(BF16)
    held_far = from_above("grad_held", [grad_sent] * groups)
    grad_q = rope_back(grad_query, tables).astype(BF16)
    chunk_more = (gate_in, run, starts, in_held, after(grad_ssm, grad_sent))

    def more_specs(back=False):
        return [
            flow(wide, back),
            flow(128, back),
            pl.BlockSpec((1, states, wide), lambda i: (steps - 1 - i if back else i, 0, 0)),
            whole,
            flow(wide, back),
        ]

    near_out = call(
        mamba_grad_near_kernel,
        (
            shape((group, wide)),
            shape((group, states)),
            shape((group, states), BF16),
            shape((group, 128)),
            shape((steps, states, wide)),
            shape((8, wide)),
        ),
        (steps,),
        chunk_specs() + more_specs(),
        (
            flow(wide),
            flow(states),
            flow(states),
            flow(128),
            pl.BlockSpec((1, states, wide), lambda i: (i, 0, 0)),
            pl.BlockSpec((8, wide), lambda i: (0, 0)),
        ),
    )(*chunk_args, *chunk_more)
    kv_terms = grad_kv_all.reshape(2, groups, half, 2 * HD)
    kv_mine, *held_far = lax.optimization_barrier(
        (after(kv_terms[0], near_out[0]), *held_far)
    )
    kv_both = kv_mine + swap(kv_terms[1], "c")
    kv_terms = kv_both.reshape(groups, 2, quarter, 2 * HD)
    kv_terms = lax.dynamic_index_in_dim(kv_terms, x, 1, False) + swap(
        lax.dynamic_index_in_dim(kv_terms, x ^ 1, 1, False), "x"
    )
    kv_far = from_above("grad_kv", kv_terms)
    skip_sums = near_out[5]
    down_own, down_got = own_and_got("down", after(down_part, kv_terms))
    grad_q, gu_part, *kv_far = lax.optimization_barrier((grad_q, gu_part, *kv_far))
    qz_w, gain_early = grad_early(groups, normed, grad_q, grad_z, w_all)
    qz_part = line_scatter("qz", qz_w)
    out_w = weight_grad([(after(mixed_own, kv_both), mixer_own), (mixed_other, mixer_other)])
    out_part = line_scatter("out", out_w)
    deep = jnp.zeros((states, wide), F32)
    for got in reversed(held_far):
        got = got.astype(F32)
        deep = got[:states] + got[states : states + 1] * deep
    grad_kv_part = kv_terms[0].astype(F32)
    for got in kv_far:
        grad_kv_part = grad_kv_part + got.astype(F32)
    deep = after(deep, grad_kv_part, qz_w, down_got)
    part_tables = tuple(
        lax.dynamic_slice_in_dim(table, c * half + x * quarter, quarter, 0) for table in tables
    )
    grad_kv_part = jnp.concatenate(
        [rope_back(grad_kv_part[:, :HD], part_tables), grad_kv_part[:, HD:]], axis=1
    ).astype(BF16)
    grad_kv = lax.dynamic_update_slice(
        jnp.zeros((group, 2 * HD), BF16), grad_kv_part, (c * half + x * quarter, 0)
    )
    grad_x, grad_bc, grad_dt, sums = call(
        mamba_grad_kernel,
        (
            shape((group, wide), BF16),
            shape((group, 2 * states), BF16),
            shape((group, 128), BF16),
            shape((8, 128)),
        ),
        (steps,),
        chunk_specs(True)
        + more_specs(True)
        + [
            flow(wide, True),
            flow(states, True),
            flow(states, True),
            flow(128, True),
            pl.BlockSpec((1, states, wide), lambda i: (steps - 1 - i, 0, 0)),
            whole,
        ],
        (
            flow(wide, True),
            flow(2 * states, True),
            flow(128, True),
            pl.BlockSpec((8, 128), lambda i: (0, 0)),
        ),
        [pltpu.VMEM((states, wide), F32)],
    )(*chunk_args, *chunk_more, *near_out[:5], deep)

    grad_x, out_part = lax.optimization_barrier((grad_x, out_part))
    x_w, two_own, two_other = grad_late(
        kv_head, groups, normed, grad_x, grad_kv, grad_bc, grad_dt, w_all, gain_early,
        gain_two_part[:, None],
    )
    x_part = line_scatter("x", x_w)
    grad_own, grad_other = assemble(
        kv_head, own_rows, grad_q, after(grad_x, x_w), grad_kv, grad_bc, grad_dt, grad_z
    )
    two_mine = two_own + swap(two_other, "c")
    grad_other = after(grad_other, two_mine)
    in_other = row_term(grad_other, w_all)
    two_terms = cube_scatter_direct("grad_two", two_mine, None, None)
    grad_own, qz_part = lax.optimization_barrier((after(grad_own, in_other), qz_part))
    in_own = row_term(grad_own, w_all)
    in_sum, in_far, in_last = cube_scatter("grad_in", in_own, in_other)
    two_terms = lax.optimization_barrier((*two_terms, in_far))[:4]
    two_part = sum(a.astype(F32) for a in two_terms)
    out_own, out_got = own_and_got("out", after(out_part, in_last))
    gu_own, gu_got = own_and_got("gu", after(gu_part, in_last))
    qz_own, qz_got = own_and_got("qz", after(qz_part, in_last))
    in_grad = in_sum
    input_part, _ = norm_back(stream_own, gain_one, in_grad)
    input_grad = grad_middle + input_part
    two_part = lax.psum_scatter(two_part.astype(BF16), "z", scatter_dimension=0).astype(F32)
    kv_grad = two_part[:, :kv_cols].reshape(kv_w.shape)
    bc_grad = two_part[:, kv_cols:lead]
    small = jnp.concatenate(
        [sums[0, :heads], sums[1, :heads], jnp.sum(skip_sums[0].reshape(heads, MP), axis=1)]
    )
    small = jnp.pad(small, (0, width - small.shape[0]))
    dt_w_grad = mm(after(grad_dt, in_other), normed, 0, 0)[:heads]
    tiny = jnp.concatenate([dt_w_grad, small[None]], axis=0)
    tiny = after(tiny, in_sum)
    for got in from_ring("tiny", tiny):
        tiny = tiny + got
    tiny_other = swap(tiny, "x")
    dt_grad = both_halves(
        *(
            lax.dynamic_slice_in_dim(a[:heads], (z * 2 + x) * rows_w, rows_w, 1).T
            for a in (tiny, tiny_other)
        )
    )
    small_sum = both_halves(*(a[heads, : 3 * heads].reshape(3, heads) for a in (tiny, tiny_other)))
    return (
        layer_out,
        input_grad,
        two_part[:, lead] / gain_mix.astype(F32),
        both_halves(qz_own[:, :inner], qz_got[:, :inner]),
        kv_grad,
        jnp.stack(
            [both_halves(qz_own[:, inner:], qz_got[:, inner:]), both_halves(*own_and_got("x", after(x_part, in_last)))],
            axis=1,
        ),
        dt_grad,
        bc_grad,
        small_sum[0],
        small_sum[1],
        small_sum[2],
        both_halves(out_own[:, :inner], out_got[:, :inner]),
        both_halves(out_own[:, inner:], out_got[:, inner:]),
        two_part[:, lead + 1],
        jnp.stack(
            [both_halves(gu_own[:, :ff], gu_got[:, :ff]), both_halves(gu_own[:, ff:], gu_got[:, ff:])],
            axis=1,
        ),
        both_halves(down_own, down_got),
    )


def solution(mesh):
    groups = mesh.shape["blk"] // 2
    fine = Mesh(mesh.devices.reshape(groups, 2, 2, mesh.shape["head"] // 2), ("z", "x", "y", "c"))
    blk, head = ("z", "x"), ("y", "c")
    every = blk + head
    rows = P(every, None)
    return jax.shard_map(
        shards,
        mesh=fine,
        in_specs=(
            rows,
            P(blk),
            rows,
            P(every),
            P(blk, head),
            P(every, None, None),
            P(blk, None, head),
            P(blk, head),
            rows,
            P(head),
            P(head),
            P(head),
            P(blk, head),
            P(blk, head),
            P(every),
            P(blk, None, head),
            P(blk, head),
        ),
        out_specs=(
            rows,
            rows,
            P(every),
            P(blk, head),
            P(every, None, None),
            P(blk, None, head),
            P(blk, head),
            rows,
            P(head),
            P(head),
            P(head),
            P(blk, head),
            P(blk, head),
            P(every),
            P(blk, None, head),
            P(blk, head),
        ),
        check_vma=False,
    )
```
